32 devices in a mesh: dp: 4 (over y, core), fsdp: 8 (over z, x).
Axes of the slice: x: 2, y: 2, z: 4, core: 2. Of those that a mesh axis runs over, the one named last changes fastest.
Arguments:
- target: bfloat16 [32768, 768], P(('dp', 'fsdp')), may hold values from -6 to 6
- memory: bfloat16 [128, 1024, 768], P(('dp', 'fsdp')), may hold values from -6 to 6
- cotangent: bfloat16 [32768, 768], P(('dp', 'fsdp')), may hold values from -6 to 6
- bucket: int32 [32], P(('dp', 'fsdp')), may hold values from 0 to 1
- source_len: int32 [128], P(('dp', 'fsdp')), may hold values from 256 to 1024, as said below
- self_qkv: bfloat16 [3, 768, 768], P(None, 'fsdp'), may hold values from -0.21875 to 0.21875
- self_out: bfloat16 [768, 768], P('fsdp'), may hold values from -0.875 to 0.875
- self_bias: bfloat16 [3, 768], P(None, 'fsdp'), may hold values from -3 to 3
- cross_qkv: bfloat16 [3, 768, 768], P(None, 'fsdp'), may hold values from -0.21875 to 0.21875
- cross_out: bfloat16 [768, 768], P('fsdp'), may hold values from -0.875 to 0.875
- cross_bias: bfloat16 [3, 768], P(None, 'fsdp'), may hold values from -3 to 3
- ffn_in: bfloat16 [768, 3072], P('fsdp'), may hold values from -0.21875 to 0.21875
- ffn_in_bias: bfloat16 [3072], P('fsdp'), may hold values from -3 to 3
- ffn_out: bfloat16 [3072, 768], P('fsdp'), may hold values from -0.109375 to 0.109375
- ffn_out_bias: bfloat16 [768], P('fsdp'), may hold values from -3 to 3
- norm_gain: bfloat16 [3, 768], P(None, 'fsdp'), may hold values from 0.25 to 1.75
- norm_bias: bfloat16 [3, 768], P(None, 'fsdp'), may hold values from -2 to 2
Outputs:
- output: bfloat16 [32768, 768], P(('dp', 'fsdp'))
- target_grad: float32 [32768, 768], P(('dp', 'fsdp'))
- memory_grad: float32 [128, 1024, 768], P(('dp', 'fsdp'))
- grad_self_qkv: float32 [3, 768, 768], P(None, 'fsdp')
- grad_self_out: float32 [768, 768], P('fsdp')
- grad_self_bias: float32 [3, 768], P(None, 'fsdp')
- grad_cross_qkv: float32 [3, 768, 768], P(None, 'fsdp')
- grad_cross_out: float32 [768, 768], P('fsdp')
- grad_cross_bias: float32 [3, 768], P(None, 'fsdp')
- grad_ffn_in: float32 [768, 3072], P('fsdp')
- grad_ffn_in_bias: float32 [3072], P('fsdp')
- grad_ffn_out: float32 [3072, 768], P('fsdp')
- grad_ffn_out_bias: float32 [768], P('fsdp')
- grad_norm_gain: float32 [3, 768], P(None, 'fsdp')
- grad_norm_bias: float32 [3, 768], P(None, 'fsdp')
The draws below stay inside these ranges and needn't reach their ends.
Inputs may be any that keep to these rules, and one draw needn't show every extreme that they name: bucket 1: the device's 1024 tokens are 4 rows of 256, row r reading memory row r of the device; bucket 0: they are one row, which reads the device's first memory row. `source_len`: some memory row has all 1024 tokens valid.
All inputs are finite; a program needn't handle non-finite values.
Results may differ from the reference program's by a relative error of at most 0.024.
The reference program's roundings to bfloat16 on the way count: a program that leaves them out, or rounds other values in their place, can miss the bound.
Values may be sent and summed in bfloat16 or wider, within the bound.
No kernel may reach another device: no remote copies, remote signals or barrier semaphores. Data moves between devices by JAX's collectives and lax.ppermute only.
A program may use at most 384 MiB of HBM per device.

```python
import jax
import jax.numpy as jnp
from jax import lax

D = 768
HEADS = 12
HEAD = 64
FF = 3072
SHORT = 256
ROWS_DEV = 4
MEM = 1024
TOK_DEV = 1024
TOKENS = 32768
ROWS = 128
N_DP = 4
N_FSDP = 8


def draw_source_len(key, part):
    key = jax.random.fold_in(key, 7)
    base_key, ranking_key = jax.random.split(key)
    lengths = jax.random.randint(base_key, (ROWS,), MEM // 4, MEM + 1, dtype=jnp.int32)
    ranking = jax.random.permutation(ranking_key, ROWS)
    lengths = lengths.at[ranking[0]].set(MEM)
    return lengths.at[ranking[1]].set(MEM // 4)


def plant(values, stream_key, smallest, largest):
    longest = values.shape.index(max(values.shape))
    spots = []
    for shift in (0, 1):
        where = [jax.random.randint(jax.random.fold_in(stream_key, axis), (), 0, length) for axis, length in enumerate(values.shape)]
        where[longest] = (where[longest] + shift) % values.shape[longest]
        spots.append(tuple(where))
    return values.at[spots[0]].set(smallest).at[spots[1]].set(largest)


def block_levels(own_key, dims, pieces, least, largest):
    factor_of = 1.0
    for dim, shards_of in pieces:
        draws = jax.random.uniform(jax.random.fold_in(jax.random.fold_in(own_key, 6), dim), (shards_of,), jnp.float32, least / len(pieces), largest / len(pieces))
        factor_of = factor_of * jnp.repeat(jnp.exp(draws), dims[dim] // shards_of).reshape((-1,) + (1,) * (len(dims) - 1 - dim))
    return factor_of


def scatter_about(rng, extent, scale, most, shards=(), held_as=jnp.bfloat16):
    drawn = jax.random.normal(rng, extent, jnp.float32) * scale
    if len(shards) > 0:
        drawn = block_levels(rng, extent, shards, -0.22, 0.18) * drawn
    return jnp.clip(drawn, min=-most, max=most).astype(held_as)


def setup_inputs(seed: int = 0) -> dict:
    key_list = jax.random.split(jax.random.key(seed), 18)
    target = scatter_about(key_list[0], (TOKENS, D), 1.0, 6.0, ((0, 32),))
    memory = scatter_about(key_list[1], (ROWS, MEM, D), 1.0, 6.0, ((0, 32),))
    cotangent = scatter_about(key_list[2], (TOKENS, D), 1.0, 6.0, ((0, 32),))
    bucket = plant(jax.random.randint(key_list[3], (N_DP * N_FSDP,), 0, 2), jax.random.fold_in(key_list[3], 1), 0, 1).astype(jnp.int32)
    source_len = draw_source_len(jax.random.fold_in(key_list[17], 71), 0)
    self_qkv = scatter_about(key_list[5], (3, D, D), D ** -0.5, 0.21875, ((1, 8),))
    self_out = scatter_about(key_list[6], (D, D), (D // 16) ** -0.5, 0.875, ((0, 8),))
    self_bias = scatter_about(key_list[7], (3, D), 0.5, 3.0, ((1, 8),))
    cross_qkv = scatter_about(key_list[8], (3, D, D), D ** -0.5, 0.21875, ((1, 8),))
    cross_out = scatter_about(key_list[9], (D, D), (D // 16) ** -0.5, 0.875, ((0, 8),))
    cross_bias = scatter_about(key_list[10], (3, D), 0.5, 3.0, ((1, 8),))
    ffn_in = scatter_about(key_list[11], (D, FF), D ** -0.5, 0.21875, ((0, 8),))
    ffn_in_bias = scatter_about(key_list[12], (FF,), 0.5, 3.0, ((0, 8),))
    ffn_out = scatter_about(key_list[13], (FF, D), FF ** -0.5, 0.109375, ((0, 8),))
    ffn_out_bias = scatter_about(key_list[14], (D,), 0.5, 3.0, ((0, 8),))
    norm_gain = jnp.clip(1.0 + 0.15 * jax.random.normal(key_list[15], (3, D), jnp.float32), 0.25, 1.75).astype(jnp.bfloat16)
    norm_bias = scatter_about(key_list[16], (3, D), 0.3, 2.0, ((1, 8),))
    return {"target": target, "memory": memory, "cotangent": cotangent, "bucket": bucket, "source_len": source_len, "self_qkv": self_qkv, "self_out": self_out, "self_bias": self_bias, "cross_qkv": cross_qkv, "cross_out": cross_out, "cross_bias": cross_bias, "ffn_in": ffn_in, "ffn_in_bias": ffn_in_bias, "ffn_out": ffn_out, "ffn_out_bias": ffn_out_bias, "norm_gain": norm_gain, "norm_bias": norm_bias}


@jax.custom_vjp
def low(v):
    return lax.optimization_barrier(v.astype(jnp.bfloat16)).astype(jnp.float32)

@jax.custom_vjp
def low_back(v):
    return v

def low_keep(v):
    return (low(v), None)

def low_pass(kept, grad):
    return (grad,)

def back_keep(v):
    return (v, None)

def back_low(kept, grad):
    return (low(grad),)
low.defvjp(low_keep, low_pass)
low_back.defvjp(back_keep, back_low)
very_low = -1e+30
epsilon = 1e-05

def matmul(left, right):
    return jnp.dot(left, right, precision=lax.Precision.HIGHEST)

def layer_norm(total, norm_scale, shift):
    middle = lax.optimization_barrier(jnp.mean(total, -1, keepdims=True))
    centred = total - middle
    variance = lax.optimization_barrier(jnp.mean(centred * centred, -1, keepdims=True))
    return centred * lax.rsqrt(variance + epsilon) * norm_scale + shift

def softmax_rows(scores):
    highest = lax.optimization_barrier(jnp.max(scores, -1, keepdims=True))
    raised = jnp.exp(scores - highest)
    return raised / lax.optimization_barrier(jnp.sum(raised, -1, keepdims=True))

def group_layer(weights, tokens, encoded, bucket_id, lengths):
    self_qkv, self_out, self_bias, cross_qkv, cross_out, cross_bias, ffn_in, ffn_in_bias, ffn_out, ffn_out_bias, norm_gain, norm_bias = weights
    query_scale = HEAD ** (-0.5)
    index = jnp.arange(TOK_DEV, dtype=jnp.int32)
    row_of = jnp.where(bucket_id == 1, index // SHORT, 0)
    place = jnp.where(bucket_id == 1, index % SHORT, index)
    allowed = (row_of[:, None] == row_of[None, :]) & (place[None, :] <= place[:, None])
    query_self = low(low_back((matmul(tokens, self_qkv[0]) + self_bias[0]) * query_scale)).reshape(TOK_DEV, HEADS, HEAD)
    key_self = low(low_back(matmul(tokens, self_qkv[1]))).reshape(TOK_DEV, HEADS, HEAD)
    value_self = low(low_back(matmul(tokens, self_qkv[2]) + self_bias[1])).reshape(TOK_DEV, HEADS, HEAD)
    scores = low_back(jnp.einsum('qhe,khe->hqk', query_self, key_self, precision=lax.Precision.HIGHEST))
    shares = low(softmax_rows(jnp.where(allowed[None], scores, very_low)))
    context = jnp.einsum('hqk,khe->qhe', shares, value_self, precision=lax.Precision.HIGHEST)
    context = low(low_back(context.reshape(TOK_DEV, D)))
    branch = low_back(matmul(context, self_out) + self_bias[2])
    first = layer_norm(tokens + branch, norm_gain[0], norm_bias[0])
    first_low = low(first)
    query_cross = low(low_back((matmul(first_low, cross_qkv[0]) + cross_bias[0]) * query_scale)).reshape(ROWS_DEV, SHORT, HEADS, HEAD)
    key_all = low(low_back(jnp.einsum('rmd,de->rme', encoded, cross_qkv[1], precision=lax.Precision.HIGHEST))).reshape(ROWS_DEV, MEM, HEADS, HEAD)
    value_all = low(low_back(jnp.einsum('rmd,de->rme', encoded, cross_qkv[2], precision=lax.Precision.HIGHEST) + cross_bias[1])).reshape(ROWS_DEV, MEM, HEADS, HEAD)
    chosen = jnp.where(bucket_id == 1, jnp.arange(ROWS_DEV, dtype=jnp.int32), 0)
    key_chosen = jnp.take(key_all, chosen, axis=0)
    value_chosen = jnp.take(value_all, chosen, axis=0)
    reach = jnp.arange(MEM, dtype=jnp.int32)[None, :] < jnp.take(lengths, chosen)[:, None]
    scores = low_back(jnp.einsum('rqhe,rkhe->rhqk', query_cross, key_chosen, precision=lax.Precision.HIGHEST))
    shares = low(softmax_rows(jnp.where(reach[:, None, None, :], scores, very_low)))
    context = jnp.einsum('rhqk,rkhe->rqhe', shares, value_chosen, precision=lax.Precision.HIGHEST)
    context = low(low_back(context.reshape(TOK_DEV, D)))
    branch = low_back(matmul(context, cross_out) + cross_bias[2])
    second = layer_norm(first + branch, norm_gain[1], norm_bias[1])
    second_low = low(second)
    hidden = low_back(matmul(second_low, ffn_in) + ffn_in_bias)
    active = low(jax.nn.gelu(hidden, approximate=False))
    branch = low_back(matmul(active, ffn_out) + ffn_out_bias)
    return layer_norm(second + branch, norm_gain[2], norm_bias[2])

def whole(weights, tokens, encoded, buckets, lengths):
    layer = jax.checkpoint(group_layer)

    def step(carry, item):
        return (carry, layer(weights, item[0], item[1], item[2], item[3]))
    _, outputs = lax.scan(step, jnp.zeros((), jnp.float32), (tokens, encoded, buckets, lengths))
    return outputs

def reference(target, memory, cotangent, bucket, source_len, self_qkv, self_out, self_bias, cross_qkv, cross_out, cross_bias, ffn_in, ffn_in_bias, ffn_out, ffn_out_bias, norm_gain, norm_bias):
    groups = N_DP * N_FSDP
    weights = tuple((weight.astype(jnp.float32) for weight in (self_qkv, self_out, self_bias, cross_qkv, cross_out, cross_bias, ffn_in, ffn_in_bias, ffn_out, ffn_out_bias, norm_gain, norm_bias)))
    tokens = target.astype(jnp.float32).reshape(groups, TOK_DEV, D)
    encoded = memory.astype(jnp.float32).reshape(groups, ROWS_DEV, MEM, D)
    lengths = source_len.reshape(groups, ROWS_DEV)

    def forward(params, inputs, sources):
        return whole(params, inputs, sources, bucket, lengths)
    outputs, pull = jax.vjp(forward, weights, tokens, encoded)
    grad_weights, grad_tokens, grad_memory = pull(cotangent.astype(jnp.float32).reshape(groups, TOK_DEV, D))
    return (outputs.reshape(TOKENS, D).astype(jnp.bfloat16), grad_tokens.reshape(TOKENS, D), grad_memory.reshape(ROWS, MEM, D), grad_weights[0], grad_weights[1], grad_weights[2], grad_weights[3], grad_weights[4], grad_weights[5], grad_weights[6], grad_weights[7], grad_weights[8], grad_weights[9], grad_weights[10], grad_weights[11])
```

```python
import functools
import math
import jax
import jax.numpy as jnp
from jax import lax
from jax.sharding import PartitionSpec as P
from jax.experimental import pallas as pl
from jax.experimental.pallas import tpu as pltpu

HEAD = 64
PAIR = 2 * HEAD
BLOCK = 256
very_low = -1e30
VMEM_LIMIT = 60 * 2**20
f32 = jnp.float32
bf16 = jnp.bfloat16


def dot_nt(left, right):
    return lax.dot_general(left, right, (((1,), (1,)), ((), ())), preferred_element_type=f32)


def dot_nn(left, right):
    return lax.dot_general(left, right, (((1,), (0,)), ((), ())), preferred_element_type=f32)


def dot_tn(left, right):
    return lax.dot_general(left, right, (((0,), (0,)), ((), ())), preferred_element_type=f32)


def split_pair(pair):
    lane = lax.broadcasted_iota(jnp.int32, pair.shape, 1)
    none = jnp.zeros_like(pair)
    return (jnp.where(lane < HEAD, pair, none), jnp.where(lane < HEAD, none, pair))


def mask_tail(scores, valid):
    width = scores.shape[0]
    if width == BLOCK:
        return jnp.where(valid, scores, very_low)
    return jnp.concatenate(
        [scores[: width - BLOCK], jnp.where(valid, scores[width - BLOCK :], very_low)], 0
    )


def attend_tile(queries, keys, values_t, valid):
    parts = []
    stats = []
    for half, query in enumerate(split_pair(queries)):
        scores = mask_tail(dot_nt(keys, query), valid)
        highest = jnp.max(scores, 0, keepdims=True)
        raised = jnp.exp(scores - highest)
        summed = jnp.sum(raised, 0, keepdims=True)
        context = dot_nn(values_t[half * HEAD : (half + 1) * HEAD], raised.astype(bf16))
        parts.append(context * (1.0 / summed))
        stats.append(highest + jnp.log(summed))
    return jnp.concatenate(parts, 0).T, jnp.concatenate(stats, 0)


def attend_back_tile(queries, keys, values, keys_t, grads, logsum, valid):
    shares_all = []
    grads_all = []
    query_parts = []
    query_halves = split_pair(queries)
    grad_halves = split_pair(grads)
    for half in range(2):
        scores = mask_tail(dot_nt(keys, query_halves[half]), valid)
        shares = jnp.exp(scores - logsum[half : half + 1])
        grad_shares = dot_nt(values, grad_halves[half])
        inner = jnp.sum(shares * grad_shares, 0, keepdims=True)
        grad_scores = (shares * (grad_shares - inner)).astype(bf16)
        query_parts.append(dot_nn(keys_t[half * HEAD : (half + 1) * HEAD], grad_scores))
        shares_all.append(shares.astype(bf16))
        grads_all.append(grad_scores)
    grad_values = dot_nn(jnp.concatenate(shares_all, 1), jnp.concatenate(grad_halves, 0))
    grad_keys = dot_nn(jnp.concatenate(grads_all, 1), jnp.concatenate(query_halves, 0))
    return jnp.concatenate(query_parts, 0).T, grad_keys, grad_values


def causal():
    key = lax.broadcasted_iota(jnp.int32, (BLOCK, BLOCK), 0)
    query = lax.broadcasted_iota(jnp.int32, (BLOCK, BLOCK), 1)
    return key <= query


def self_kernel(info, q_ref, k_ref, v_ref, o_ref, stat_ref):
    tokens = q_ref.shape[0]
    valid = causal()
    values_t = v_ref[...].T

    def run(whole):
        for part in range(tokens // BLOCK):
            rows = pl.ds(part * BLOCK, BLOCK)
            low = 0 if whole else part * BLOCK
            high = (part + 1) * BLOCK
            context, stats = attend_tile(
                q_ref[rows, :], k_ref[low:high, :], values_t[:, low:high], valid
            )
            o_ref[rows, :] = context.astype(bf16)
            stat_ref[0, :, rows] = stats

    pl.when(info[0] == 1)(functools.partial(run, False))
    pl.when(info[0] != 1)(functools.partial(run, True))


def self_back_kernel(
    info, q_ref, k_ref, v_ref, g_ref, stat_ref, dq_ref, dk_ref, dv_ref, key_sum, value_sum
):
    tokens = q_ref.shape[0]
    valid = causal()
    keys_t = k_ref[...].T

    def run(whole):
        for part in reversed(range(tokens // BLOCK)):
            rows = pl.ds(part * BLOCK, BLOCK)
            low = 0 if whole else part * BLOCK
            high = (part + 1) * BLOCK
            grad_queries, grad_keys, grad_values = attend_back_tile(
                q_ref[rows, :],
                k_ref[low:high, :],
                v_ref[low:high, :],
                keys_t[:, low:high],
                g_ref[rows, :],
                stat_ref[0, :, rows],
                valid,
            )
            dq_ref[rows, :] = (grad_queries.astype(bf16).astype(f32) * HEAD**-0.5).astype(bf16)
            if not whole:
                dk_ref[rows, :] = grad_keys.astype(bf16)
                dv_ref[rows, :] = grad_values.astype(bf16)
            elif high == tokens:
                key_sum[...] = grad_keys
                value_sum[...] = grad_values
            else:
                key_sum[:high, :] += grad_keys
                value_sum[:high, :] += grad_values
        if whole:
            dk_ref[...] = key_sum[...].astype(bf16)
            dv_ref[...] = value_sum[...].astype(bf16)

    pl.when(info[0] == 1)(functools.partial(run, False))
    pl.when(info[0] != 1)(functools.partial(run, True))


def cross_kernel(info, q_ref, k_ref, v_ref, o_ref, stat_ref):
    row = jnp.where(info[0] == 1, pl.program_id(1), 0)
    length = info[1 + row]
    mem_len = k_ref.shape[1]
    key = lax.broadcasted_iota(jnp.int32, (BLOCK, BLOCK), 0)

    def run(width):
        valid = key < length - (width - BLOCK)
        context, stats = attend_tile(
            q_ref[...], k_ref[0, :width, :], v_ref[0, :width, :].T, valid
        )
        o_ref[...] = context.astype(bf16)
        stat_ref[0] = stats

    for width in range(BLOCK, mem_len + 1, BLOCK):
        pl.when((length > width - BLOCK) & (length <= width))(functools.partial(run, width))


def cross_back_kernel(
    info, q_ref, k_ref, v_ref, g_ref, stat_ref, dq_ref, dk_ref, dv_ref, key_sum, value_sum
):
    part = pl.program_id(1)
    short = info[0] == 1
    row = jnp.where(short, part, 0)
    length = info[1 + row]
    mem_len = k_ref.shape[1]
    key = lax.broadcasted_iota(jnp.int32, (BLOCK, BLOCK), 0)

    def run(width):
        valid = key < length - (width - BLOCK)
        grad_queries, grad_keys, grad_values = attend_back_tile(
            q_ref[...],
            k_ref[0, :width, :],
            v_ref[0, :width, :],
            k_ref[0, :width, :].T,
            g_ref[...],
            stat_ref[0],
            valid,
        )
        dq_ref[...] = (grad_queries.astype(bf16).astype(f32) * HEAD**-0.5).astype(bf16)
        if width < mem_len:
            rest = jnp.zeros((mem_len - width, PAIR), bf16)
            dk_ref[0, width:, :] = rest
            dv_ref[0, width:, :] = rest

        @pl.when(short)
        def _():
            dk_ref[0, :width, :] = grad_keys.astype(bf16)
            dv_ref[0, :width, :] = grad_values.astype(bf16)

        @pl.when(jnp.logical_not(short))
        def _():
            @pl.when(part == 0)
            def _():
                key_sum[:width, :] = grad_keys
                value_sum[:width, :] = grad_values

            @pl.when(part != 0)
            def _():
                key_sum[:width, :] += grad_keys
                value_sum[:width, :] += grad_values

            @pl.when(part == pl.num_programs(1) - 1)
            def _():
                dk_ref[0, :width, :] = key_sum[:width, :].astype(bf16)
                dv_ref[0, :width, :] = value_sum[:width, :].astype(bf16)

    for width in range(BLOCK, mem_len + 1, BLOCK):
        pl.when((length > width - BLOCK) & (length <= width))(functools.partial(run, width))


def params():
    return pltpu.CompilerParams(vmem_limit_bytes=VMEM_LIMIT)


def cost(matmuls, moved=2**23):
    flops = 2 * sum(math.prod(sizes) for sizes in matmuls)
    return pl.CostEstimate(flops=flops, bytes_accessed=moved, transcendentals=0)


def self_attend(info, queries, keys, values):
    tokens, width = queries.shape
    pairs = width // PAIR
    whole = pl.BlockSpec((tokens, PAIR), lambda pair, info: (0, pair))
    return pl.pallas_call(
        self_kernel,
        grid_spec=pltpu.PrefetchScalarGridSpec(
            num_scalar_prefetch=1,
            grid=(pairs,),
            in_specs=[whole] * 3,
            out_specs=[whole, pl.BlockSpec((1, 2, tokens), lambda pair, info: (pair, 0, 0))],
        ),
        out_shape=[
            jax.ShapeDtypeStruct((tokens, width), bf16),
            jax.ShapeDtypeStruct((pairs, 2, tokens), f32),
        ],
        compiler_params=params(),
        name="self_attend",
        cost_estimate=cost([(tokens, tokens, width)] * 8),
    )(info, queries, keys, values)


def self_attend_back(info, queries, keys, values, grads, stats):
    tokens, width = queries.shape
    pairs = width // PAIR
    whole = pl.BlockSpec((tokens, PAIR), lambda pair, info: (0, pair))
    return pl.pallas_call(
        self_back_kernel,
        grid_spec=pltpu.PrefetchScalarGridSpec(
            num_scalar_prefetch=1,
            grid=(pairs,),
            in_specs=[whole] * 4
            + [pl.BlockSpec((1, 2, tokens), lambda pair, info: (pair, 0, 0))],
            out_specs=[whole] * 3,
            scratch_shapes=[pltpu.VMEM((tokens, PAIR), f32)] * 2,
        ),
        out_shape=[jax.ShapeDtypeStruct((tokens, width), bf16)] * 3,
        compiler_params=params(),
        name="self_attend_back",
        cost_estimate=cost([(tokens, tokens, width)] * 12),
    )(info, queries, keys, values, grads, stats)


def row_of(info, part):
    return jnp.where(info[0] == 1, part, 0)


def cross_attend(info, queries, keys, values):
    tokens, width = queries.shape
    rows, mem_len, _ = keys.shape
    pairs = width // PAIR
    tile = pl.BlockSpec((BLOCK, PAIR), lambda pair, part, info: (part, pair))
    memory = pl.BlockSpec((1, mem_len, PAIR), lambda pair, part, info: (row_of(info, part), 0, pair))
    return pl.pallas_call(
        cross_kernel,
        grid_spec=pltpu.PrefetchScalarGridSpec(
            num_scalar_prefetch=1,
            grid=(pairs, tokens // BLOCK),
            in_specs=[tile, memory, memory],
            out_specs=[
                tile,
                pl.BlockSpec((1, 2, BLOCK), lambda pair, part, info: (pair, 0, part)),
            ],
        ),
        out_shape=[
            jax.ShapeDtypeStruct((tokens, width), bf16),
            jax.ShapeDtypeStruct((pairs, 2, tokens), f32),
        ],
        compiler_params=params(),
        name="cross_attend",
        cost_estimate=cost([(tokens, mem_len, width)] * 16),
    )(info, queries, keys, values)


def cross_attend_back(info, queries, keys, values, grads, stats):
    tokens, width = queries.shape
    rows, mem_len, _ = keys.shape
    pairs = width // PAIR
    tile = pl.BlockSpec((BLOCK, PAIR), lambda pair, part, info: (part, pair))
    memory = pl.BlockSpec((1, mem_len, PAIR), lambda pair, part, info: (row_of(info, part), 0, pair))
    return pl.pallas_call(
        cross_back_kernel,
        grid_spec=pltpu.PrefetchScalarGridSpec(
            num_scalar_prefetch=1,
            grid=(pairs, tokens // BLOCK),
            in_specs=[
                tile,
                memory,
                memory,
                tile,
                pl.BlockSpec((1, 2, BLOCK), lambda pair, part, info: (pair, 0, part)),
            ],
            out_specs=[tile, memory, memory],
            scratch_shapes=[pltpu.VMEM((mem_len, PAIR), f32)] * 2,
        ),
        out_shape=[jax.ShapeDtypeStruct((tokens, width), bf16)]
        + [jax.ShapeDtypeStruct(keys.shape, bf16)] * 2,
        compiler_params=params(),
        name="cross_attend_back",
        cost_estimate=cost([(tokens, mem_len, width)] * 24),
    )(info, queries, keys, values, grads, stats)


epsilon = 1e-05


def normalise(total):
    middle = jnp.mean(total, -1, keepdims=True)
    centred = total - middle
    variance = jnp.mean(centred * centred, -1, keepdims=True)
    scale = lax.rsqrt(variance + epsilon)
    return centred * scale, scale


def normalise_back(grad, gain, normal, scale):
    scaled = grad * gain
    first = jnp.mean(scaled, -1, keepdims=True)
    second = jnp.mean(scaled * normal, -1, keepdims=True)
    return (scaled - first - normal * second) * scale


def add_rows(ref, row, value):
    ref[row : row + 1, :] += jnp.sum(value, 0, keepdims=True)


def start_sums(*refs):
    @pl.when(pl.program_id(0) == 0)
    def _():
        for ref in refs:
            ref[...] = jnp.zeros_like(ref)


def full(array):
    return pl.BlockSpec(memory_space=pltpu.VMEM)


def row_block(rows, width):
    return pl.BlockSpec((rows, width), lambda part: (part, 0))


def keep_block(rows, width):
    return pl.BlockSpec((rows, width), lambda part: (0, 0))


def first_kernel(x_ref, c_ref, out_w, query_w, vec_ref, z_ref, low_ref, q_ref):
    branch = dot_nn(c_ref[...], out_w[...]) + vec_ref[0:1, :]
    total = x_ref[...].astype(f32) + branch
    normal, _ = normalise(total)
    first_low = (normal * vec_ref[2:3, :] + vec_ref[3:4, :]).astype(bf16)
    z_ref[...] = total
    low_ref[...] = first_low
    q_ref[...] = ((dot_nn(first_low, query_w[...]) + vec_ref[1:2, :]) * HEAD**-0.5).astype(bf16)


def first_norm(x, context, out_w, query_w, vectors, rows=256):
    tokens, width = x.shape
    block = row_block(rows, width)
    return pl.pallas_call(
        first_kernel,
        grid=(tokens // rows,),
        in_specs=[block, block, full(out_w), full(query_w), full(vectors)],
        out_specs=[block] * 3,
        out_shape=[
            jax.ShapeDtypeStruct((tokens, width), f32),
            jax.ShapeDtypeStruct((tokens, width), bf16),
            jax.ShapeDtypeStruct((tokens, width), bf16),
        ],
        compiler_params=params(),
        name="first_norm",
        cost_estimate=cost([(tokens, width, width)] * 4),
    )(x, context, out_w, query_w, vectors)


def ffn_kernel(
    z_ref,
    c_ref,
    cot_ref,
    out_w,
    in_w,
    ffn_w,
    vec_ref,
    bias_ref,
    out_ref,
    low_ref,
    act_ref,
    du_ref,
    df_ref,
    do_ref,
    dz_ref,
    dc_ref,
    sum_ref,
    wide_ref,
    slope_ref,
):
    start_sums(sum_ref, wide_ref)
    width = z_ref.shape[1]
    gain_first, shift_first = vec_ref[2:3, :], vec_ref[3:4, :]
    gain_mid, shift_mid = vec_ref[4:5, :], vec_ref[5:6, :]
    gain_last, shift_last = vec_ref[6:7, :], vec_ref[7:8, :]
    normal_first, _ = normalise(z_ref[...])
    first = normal_first * gain_first + shift_first
    normal_mid, scale_mid = normalise(first + dot_nn(c_ref[...], out_w[...]) + vec_ref[0:1, :])
    second = normal_mid * gain_mid + shift_mid
    second_low = second.astype(bf16)
    low_ref[...] = second_low
    total = second + vec_ref[1:2, :]
    for block in range(in_w.shape[0]):
        cols = pl.ds(block * width, width)
        value = dot_nn(second_low, in_w[block]) + bias_ref[:, cols]
        share = 0.5 * (1.0 + lax.erf(value * 0.5**0.5))
        density = jnp.exp(-0.5 * value * value) * 0.3989422804014327
        active = (value * share).astype(bf16)
        slope_ref[:, cols] = share + value * density
        act_ref[:, cols] = active
        total = total + dot_nn(active, ffn_w[block])
    normal_last, scale_last = normalise(total)
    out_ref[...] = (normal_last * gain_last + shift_last).astype(bf16)
    cot = cot_ref[...].astype(f32)
    add_rows(sum_ref, 0, cot * normal_last)
    add_rows(sum_ref, 1, cot)
    grad_last = normalise_back(cot, gain_last, normal_last, scale_last)
    grad_low = grad_last.astype(bf16)
    df_ref[...] = grad_low
    add_rows(sum_ref, 2, grad_low.astype(f32))
    grad_second = grad_last
    for block in range(in_w.shape[0]):
        cols = pl.ds(block * width, width)
        grad_hidden = (dot_nt(grad_low, ffn_w[block]) * slope_ref[:, cols]).astype(bf16)
        du_ref[:, cols] = grad_hidden
        wide_ref[:, cols] += jnp.sum(grad_hidden.astype(f32), 0, keepdims=True)
        grad_second = grad_second + dot_nt(grad_hidden, in_w[block])
    add_rows(sum_ref, 3, grad_second * normal_mid)
    add_rows(sum_ref, 4, grad_second)
    grad_mid = normalise_back(grad_second, gain_mid, normal_mid, scale_mid)
    dz_ref[...] = grad_mid
    grad_low = grad_mid.astype(bf16)
    do_ref[...] = grad_low
    add_rows(sum_ref, 5, grad_low.astype(f32))
    dc_ref[...] = dot_nt(grad_low, out_w[...]).astype(bf16)


def ffn_block(z, context, cotangent, out_w, in_w, ffn_w, vectors, bias, rows=256):
    tokens, width = z.shape
    hidden = in_w.shape[0] * width
    block = row_block(rows, width)
    wide = row_block(rows, hidden)
    narrow_shape = jax.ShapeDtypeStruct((tokens, width), bf16)
    wide_shape = jax.ShapeDtypeStruct((tokens, hidden), bf16)
    return pl.pallas_call(
        ffn_kernel,
        grid=(tokens // rows,),
        in_specs=[block] * 3 + [full(None)] * 5,
        out_specs=[block, block, wide, wide, block, block, block, block]
        + [keep_block(8, width), keep_block(1, hidden)],
        out_shape=[
            narrow_shape,
            narrow_shape,
            wide_shape,
            wide_shape,
            narrow_shape,
            narrow_shape,
            jax.ShapeDtypeStruct((tokens, width), f32),
            narrow_shape,
            jax.ShapeDtypeStruct((8, width), f32),
            jax.ShapeDtypeStruct((1, hidden), f32),
        ],
        scratch_shapes=[pltpu.VMEM((rows, hidden), f32)],
        compiler_params=params(),
        name="ffn_block",
        cost_estimate=cost([(tokens, width, hidden)] * 8),
    )(z, context, cotangent, out_w, in_w, ffn_w, vectors, bias)


def first_back_kernel(
    dz2_ref, dq_ref, z_ref, query_w, out_w, vec_ref, dz_ref, do_ref, dc_ref, sum_ref
):
    start_sums(sum_ref)
    grad_query = dq_ref[...]
    grad_first = dz2_ref[...] + dot_nt(grad_query, query_w[...])
    normal, scale = normalise(z_ref[...])
    add_rows(sum_ref, 0, grad_first * normal)
    add_rows(sum_ref, 1, grad_first)
    grad_start = normalise_back(grad_first, vec_ref[2:3, :], normal, scale)
    dz_ref[...] = grad_start
    grad_low = grad_start.astype(bf16)
    do_ref[...] = grad_low
    add_rows(sum_ref, 2, grad_low.astype(f32))
    add_rows(sum_ref, 3, grad_query.astype(f32))
    dc_ref[...] = dot_nt(grad_low, out_w[...]).astype(bf16)


def first_back(dz2, grad_query, z, query_w, out_w, vectors, rows=256):
    tokens, width = z.shape
    block = row_block(rows, width)
    return pl.pallas_call(
        first_back_kernel,
        grid=(tokens // rows,),
        in_specs=[block] * 3 + [full(None)] * 3,
        out_specs=[block] * 3 + [keep_block(8, width)],
        out_shape=[
            jax.ShapeDtypeStruct((tokens, width), f32),
            jax.ShapeDtypeStruct((tokens, width), bf16),
            jax.ShapeDtypeStruct((tokens, width), bf16),
            jax.ShapeDtypeStruct((8, width), f32),
        ],
        compiler_params=params(),
        name="first_back",
        cost_estimate=cost([(tokens, width, width)] * 4),
    )(dz2, grad_query, z, query_w, out_w, vectors)


def needed(info, row, part, rows):
    return ((info[0] == 1) | (row == 0)) & (part * rows < info[1 + row])


def needed_place(info, row, part, rows):
    used = jnp.where(info[0] == 1, row, 0)
    last = (info[1 + used] + rows - 1) // rows - 1
    return used, jnp.where(info[0] == 1, jnp.minimum(part, last), jnp.where(row == 0, jnp.minimum(part, last), last))


def project_kernel(rows, info, m_ref, w_ref, b_ref, k_ref, v_ref):
    row, part = pl.program_id(0), pl.program_id(1)

    @pl.when(needed(info, row, part, rows))
    def _():
        memory = m_ref[0]
        k_ref[0] = dot_nn(memory, w_ref[1]).astype(bf16)
        v_ref[0] = (dot_nn(memory, w_ref[2]) + b_ref[...]).astype(bf16)


def project_memory(info, memory, weights, bias, rows=256):
    count, length, width = memory.shape
    place = lambda row, part, info: needed_place(info, row, part, rows) + (0,)
    block = pl.BlockSpec((1, rows, width), place)
    return pl.pallas_call(
        functools.partial(project_kernel, rows),
        grid_spec=pltpu.PrefetchScalarGridSpec(
            num_scalar_prefetch=1,
            grid=(count, length // rows),
            in_specs=[block, full(None), full(None)],
            out_specs=[block] * 2,
        ),
        out_shape=[jax.ShapeDtypeStruct(memory.shape, bf16)] * 2,
        compiler_params=params(),
        name="project_memory",
        cost_estimate=cost([(count, length, width, width)] * 2),
    )(info, memory, weights, bias)


def memory_back_kernel(rows, info, dk_ref, dv_ref, w_ref, out_ref):
    row, part = pl.program_id(0), pl.program_id(1)
    here = needed(info, row, part, rows)

    @pl.when(here)
    def _():
        out_ref[0] = dot_nt(dk_ref[0], w_ref[1]) + dot_nt(dv_ref[0], w_ref[2])

    @pl.when(jnp.logical_not(here))
    def _():
        out_ref[...] = jnp.zeros_like(out_ref)


def memory_back(info, grad_keys, grad_values, weights, rows=256):
    count, length, width = grad_keys.shape
    block = pl.BlockSpec(
        (1, rows, width), lambda row, part, info: needed_place(info, row, part, rows) + (0,)
    )
    return pl.pallas_call(
        functools.partial(memory_back_kernel, rows),
        grid_spec=pltpu.PrefetchScalarGridSpec(
            num_scalar_prefetch=1,
            grid=(count, length // rows),
            in_specs=[block, block, full(None)],
            out_specs=pl.BlockSpec((1, rows, width), lambda row, part, info: (row, part, 0)),
        ),
        out_shape=jax.ShapeDtypeStruct(grad_keys.shape, f32),
        compiler_params=params(),
        name="memory_back",
        cost_estimate=cost([(count, length, width, width)] * 2),
    )(info, grad_keys, grad_values, weights)


def memory_weights_kernel(rows, info, m_ref, dk_ref, dv_ref, w_ref, sum_ref, key_sum, value_sum):
    row, part = pl.program_id(0), pl.program_id(1)

    @pl.when((row == 0) & (part == 0))
    def _():
        key_sum[...] = jnp.zeros_like(key_sum)
        value_sum[...] = jnp.zeros_like(value_sum)
        sum_ref[...] = jnp.zeros_like(sum_ref)

    @pl.when(needed(info, row, part, rows))
    def _():
        memory = m_ref[0]
        key_sum[...] += dot_tn(memory, dk_ref[0])
        value_sum[...] += dot_tn(memory, dv_ref[0])
        sum_ref[...] += jnp.sum(dv_ref[0].astype(f32), 0, keepdims=True)

    @pl.when((row == pl.num_programs(0) - 1) & (part == pl.num_programs(1) - 1))
    def _():
        w_ref[0] = key_sum[...].astype(bf16)
        w_ref[1] = value_sum[...].astype(bf16)


def memory_weights(info, memory, grad_keys, grad_values, rows=512):
    count, length, width = memory.shape
    block = pl.BlockSpec(
        (1, rows, width), lambda row, part, info: needed_place(info, row, part, rows) + (0,)
    )
    return pl.pallas_call(
        functools.partial(memory_weights_kernel, rows),
        grid_spec=pltpu.PrefetchScalarGridSpec(
            num_scalar_prefetch=1,
            grid=(count, length // rows),
            in_specs=[block] * 3,
            out_specs=[
                pl.BlockSpec((2, width, width), lambda row, part, info: (0, 0, 0)),
                pl.BlockSpec((1, width), lambda row, part, info: (0, 0)),
            ],
            scratch_shapes=[pltpu.VMEM((width, width), f32)] * 2,
        ),
        out_shape=[
            jax.ShapeDtypeStruct((2, width, width), bf16),
            jax.ShapeDtypeStruct((1, width), f32),
        ],
        compiler_params=params(),
        name="memory_weights",
        cost_estimate=cost([(count, length, width, width)] * 2),
    )(info, memory, grad_keys, grad_values)


def unit(ref, number, count):
    rows = ref.shape[1] // count
    return ref[:, number * rows : (number + 1) * rows, :].reshape(ref.shape[0] * rows, ref.shape[2])


def put_unit(ref, number, count, value):
    rows = ref.shape[1] // count
    ref[:, number * rows : (number + 1) * rows, :] = value.astype(bf16).reshape(
        ref.shape[0], rows, ref.shape[2]
    )


def qkv_kernel(x_ref, w_ref, b_ref, q_ref, k_ref, v_ref):
    x = x_ref[...]
    q_ref[...] = ((dot_nn(x, unit(w_ref, 0, 3)) + b_ref[0:1, :]) * HEAD**-0.5).astype(bf16)
    k_ref[...] = dot_nn(x, unit(w_ref, 1, 3)).astype(bf16)
    v_ref[...] = (dot_nn(x, unit(w_ref, 2, 3)) + b_ref[1:2, :]).astype(bf16)


def project_self(x, weights, bias, rows=256):
    tokens, width = x.shape
    block = row_block(rows, width)
    return pl.pallas_call(
        qkv_kernel,
        grid=(tokens // rows,),
        in_specs=[block, full(None), full(None)],
        out_specs=[block] * 3,
        out_shape=[jax.ShapeDtypeStruct((tokens, width), bf16)] * 3,
        compiler_params=params(),
        name="project_self",
        cost_estimate=cost([(tokens, width, width)] * 4),
    )(x, weights, bias)


def target_back_kernel(z_ref, q_ref, k_ref, v_ref, w_ref, out_ref):
    out_ref[...] = (
        z_ref[...]
        + dot_nt(q_ref[...], unit(w_ref, 0, 3))
        + dot_nt(k_ref[...], unit(w_ref, 1, 3))
        + dot_nt(v_ref[...], unit(w_ref, 2, 3))
    )


def target_back(dz, grad_queries, grad_keys, grad_values, weights, rows=256):
    tokens, width = dz.shape
    block = row_block(rows, width)
    return pl.pallas_call(
        target_back_kernel,
        grid=(tokens // rows,),
        in_specs=[block] * 4 + [full(None)],
        out_specs=block,
        out_shape=jax.ShapeDtypeStruct((tokens, width), f32),
        compiler_params=params(),
        name="target_back",
        cost_estimate=cost([(tokens, width, width)] * 4),
    )(dz, grad_queries, grad_keys, grad_values, weights)


def self_weights_kernel(x_ref, q_ref, k_ref, v_ref, w_ref, sum_ref):
    x = x_ref[...]
    sum_ref[...] = jnp.zeros_like(sum_ref)
    for number, ref in enumerate((q_ref, k_ref, v_ref)):
        grads = ref[...]
        put_unit(w_ref, number, 3, dot_tn(x, grads))
        sum_ref[number : number + 1, :] = jnp.sum(grads.astype(f32), 0, keepdims=True)


def self_weights(x, grad_queries, grad_keys, grad_values, pieces):
    tokens, width = x.shape
    return pl.pallas_call(
        self_weights_kernel,
        out_shape=[
            jax.ShapeDtypeStruct((pieces, 3 * width // pieces, width), bf16),
            jax.ShapeDtypeStruct((8, width), f32),
        ],
        compiler_params=params(),
        name="self_weights",
        cost_estimate=cost([(tokens, width, width)] * 4),
    )(x, grad_queries, grad_keys, grad_values)


def ffn_weights_kernel(h_ref, du_ref, a_ref, df_ref, w_ref):
    pieces, rows, width = w_ref.shape[1:]
    w_ref[0, :, : rows // 2, :] = (
        dot_tn(h_ref[...], du_ref[...]).astype(bf16).reshape(pieces, rows // 2, width)
    )
    w_ref[0, :, rows // 2 :, :] = (
        dot_tn(a_ref[...], df_ref[...]).astype(bf16).reshape(pieces, rows // 2, width)
    )


def ffn_weights(second_low, grad_hidden, active, grad_out, pieces):
    tokens, width = second_low.shape
    blocks = active.shape[1] // width
    whole = pl.BlockSpec((tokens, width), lambda part: (0, 0))
    part = pl.BlockSpec((tokens, width), lambda part: (0, part))
    return pl.pallas_call(
        ffn_weights_kernel,
        grid=(blocks,),
        in_specs=[whole, part, part, whole],
        out_specs=pl.BlockSpec(
            (1, pieces, 2 * width // pieces, width), lambda part: (part, 0, 0, 0)
        ),
        out_shape=jax.ShapeDtypeStruct((blocks, pieces, 2 * width // pieces, width), bf16),
        compiler_params=params(),
        name="ffn_weights",
        cost_estimate=cost([(tokens, width, blocks * width)] * 2),
    )(second_low, grad_hidden, active, grad_out)


def wide(array):
    return array.astype(f32)


def weight_grad(left, right):
    return dot_tn(left, right).astype(bf16)


def forward_back(
    target, memory, cotangent, info, pieces, self_qkv, self_out, cross_qkv, cross_out, ffn, small
):
    self_bias, cross_bias, ffn_in_bias, ffn_out_bias, gain, shift = [wide(item) for item in small]
    queries, keys, values = project_self(target, self_qkv, self_bias)
    context_self, stats_self = self_attend(info, queries, keys, values)
    vec_first = jnp.stack([self_bias[2], cross_bias[0], gain[0], shift[0]])
    total_first, first_low, query_cross = first_norm(
        target, context_self, self_out, cross_qkv[0], vec_first
    )
    key_cross, value_cross = project_memory(info, memory, cross_qkv, cross_bias[1:2])
    context_cross, stats_cross = cross_attend(info, query_cross, key_cross, value_cross)
    vec_ffn = jnp.stack(
        [cross_bias[2], ffn_out_bias, gain[0], shift[0], gain[1], shift[1], gain[2], shift[2]]
    )
    output, second_low, active, du, df, do_cross, dz2, dc_cross, sums_ffn, sums_wide = ffn_block(
        total_first, context_cross, cotangent, cross_out, ffn[0], ffn[1], vec_ffn, ffn_in_bias[None]
    )
    grad_ffn = ffn_weights(second_low, du, active, df, pieces)
    grad_cross_out = weight_grad(context_cross, do_cross)
    dq_cross, dk_cross, dv_cross = cross_attend_back(
        info, query_cross, key_cross, value_cross, dc_cross, stats_cross
    )
    grad_cross_kv, sum_value_cross = memory_weights(info, memory, dk_cross, dv_cross)
    grad_cross_q = weight_grad(first_low, dq_cross)
    dz1, do_self, dc_self, sums_first = first_back(
        dz2, dq_cross, total_first, cross_qkv[0], self_out, vec_first
    )
    grad_self_out = weight_grad(context_self, do_self)
    grad_mid = jnp.concatenate(
        [
            item.reshape(pieces, item.shape[0] // pieces, item.shape[1])
            for item in (grad_cross_q, grad_cross_kv[0], grad_cross_kv[1], grad_cross_out, grad_self_out)
        ],
        1,
    )
    dq_self, dk_self, dv_self = self_attend_back(
        info, queries, keys, values, dc_self, stats_self
    )
    grad_self, sums_self = self_weights(target, dq_self, dk_self, dv_self, pieces)
    target_grad = target_back(dz1, dq_self, dk_self, dv_self, self_qkv)
    memory_grad = memory_back(info, dk_cross, dv_cross, cross_qkv)
    grad_small = (
        jnp.stack([sums_self[0], sums_self[2], sums_first[2]]),
        jnp.stack([sums_first[3], sum_value_cross[0], sums_ffn[5]]),
        sums_wide[0],
        sums_ffn[2],
        jnp.stack([sums_first[0], sums_ffn[3], sums_ffn[0]]),
        jnp.stack([sums_first[1], sums_ffn[4], sums_ffn[1]]),
    )
    return (output, target_grad, memory_grad), grad_ffn, grad_mid, grad_self, grad_small


def pair_swap(array, axis, bit):
    count = lax.axis_size(axis)
    return lax.ppermute(array, axis, [(place, place ^ bit) for place in range(count)])


def ring(array, axis, shift):
    count = lax.axis_size(axis)
    return lax.ppermute(array, axis, [(place, (place + shift) % count) for place in range(count)])


def pick(array, axis, index):
    return lax.dynamic_index_in_dim(array, index, axis, keepdims=False)


def places():
    dp, fsdp = lax.axis_index("dp"), lax.axis_index("fsdp")
    return dp // 2, dp % 2, fsdp // 2, fsdp % 2


def add_half(array, axis, mine, mesh_axis, bit):
    got = pair_swap(pick(array, axis, 1 - mine), mesh_axis, bit)
    return (wide(pick(array, axis, mine)) + wide(got)).astype(bf16)


def add_depth(array, depth):
    total = wide(pick(array, 0, depth))
    for step in (1, 2, 3):
        total = total + wide(ring(pick(array, 0, (depth + step) % 4), "fsdp", 2 * step))
    return total.astype(bf16)


def reduce_pieces(grads):
    high, core, depth, side = places()
    pieces, rows, width = grads.shape
    parts = grads.reshape(4, 2, 2, 2, rows // 4, width)
    parts = add_half(parts, 3, core, "dp", 1)
    half = rows // 8 // 8 * 8
    one, two = parts[:, :, :, :half], parts[:, :, :, half:]
    one, two = add_half(one, 2, high, "dp", 2), add_half(two, 1, side, "fsdp", 1)
    one, two = lax.optimization_barrier((one, two))
    one, two = add_half(one, 1, side, "fsdp", 1), add_half(two, 1, high, "dp", 2)
    one, two = lax.optimization_barrier((one, two))
    return jnp.concatenate([add_depth(one, depth), add_depth(two, depth)], 0)


def join_pair(array, axis, mine, mesh_axis, bit):
    got = pair_swap(array, mesh_axis, bit)
    first = jnp.where(mine == 0, array, got)
    second = jnp.where(mine == 0, got, array)
    return jnp.stack([first, second], axis)


def share_dp(array):
    high, core, _, _ = places()
    both = join_pair(array, 0, high, "dp", 2)
    return join_pair(both, 1, core, "dp", 1).reshape((4,) + array.shape)


def join_depth(array, depth):
    parts = [array] + [ring(array, "fsdp", 2 * step) for step in (1, 2, 3)]
    out = jnp.zeros((4,) + array.shape, array.dtype)
    for step, part in enumerate(parts):
        out = lax.dynamic_update_index_in_dim(out, part, (depth - step) % 4, 0)
    return out


def gather_pieces(array):
    high, core, depth, side = places()
    half = array.shape[0] // 2 // 8 * 8
    one, two = join_depth(array[:half], depth), join_depth(array[half:], depth)
    one, two = lax.optimization_barrier((one, two))
    one, two = join_pair(one, 1, side, "fsdp", 1), join_pair(two, 1, high, "dp", 2)
    one, two = lax.optimization_barrier((one, two))
    one, two = join_pair(one, 2, high, "dp", 2), join_pair(two, 1, side, "fsdp", 1)
    both = jnp.concatenate([one, two], 3)
    return join_pair(both, 3, core, "dp", 1).reshape((8, 4) + array.shape)


def split_small(rows, unit_rows):
    take = lambda low, count: rows[:, low * unit_rows : (low + count) * unit_rows]
    three = lambda low: jnp.swapaxes(
        take(low, 3).reshape(rows.shape[0], 3, unit_rows), 0, 1
    ).reshape(3, -1)
    return three(0), three(3), take(6, 4), take(10, 1).reshape(-1), three(11), three(14)


def fast_layer(
    target, memory, cotangent, bucket, source_len, self_qkv, self_out, self_bias, cross_qkv,
    cross_out, cross_bias, ffn_in, ffn_in_bias, ffn_out, ffn_out_bias, norm_gain, norm_bias,
):
    dp = lax.axis_index("dp")
    width = target.shape[1]
    own = self_out.shape[0]
    pieces = width // own
    info = jnp.concatenate([bucket, source_len])
    vectors = jnp.concatenate(
        [item.reshape(-1) for item in (self_bias, cross_bias, ffn_in_bias, ffn_out_bias, norm_gain, norm_bias)]
    )
    vectors = jnp.pad(vectors, (0, 8 * width - vectors.shape[0])).reshape(8, width)
    quarter = 3 * own // 4
    head = jnp.concatenate(
        [lax.dynamic_slice_in_dim(self_qkv.reshape(3 * own, width), dp * quarter, quarter, 0), vectors], 0
    )
    head = gather_pieces(head)
    self_qkv_w = head[:, :, :quarter].reshape(pieces, 3 * own, width)
    small = split_small(head[:, 0, quarter:].reshape(pieces, -1), own)
    small = list(small)
    small[2] = jnp.swapaxes(small[2].reshape(pieces, 4, own), 0, 1).reshape(-1)
    units = jnp.concatenate([self_out[None], cross_qkv], 0)
    mid = lax.all_gather(pick(units, 0, dp), ("dp", "fsdp"), axis=0, tiled=True)
    mid = mid.reshape(4, width, width)
    cross_rows = lax.dynamic_slice_in_dim(cross_out, dp * (own // 4), own // 4, 0)
    in_cols = pick(ffn_in.reshape(own, pieces, 4, own), 2, dp).reshape(own, width)
    out_rows = pick(ffn_out.reshape(4, own, width), 0, dp)
    tail = lax.all_gather(
        jnp.concatenate([in_cols, out_rows, cross_rows], 0), ("dp", "fsdp"), axis=0, tiled=False
    ).reshape(4, pieces, 2 * own + own // 4, width)
    ffn = (
        tail[:, :, :own].reshape(4, width, width),
        tail[:, :, own : 2 * own].reshape(4, width, width),
    )
    cross_out_w = jnp.swapaxes(tail[:, :, 2 * own :], 0, 1).reshape(width, width)
    outs, grad_ffn, grad_mid, grad_self, grad_small = forward_back(
        target, memory, cotangent, info, pieces, self_qkv_w, mid[0], mid[1:], cross_out_w, ffn, small
    )
    sum_ffn = lax.psum_scatter(
        grad_ffn.reshape(-1, width), ("dp", "fsdp"), scatter_dimension=0, tiled=True
    )
    sum_mid = reduce_pieces(grad_mid)
    grad_small = list(grad_small)
    grad_small[2] = jnp.swapaxes(grad_small[2].reshape(4, pieces, own), 0, 1).reshape(-1)
    per_owner = jnp.concatenate(
        [
            jnp.swapaxes(item.reshape(item.shape[0], pieces, -1), 0, 1).reshape(pieces, -1)
            if item.ndim == 2
            else item.reshape(pieces, -1)
            for item in grad_small
        ],
        1,
    )
    per_owner = jnp.pad(per_owner, ((0, 0), (0, 4 * width - per_owner.shape[1])))
    per_owner = jnp.pad(per_owner.reshape(pieces, 4, 1, width), ((0, 0), (0, 0), (0, 7), (0, 0)))
    grad_self = jnp.concatenate(
        [grad_self.reshape(pieces, 4, quarter, width), per_owner.astype(bf16)], 2
    )
    sum_self = reduce_pieces(grad_self.reshape(pieces, -1, width))
    everything = share_dp(jnp.concatenate([sum_ffn, sum_mid, sum_self], 0))
    everything = everything.astype(f32)
    low = 0
    parts = []
    for count in (own, own, 5 * own // 4, quarter, 8):
        parts.append(everything[:, low : low + count])
        low += count
    grad_in = jnp.moveaxis(parts[0].reshape(4, own, pieces, own), 0, 2).reshape(own, 4 * width)
    grad_out = parts[1].reshape(4 * own, width)
    mid_rows = parts[2].reshape(5, own, width)
    self_rows = parts[3].reshape(3, own, width)
    flat = parts[4][:, 0].reshape(-1)
    bias_self = flat[: 3 * own].reshape(3, own)
    bias_cross = flat[3 * own : 6 * own].reshape(3, own)
    bias_in = flat[6 * own : 10 * own]
    bias_out = flat[10 * own : 11 * own]
    gain = flat[11 * own : 14 * own].reshape(3, own)
    shift = flat[14 * own : 17 * own].reshape(3, own)
    return outs + (
        self_rows, mid_rows[4], bias_self, mid_rows[:3], mid_rows[3], bias_cross, grad_in, bias_in,
        grad_out, bias_out, gain, shift,
    )


def plain_layer(
    target, memory, cotangent, bucket, source_len, self_qkv, self_out, self_bias, cross_qkv,
    cross_out, cross_bias, ffn_in, ffn_in_bias, ffn_out, ffn_out_bias, norm_gain, norm_bias,
):
    gather = lambda item, axis: lax.all_gather(item, "fsdp", axis=axis, tiled=True)
    info = jnp.concatenate([bucket, source_len])
    width = target.shape[1]
    blocks = ffn_out.shape[0] * lax.axis_size("fsdp") // width
    ffn_in_w = jnp.swapaxes(gather(ffn_in, 0).reshape(width, blocks, width), 0, 1)
    ffn_out_w = gather(ffn_out, 0).reshape(blocks, width, width)
    small = (
        gather(self_bias, 1), gather(cross_bias, 1), gather(ffn_in_bias, 0), gather(ffn_out_bias, 0),
        gather(norm_gain, 1), gather(norm_bias, 1),
    )
    outs, grad_ffn, grad_mid, grad_self, grad_small = forward_back(
        target, memory, cotangent, info, 1, gather(self_qkv, 1).reshape(1, 3 * width, width),
        gather(self_out, 0), gather(cross_qkv, 1), gather(cross_out, 0), (ffn_in_w, ffn_out_w), small,
    )

    def reduce(grad, axis):
        piece = lax.psum_scatter(wide(grad), "fsdp", scatter_dimension=axis, tiled=True)
        return lax.psum(piece, "dp")

    grad_in = jnp.swapaxes(grad_ffn[:, 0, :width], 0, 1).reshape(width, blocks * width)
    grad_out = grad_ffn[:, 0, width:].reshape(blocks * width, width)
    mid = grad_mid.reshape(5, width, width)
    return outs + (
        reduce(grad_self.reshape(3, width, width), 1),
        reduce(mid[4], 0),
        reduce(grad_small[0], 1),
        reduce(mid[:3], 1),
        reduce(mid[3], 0),
        reduce(grad_small[1], 1),
        reduce(grad_in, 0),
        reduce(grad_small[2], 0),
        reduce(grad_out, 0),
        reduce(grad_small[3], 0),
        reduce(grad_small[4], 1),
        reduce(grad_small[5], 1),
    )


def solution(mesh):
    rows = P(("dp", "fsdp"))
    first = P("fsdp")
    second = P(None, "fsdp")
    weights = (second, first, second, second, first, second, first, first, first, first, second, second)
    layer = fast_layer if (mesh.shape["dp"], mesh.shape["fsdp"]) == (4, 8) else plain_layer
    return jax.shard_map(
        layer,
        mesh=mesh,
        in_specs=(rows,) * 5 + weights,
        out_specs=(rows,) * 3 + weights,
        check_vma=False,
    )
```

```python
import functools
import math
import jax
import jax.numpy as jnp
from jax import lax
from jax.sharding import PartitionSpec as P
from jax.experimental import pallas as pl
from jax.experimental.pallas import tpu as pltpu

HEAD = 64
PAIR = 2 * HEAD
BLOCK = 256
very_low = -1e30
VMEM_LIMIT = 60 * 2**20
f32 = jnp.float32
bf16 = jnp.bfloat16


def dot_nt(left, right):
    return lax.dot_general(left, right, (((1,), (1,)), ((), ())), preferred_element_type=f32)


def dot_nn(left, right):
    return lax.dot_general(left, right, (((1,), (0,)), ((), ())), preferred_element_type=f32)


def dot_tn(left, right):
    return lax.dot_general(left, right, (((0,), (0,)), ((), ())), preferred_element_type=f32)


def split_pair(pair):
    lane = lax.broadcasted_iota(jnp.int32, pair.shape, 1)
    none = jnp.zeros_like(pair)
    return (jnp.where(lane < HEAD, pair, none), jnp.where(lane < HEAD, none, pair))


def mask_tail(scores, valid):
    width = scores.shape[0]
    if width == BLOCK:
        return jnp.where(valid, scores, very_low)
    return jnp.concatenate(
        [scores[: width - BLOCK], jnp.where(valid, scores[width - BLOCK :], very_low)], 0
    )


def stacked(pair):
    return jnp.concatenate(split_pair(pair), 0)


def score_tile(queries, keys, valid):
    return mask_tail(dot_nt(keys, stacked(queries)), valid)


def attend_tile(scores, values):
    count = scores.shape[1] // 2
    values_t = values.T
    highest = jnp.max(scores, 0, keepdims=True)
    raised = jnp.exp(scores - highest)
    summed = jnp.sum(raised, 0, keepdims=True)
    raised = raised.astype(bf16)
    context = jnp.concatenate(
        [
            dot_nn(values_t[half * HEAD : (half + 1) * HEAD], raised[:, half * count : (half + 1) * count])
            / summed[:, half * count : (half + 1) * count]
            for half in range(2)
        ],
        0,
    )
    return context.T.astype(bf16), highest + jnp.log(summed)


def head_sums(pair):
    turned = pair.T
    return jnp.concatenate(
        [jnp.sum(turned[half * HEAD : (half + 1) * HEAD], 0, keepdims=True) for half in range(2)], 1
    )


def back_tile(scores, queries, keys, values, grads, contexts, logsum):
    count = scores.shape[1] // 2
    grad_rows = stacked(grads)
    grad_shares = dot_nt(values, grad_rows)
    inner = head_sums(grads.astype(f32) * contexts.astype(f32))
    keys_t = keys.T
    shares = jnp.exp(scores - logsum)
    grad_scores = (shares * (grad_shares - inner)).astype(bf16)
    grad_values = dot_nn(shares.astype(bf16), grad_rows)
    grad_keys = dot_nn(grad_scores, stacked(queries))
    grad_queries = jnp.concatenate(
        [
            dot_nn(keys_t[half * HEAD : (half + 1) * HEAD], grad_scores[:, half * count : (half + 1) * count])
            for half in range(2)
        ],
        0,
    ).T
    grad_queries = (grad_queries.astype(bf16).astype(f32) * HEAD**-0.5).astype(bf16)
    return grad_queries, grad_keys, grad_values


def causal(columns):
    key = lax.broadcasted_iota(jnp.int32, (BLOCK, columns), 0)
    query = lax.broadcasted_iota(jnp.int32, (BLOCK, columns), 1) % BLOCK
    return key <= query


def key_spans(tokens, whole):
    return [
        (0 if whole else low, low, low + BLOCK) for low in range(0, tokens, BLOCK)
    ]


def self_kernel(skip, info, q_ref, k_ref, v_ref, o_ref, stat_ref):
    tokens = q_ref.shape[0]
    valid = causal(2 * BLOCK)

    def run(whole):
        spans = key_spans(tokens, whole)
        score = lambda span: score_tile(q_ref[span[1] : span[2], :], k_ref[span[0] : span[2], :], valid)
        ahead = score(spans[0])
        for part, (low, start, stop) in enumerate(spans):
            scores = ahead
            if part + 1 < len(spans):
                ahead = score(spans[part + 1])
            o_ref[start:stop, :], stat_ref[0, part] = attend_tile(scores, v_ref[low:stop, :])

    pl.when(info[0] == 1)(functools.partial(run, False))
    pl.when(info[0] != 1)(functools.partial(run, True))


def self_back_kernel(skip, info, q_ref, k_ref, v_ref, g_ref, o_ref, stat_ref, *refs):
    dq_ref, dk_ref, dv_ref, key_sum, value_sum = refs[skip:]
    tokens = q_ref.shape[0]
    valid = causal(2 * BLOCK)

    def run(whole):
        spans = key_spans(tokens, whole)[::-1]
        score = lambda span: score_tile(q_ref[span[1] : span[2], :], k_ref[span[0] : span[2], :], valid)
        ahead = score(spans[0])
        for step, (low, start, stop) in enumerate(spans):
            scores = ahead
            if step + 1 < len(spans):
                ahead = score(spans[step + 1])
            dq_ref[start:stop, :], grad_keys, grad_values = back_tile(
                scores,
                q_ref[start:stop, :],
                k_ref[low:stop, :],
                v_ref[low:stop, :],
                g_ref[start:stop, :],
                o_ref[start:stop, :],
                stat_ref[0, start // BLOCK],
            )
            if not whole:
                dk_ref[start:stop, :] = grad_keys.astype(bf16)
                dv_ref[start:stop, :] = grad_values.astype(bf16)
            elif stop == tokens:
                key_sum[...] = grad_keys
                value_sum[...] = grad_values
            else:
                key_sum[:stop, :] += grad_keys
                value_sum[:stop, :] += grad_values
        if whole:
            dk_ref[...] = key_sum[...].astype(bf16)
            dv_ref[...] = value_sum[...].astype(bf16)

    pl.when(info[0] == 1)(functools.partial(run, False))
    pl.when(info[0] != 1)(functools.partial(run, True))


def by_length(info, row, mem_len, run):
    length = info[1 + row]
    for width in range(BLOCK, mem_len + 1, BLOCK):

        @pl.when((length > width - BLOCK) & (length <= width))
        def _(width=width):
            run(width, lambda columns: lax.broadcasted_iota(jnp.int32, (BLOCK, columns), 0) < length - (width - BLOCK))


def cross_kernel(skip, info, q_ref, k_ref, v_ref, o_ref, stat_ref):
    tokens = q_ref.shape[0]
    count, mem_len, _ = k_ref.shape
    parts = tokens // BLOCK

    @pl.when(info[0] == 1)
    def _():
        def step(row, none):
            rows = pl.ds(pl.multiple_of(row * BLOCK, BLOCK), BLOCK)

            def run(width, valid):
                scores = score_tile(q_ref[rows, :], k_ref[row, :width, :], valid(2 * BLOCK))
                o_ref[rows, :], stat_ref[0, row] = attend_tile(scores, v_ref[row, :width, :])

            by_length(info, row, mem_len, run)
            return none

        lax.fori_loop(0, count, step, None)

    @pl.when(info[0] != 1)
    def _():
        def run(width, valid):
            scores = score_tile(q_ref[...], k_ref[0, :width, :], valid(2 * tokens))
            o_ref[...], stats = attend_tile(scores, v_ref[0, :width, :])
            for part in range(parts):
                low = part * BLOCK
                stat_ref[0, part] = jnp.concatenate(
                    [stats[:, low : low + BLOCK], stats[:, tokens + low : tokens + low + BLOCK]], 1
                )

        by_length(info, 0, mem_len, run)


def cross_back_kernel(skip, info, q_ref, k_ref, v_ref, g_ref, o_ref, stat_ref, *refs):
    dq_ref, dk_ref, dv_ref = refs[skip:]
    tokens = q_ref.shape[0]
    count, mem_len, _ = k_ref.shape
    parts = tokens // BLOCK

    def store(row, width, grad_keys, grad_values):
        dk_ref[row, :width, :] = grad_keys.astype(bf16)
        dv_ref[row, :width, :] = grad_values.astype(bf16)
        if width < mem_len:
            rest = jnp.zeros((mem_len - width, PAIR), bf16)
            dk_ref[row, width:, :] = rest
            dv_ref[row, width:, :] = rest

    @pl.when(info[0] == 1)
    def _():
        def step(row, none):
            rows = pl.ds(pl.multiple_of(row * BLOCK, BLOCK), BLOCK)

            def run(width, valid):
                keys = k_ref[row, :width, :]
                scores = score_tile(q_ref[rows, :], keys, valid(2 * BLOCK))
                dq_ref[rows, :], grad_keys, grad_values = back_tile(
                    scores, q_ref[rows, :], keys, v_ref[row, :width, :], g_ref[rows, :], o_ref[rows, :],
                    stat_ref[0, row],
                )
                store(row, width, grad_keys, grad_values)

            by_length(info, row, mem_len, run)
            return none

        lax.fori_loop(0, count, step, None)

    @pl.when(info[0] != 1)
    def _():
        def run(width, valid):
            keys = k_ref[0, :width, :]
            scores = score_tile(q_ref[...], keys, valid(2 * tokens))
            stats = jnp.concatenate(
                [stat_ref[0, part][:, half * BLOCK : (half + 1) * BLOCK] for half in range(2) for part in range(parts)],
                1,
            )
            dq_ref[...], grad_keys, grad_values = back_tile(
                scores, q_ref[...], keys, v_ref[0, :width, :], g_ref[...], o_ref[...], stats
            )
            store(0, width, grad_keys, grad_values)

        by_length(info, 0, mem_len, run)


def params():
    return pltpu.CompilerParams(vmem_limit_bytes=VMEM_LIMIT)


def cost(matmuls, moved=2**23):
    flops = 2 * sum(math.prod(sizes) for sizes in matmuls)
    return pl.CostEstimate(flops=flops, bytes_accessed=moved, transcendentals=0)


def attend_call(kernel, name, info, queries, keys, values, rest=None, first=0, count=None, start=()):
    tokens, width = queries.shape
    pairs = width // PAIR
    count = count or pairs
    parts = tokens // BLOCK
    back = rest is not None
    own = pl.BlockSpec((tokens, PAIR), lambda pair, info: (0, pair + first))
    stat = pl.BlockSpec((1, parts, 1, 2 * BLOCK), lambda pair, info: (pair + first, 0, 0, 0))
    if keys.ndim == 2:
        other = own
        scratch = [pltpu.VMEM((tokens, PAIR), f32)] * 2 if back else []
    else:
        other = pl.BlockSpec(keys.shape[:2] + (PAIR,), lambda pair, info: (0, 0, pair + first))
        scratch = []
    queries_shape = jax.ShapeDtypeStruct((tokens, width), bf16)
    keys_shape = jax.ShapeDtypeStruct(keys.shape, bf16)
    stat_shape = jax.ShapeDtypeStruct((pairs, parts, 1, 2 * BLOCK), f32)
    inputs = (queries, keys, values) + (rest or ())
    return pl.pallas_call(
        functools.partial(kernel, len(start)),
        grid_spec=pltpu.PrefetchScalarGridSpec(
            num_scalar_prefetch=1,
            grid=(count,),
            in_specs=[own, other, other]
            + ([own, own, stat] if back else [])
            + [pl.BlockSpec(memory_space=pl.ANY)] * len(start),
            out_specs=[own, other, other] if back else [own, stat],
            scratch_shapes=scratch,
        ),
        out_shape=[queries_shape, keys_shape, keys_shape] if back else [queries_shape, stat_shape],
        input_output_aliases={1 + len(inputs) + place: place for place in range(len(start))},
        compiler_params=params(),
        name=name,
        cost_estimate=cost([(tokens, tokens, width)] * (24 if back else 12)),
    )(info, *inputs, *start)


def self_attend(info, queries, keys, values):
    return attend_call(self_kernel, "self_attend", info, queries, keys, values)


def cross_attend(info, queries, keys, values):
    return attend_call(cross_kernel, "cross_attend", info, queries, keys, values)


def self_attend_back(info, queries, keys, values, *rest, **span):
    return attend_call(self_back_kernel, "self_attend_back", info, queries, keys, values, rest, **span)


def cross_attend_back(info, queries, keys, values, *rest, **span):
    return attend_call(cross_back_kernel, "cross_attend_back", info, queries, keys, values, rest, **span)


epsilon = 1e-05
VECTORS = 32


def normalise(total):
    middle = jnp.mean(total, -1, keepdims=True)
    centred = total - middle
    variance = jnp.mean(centred * centred, -1, keepdims=True)
    scale = lax.rsqrt(variance + epsilon)
    return centred * scale, scale


def normalise_back(grad, gain, normal, scale):
    scaled = grad * gain
    first = jnp.mean(scaled, -1, keepdims=True)
    second = jnp.mean(scaled * normal, -1, keepdims=True)
    return (scaled - first - normal * second) * scale


def add_rows(ref, row, value):
    ref[row : row + 1, :] += jnp.sum(value, 0, keepdims=True)


def start_sums(*refs):
    @pl.when(pl.program_id(0) == 0)
    def _():
        for ref in refs:
            ref[...] = jnp.zeros_like(ref)


def full(array):
    return pl.BlockSpec(memory_space=pltpu.VMEM)


def row_block(rows, width):
    return pl.BlockSpec((rows, width), lambda part, *info: (part, 0))


def keep_block(rows, width):
    return pl.BlockSpec((rows, width), lambda part, *info: (0, 0))


def unit(ref, high=0):
    return ref[:, high].reshape(ref.shape[0] * ref.shape[2], ref.shape[3])


def by_core(info, mine, got, run):
    core = info[info.shape[0] - 1]
    pl.when(core == 0)(lambda: run(mine, got))
    pl.when(core != 0)(lambda: run(got, mine))


def unit_block(array, high):
    return pl.BlockSpec(
        array.shape[:1] + (1,) + array.shape[2:],
        lambda *place: (0, high, 0, 0),
        pipeline_mode=pl.Buffered(1),
    )


def first_kernel(info, x_ref, c_ref, mine, got, vec_ref, z_ref, low_ref, q_ref):
    def run(even, odd):
        total = x_ref[...].astype(f32) + dot_nn(c_ref[...], unit(even)) + vec_ref[2 : 3, :]
        normal, _ = normalise(total)
        first_low = (normal * vec_ref[32 : 33, :] + vec_ref[40 : 41, :]).astype(bf16)
        z_ref[...] = total
        low_ref[...] = first_low
        q_ref[...] = ((dot_nn(first_low, unit(odd)) + vec_ref[8 : 9, :]) * HEAD**-0.5).astype(bf16)

    by_core(info, mine, got, run)


def row_call(kernel, name, info, grid, in_specs, out_specs, out_shape, matmuls, inputs, scratch=(), aliases=None):
    return pl.pallas_call(
        kernel,
        grid_spec=pltpu.PrefetchScalarGridSpec(
            num_scalar_prefetch=1,
            grid=grid,
            in_specs=in_specs,
            out_specs=out_specs,
            scratch_shapes=scratch,
        ),
        out_shape=out_shape,
        input_output_aliases=aliases or {},
        compiler_params=params(),
        name=name,
        cost_estimate=cost(matmuls),
    )(info, *inputs)


def first_norm(info, x, context, mid, vectors, rows=256):
    tokens, width = x.shape
    block = row_block(rows, width)
    low = jax.ShapeDtypeStruct((tokens, width), bf16)
    return row_call(
        first_kernel, "first_norm", info, (tokens // rows,),
        [block, block, unit_block(mid[0], 0), unit_block(mid[1], 0), full(vectors)],
        [block] * 3, [jax.ShapeDtypeStruct((tokens, width), f32), low, low],
        [(tokens, width, width)] * 4, (x, context, *mid, vectors),
    )


def chunks(blocks, pieces, block):
    return [divmod(number, blocks) for number in range(block * pieces, (block + 1) * pieces)]


def ffn_kernel(
    info,
    z_ref,
    c_ref,
    cot_ref,
    mine,
    got,
    tail_ref,
    vec_ref,
    out_ref,
    low_ref,
    act_ref,
    du_ref,
    df_ref,
    do_ref,
    dz_ref,
    dc_ref,
    sum_ref,
    wide_ref,
    slope_ref,
    out_w,
):
    start_sums(sum_ref, wide_ref)

    @pl.when(pl.program_id(0) == 0)
    def _():
        def load(even, odd):
            out_w[...] = unit(odd)

        by_core(info, mine, got, load)

    width = z_ref.shape[1]
    blocks, pieces, both = tail_ref.shape[:3]
    in_w = lambda block: tail_ref[block, :, : both // 2].reshape(width, width)
    ffn_w = lambda block: jnp.concatenate(
        [tail_ref[d, f, both // 2 :, :] for f, d in chunks(blocks, pieces, block)], 0
    )
    gain_first, gain_mid, gain_last = [vec_ref[row : row + 1, :] for row in (32, 33, 34)]
    shift_first, shift_mid, shift_last = [vec_ref[row : row + 1, :] for row in (40, 41, 42)]
    normal_first, _ = normalise(z_ref[...])
    first = normal_first * gain_first + shift_first
    normal_mid, scale_mid = normalise(first + dot_nn(c_ref[...], out_w[...]) + vec_ref[10 : 11, :])
    second = normal_mid * gain_mid + shift_mid
    second_low = second.astype(bf16)
    low_ref[...] = second_low
    total = second + vec_ref[24 : 25, :]
    ahead = dot_nn(second_low, in_w(0))
    for block in range(blocks):
        cols = pl.ds(block * width, width)
        value = ahead + vec_ref[16 + block : 17 + block, :]
        if block + 1 < blocks:
            ahead = dot_nn(second_low, in_w(block + 1))
        share = 0.5 * (1.0 + lax.erf(value * 0.5**0.5))
        density = jnp.exp(-0.5 * value * value) * 0.3989422804014327
        active = (value * share).astype(bf16)
        slope_ref[:, cols] = share + value * density
        act_ref[:, cols] = active
        total = total + dot_nn(active, ffn_w(block))
    normal_last, scale_last = normalise(total)
    out_ref[...] = (normal_last * gain_last + shift_last).astype(bf16)
    cot = cot_ref[...].astype(f32)
    add_rows(sum_ref, 0, cot * normal_last)
    add_rows(sum_ref, 1, cot)
    grad_last = normalise_back(cot, gain_last, normal_last, scale_last)
    grad_low = grad_last.astype(bf16)
    df_ref[...] = grad_low
    add_rows(sum_ref, 2, grad_low.astype(f32))
    grad_second = grad_last
    ahead = dot_nt(grad_low, ffn_w(0))
    for block in range(blocks):
        cols = pl.ds(block * width, width)
        grad_hidden = (ahead * slope_ref[:, cols]).astype(bf16)
        if block + 1 < blocks:
            ahead = dot_nt(grad_low, ffn_w(block + 1))
        du_ref[:, cols] = grad_hidden
        wide_ref[:, cols] += jnp.sum(grad_hidden.astype(f32), 0, keepdims=True)
        grad_second = grad_second + dot_nt(grad_hidden, in_w(block))
    add_rows(sum_ref, 3, grad_second * normal_mid)
    add_rows(sum_ref, 4, grad_second)
    grad_mid = normalise_back(grad_second, gain_mid, normal_mid, scale_mid)
    dz_ref[...] = grad_mid
    grad_low = grad_mid.astype(bf16)
    do_ref[...] = grad_low
    add_rows(sum_ref, 5, grad_low.astype(f32))
    dc_ref[...] = dot_nt(grad_low, out_w[...]).astype(bf16)


def ffn_block(info, z, context, cotangent, head, tail, vectors, rows=256):
    tokens, width = z.shape
    hidden = tail.shape[0] * width
    block = row_block(rows, width)
    wide = row_block(rows, hidden)
    narrow_shape = jax.ShapeDtypeStruct((tokens, width), bf16)
    wide_shape = jax.ShapeDtypeStruct((tokens, hidden), bf16)
    return row_call(
        ffn_kernel, "ffn_block", info, (tokens // rows,),
        [block] * 3 + [unit_block(head[0], 1), unit_block(head[1], 1), full(tail), full(vectors)],
        [block, block, wide, wide, block, block, block, block, keep_block(8, width), keep_block(1, hidden)],
        [
            narrow_shape, narrow_shape, wide_shape, wide_shape, narrow_shape, narrow_shape,
            jax.ShapeDtypeStruct((tokens, width), f32), narrow_shape,
            jax.ShapeDtypeStruct((8, width), f32), jax.ShapeDtypeStruct((1, hidden), f32),
        ],
        [(tokens, width, hidden)] * 8, (z, context, cotangent, *head, tail, vectors),
        [pltpu.VMEM((rows, hidden), f32), pltpu.VMEM((width, width), bf16)],
    )


def first_back_kernel(info, dz2_ref, dq_ref, z_ref, mine, got, vec_ref, dz_ref, do_ref, dc_ref, sum_ref):
    start_sums(sum_ref)

    def run(even, odd):
        grad_query = dq_ref[...]
        grad_first = dz2_ref[...] + dot_nt(grad_query, unit(odd))
        normal, scale = normalise(z_ref[...])
        add_rows(sum_ref, 0, grad_first * normal)
        add_rows(sum_ref, 1, grad_first)
        grad_start = normalise_back(grad_first, vec_ref[32 : 33, :], normal, scale)
        dz_ref[...] = grad_start
        grad_low = grad_start.astype(bf16)
        do_ref[...] = grad_low
        add_rows(sum_ref, 2, grad_low.astype(f32))
        add_rows(sum_ref, 3, grad_query.astype(f32))
        dc_ref[...] = dot_nt(grad_low, unit(even)).astype(bf16)

    by_core(info, mine, got, run)


def first_back(info, dz2, grad_query, z, mid, vectors, rows=256):
    tokens, width = z.shape
    block = row_block(rows, width)
    low = jax.ShapeDtypeStruct((tokens, width), bf16)
    return row_call(
        first_back_kernel, "first_back", info, (tokens // rows,),
        [block] * 3 + [unit_block(mid[0], 0), unit_block(mid[1], 0), full(vectors)],
        [block] * 3 + [keep_block(8, width)],
        [jax.ShapeDtypeStruct((tokens, width), f32), low, low, jax.ShapeDtypeStruct((8, width), f32)],
        [(tokens, width, width)] * 4, (dz2, grad_query, z, *mid, vectors),
    )


def needed(info, row, part, rows):
    return ((info[0] == 1) | (row == 0)) & (part * rows < info[1 + row])


def needed_place(info, row, part, rows):
    used = jnp.where(info[0] == 1, row, 0)
    last = (info[1 + used] + rows - 1) // rows - 1
    return used, jnp.where(info[0] == 1, jnp.minimum(part, last), jnp.where(row == 0, jnp.minimum(part, last), last))


def project_kernel(rows, info, m_ref, mine, got, b_ref, k_ref, v_ref):
    @pl.when(needed(info, pl.program_id(0), pl.program_id(1), rows))
    def _():
        def run(even, odd):
            memory = m_ref[0]
            k_ref[0] = dot_nn(memory, unit(even)).astype(bf16)
            v_ref[0] = (dot_nn(memory, unit(odd)) + b_ref[9 : 10, :]).astype(bf16)

        by_core(info, mine, got, run)


def memory_block(rows, width, first=0):
    return pl.BlockSpec(
        (1, rows, width), lambda row, part, info: needed_place(info, row + first, part, rows) + (0,)
    )


def project_memory(info, memory, mid, vectors, rows=512):
    count, length, width = memory.shape
    block = memory_block(rows, width)
    return row_call(
        functools.partial(project_kernel, rows), "project_memory", info, (count, length // rows),
        [block, unit_block(mid[0], 1), unit_block(mid[1], 1), full(vectors)], [block] * 2,
        [jax.ShapeDtypeStruct(memory.shape, bf16)] * 2,
        [(count, length, width, width)] * 2, (memory, *mid, vectors),
    )


def memory_back_kernel(rows, first, info, dk_ref, dv_ref, mine, got, *refs):
    out_ref = refs[-1]
    here = needed(info, pl.program_id(0) + first, pl.program_id(1), rows)

    @pl.when(here)
    def _():
        def run(even, odd):
            out_ref[0] = dot_nt(dk_ref[0], unit(even)) + dot_nt(dv_ref[0], unit(odd))

        by_core(info, mine, got, run)

    @pl.when(jnp.logical_not(here))
    def _():
        out_ref[...] = jnp.zeros_like(out_ref)


def memory_back(info, grad_keys, grad_values, mid, first, count, start=(), rows=512):
    length, width = grad_keys.shape[1:]
    block = memory_block(rows, width, first)
    return row_call(
        functools.partial(memory_back_kernel, rows, first), "memory_back", info, (count, length // rows),
        [block, block, unit_block(mid[0], 1), unit_block(mid[1], 1)]
        + [pl.BlockSpec(memory_space=pl.ANY)] * len(start),
        pl.BlockSpec((1, rows, width), lambda row, part, info: (row + first, part, 0)),
        jax.ShapeDtypeStruct(grad_keys.shape, f32),
        [(count, length, width, width)] * 2, (grad_keys, grad_values, *mid, *start),
        aliases={5: 0} if start else {},
    )


def unit_copy(info, stage, sent, mine, other, number, act):
    width = stage.shape[1]
    here = info[info.shape[0] - 1] == number % 2
    for ref, chosen in ((mine, here), (other, jnp.logical_not(here))):

        @pl.when(chosen)
        def _(ref=ref):
            rows = ref.at[pl.ds(number // 2 * width, width), :]
            act(pltpu.make_async_copy(stage.at[number], rows, sent.at[number]))


def put_unit(info, stage, sent, mine, other, number, value):
    stage[number] = value.astype(bf16)
    unit_copy(info, stage, sent, mine, other, number, lambda copy: copy.start())


def end_units(info, stage, sent, mine, other):
    for number in range(4):
        unit_copy(info, stage, sent, mine, other, number, lambda copy: copy.wait())


def unit_scratch(width):
    return [pltpu.VMEM((4, width, width), bf16), pltpu.SemaphoreType.DMA((4,))]


def mid_weights_kernel(
    rows, info, m_ref, dk_ref, dv_ref, first_ref, dq_ref, self_ref, dself_ref,
    mine, other, sum_ref, key_sum, value_sum, stage, sent,
):
    row, part = pl.program_id(0), pl.program_id(1)
    out = (info, stage, sent, mine, other)

    @pl.when((row == 0) & (part == 0))
    def _():
        put_unit(*out, 0, dot_tn(self_ref[...], dself_ref[...]))
        put_unit(*out, 1, dot_tn(first_ref[...], dq_ref[...]))
        key_sum[...] = jnp.zeros_like(key_sum)
        value_sum[...] = jnp.zeros_like(value_sum)
        sum_ref[...] = jnp.zeros_like(sum_ref)

    @pl.when(needed(info, row, part, rows))
    def _():
        memory = m_ref[0]
        key_sum[...] += dot_tn(memory, dk_ref[0])
        value_sum[...] += dot_tn(memory, dv_ref[0])
        sum_ref[...] += jnp.sum(dv_ref[0].astype(f32), 0, keepdims=True)

    @pl.when((row == pl.num_programs(0) - 1) & (part == pl.num_programs(1) - 1))
    def _():
        put_unit(*out, 2, key_sum[...])
        put_unit(*out, 3, value_sum[...])
        end_units(*out)


def mid_weights(info, memory, grad_keys, grad_values, pairs):
    count, rows, width = memory.shape
    block = memory_block(rows, width)
    half = jax.ShapeDtypeStruct((2 * width, width), bf16)
    return row_call(
        functools.partial(mid_weights_kernel, rows), "mid_weights", info, (count, 1),
        [block] * 3 + [full(None)] * 4,
        [pl.BlockSpec(memory_space=pl.ANY)] * 2 + [pl.BlockSpec((1, width), lambda row, part, info: (0, 0))],
        [half, half, jax.ShapeDtypeStruct((1, width), f32)],
        [(count, rows, width, width)] * 2, (memory, grad_keys, grad_values, *pairs),
        [pltpu.VMEM((width, width), f32)] * 2 + unit_scratch(width),
    )


def qkv_kernel(info, x_ref, mine, got, vec_ref, q_ref, k_ref, v_ref):
    def run(even, odd):
        x = x_ref[...]
        q_ref[...] = ((dot_nn(x, unit(even, 0)) + vec_ref[0 : 1, :]) * HEAD**-0.5).astype(bf16)
        k_ref[...] = dot_nn(x, unit(odd, 0)).astype(bf16)
        v_ref[...] = (dot_nn(x, unit(even, 1)) + vec_ref[1 : 2, :]).astype(bf16)

    by_core(info, mine, got, run)


def project_self(info, x, head, vectors, rows=512):
    tokens, width = x.shape
    block = row_block(rows, width)
    return row_call(
        qkv_kernel, "project_self", info, (tokens // rows,),
        [block, full(None), full(None), full(None)], [block] * 3,
        [jax.ShapeDtypeStruct((tokens, width), bf16)] * 3,
        [(tokens, width, width)] * 4, (x, *head, vectors),
    )


def target_back_kernel(info, z_ref, q_ref, k_ref, v_ref, mine, got, out_ref):
    def run(even, odd):
        out_ref[...] = (
            z_ref[...]
            + dot_nt(q_ref[...], unit(even, 0))
            + dot_nt(k_ref[...], unit(odd, 0))
            + dot_nt(v_ref[...], unit(even, 1))
        )

    by_core(info, mine, got, run)


def target_back(info, dz, grads, head, rows=256):
    tokens, width = dz.shape
    block = row_block(rows, width)
    return row_call(
        target_back_kernel, "target_back", info, (tokens // rows,),
        [block] * 4 + [full(None)] * 2, block, jax.ShapeDtypeStruct((tokens, width), f32),
        [(tokens, width, width)] * 4, (dz, *grads, *head),
    )


def self_weights_kernel(
    info, x_hbm, q_hbm, k_hbm, v_hbm, cross_hbm, dcross_hbm, first_ref, value_ref, ffn_ref, wide_ref,
    mine, other, held, arrived, stage, sent, vectors, vectors_sent,
):
    sources = (cross_hbm, dcross_hbm, x_hbm, q_hbm, k_hbm, v_hbm)
    copies = [
        pltpu.make_async_copy(source, held.at[place], arrived.at[place])
        for place, source in enumerate(sources)
    ]
    for copy in copies:
        copy.start()
    width = x_hbm.shape[1]
    out = (info, stage, sent, mine, other)
    copies[0].wait()
    copies[1].wait()
    put_unit(*out, 3, dot_tn(held[0], held[1]))
    copies[2].wait()
    sums = []
    for number in range(3):
        copies[3 + number].wait()
        put_unit(*out, number, dot_tn(held[2], held[3 + number]))
        sums.append(jnp.sum(held[3 + number].astype(f32), 0, keepdims=True))
    row = lambda ref, number: ref[number : number + 1, :]
    vectors[...] = jnp.concatenate(
        [sums[0], sums[2], row(first_ref, 2), row(first_ref, 3), value_ref[...], row(ffn_ref, 5)]
        + [wide_ref[:, low : low + width] for low in range(0, wide_ref.shape[1], width)]
        + [
            row(ffn_ref, 2), row(first_ref, 0), row(ffn_ref, 3), row(ffn_ref, 0), row(first_ref, 1),
            row(ffn_ref, 4), row(ffn_ref, 1), jnp.zeros((VECTORS - 17, width), f32),
        ],
        0,
    ).astype(bf16)
    ends = [
        pltpu.make_async_copy(vectors, ref.at[pl.ds(2 * width, VECTORS), :], vectors_sent.at[place])
        for place, ref in enumerate((mine, other))
    ]
    for copy in ends:
        copy.start()
    end_units(*out)
    for copy in ends:
        copy.wait()


def self_weights(info, x, grads, cross, sums):
    tokens, width = x.shape
    half = jax.ShapeDtypeStruct((2 * width + VECTORS, width), bf16)
    return row_call(
        self_weights_kernel, "self_weights", info, (),
        [pl.BlockSpec(memory_space=pl.ANY)] * 6 + [full(None)] * 4, [pl.BlockSpec(memory_space=pl.ANY)] * 2,
        [half, half],
        [(tokens, width, width)] * 4, (x, *grads, *cross, *sums),
        [pltpu.VMEM((6, tokens, width), bf16), pltpu.SemaphoreType.DMA((6,))]
        + unit_scratch(width)
        + [pltpu.VMEM((VECTORS, width), bf16), pltpu.SemaphoreType.DMA((2,))],
    )


def ffn_weights_kernel(h_ref, du_ref, a_ref, df_ref, w_hbm, into, outof, sent):
    part = pl.program_id(0)
    blocks, pieces, rows, width = w_hbm.shape
    half = rows // 2
    owners = pieces // blocks if pieces >= blocks else 1
    slot = part % 2

    def copies(part, slot):
        if pieces >= blocks:
            rows_out = w_hbm.at[:, pl.ds(part * owners, owners), pl.ds(half, half), :]
        else:
            rows_out = w_hbm.at[pl.ds(part, 1), :, pl.ds(half, half), :]
        return (
            pltpu.make_async_copy(into.at[slot], w_hbm.at[part, :, pl.ds(0, half), :], sent.at[slot, 0]),
            pltpu.make_async_copy(outof.at[slot], rows_out, sent.at[slot, 1]),
        )

    @pl.when(part >= 2)
    def _():
        for copy in copies(part - 2, slot):
            copy.wait()

    into[slot] = dot_tn(h_ref[...], du_ref[...]).astype(bf16).reshape(pieces, half, width)
    grad_out = dot_tn(a_ref[...], df_ref[...]).astype(bf16)
    for place in range(pieces):
        piece = grad_out[place * half : (place + 1) * half]
        if pieces >= blocks:
            outof[slot, place % blocks, place // blocks] = piece
        else:
            outof[slot, 0, place] = piece
    for copy in copies(part, slot):
        copy.start()

    @pl.when(part == pl.num_programs(0) - 1)
    def _():
        for copy in copies(part - 1, 1 - slot) + copies(part, slot):
            copy.wait()


def ffn_weights(second_low, grad_hidden, active, grad_out, pieces):
    tokens, width = second_low.shape
    blocks = active.shape[1] // width
    whole = pl.BlockSpec((tokens, width), lambda part: (0, 0), pipeline_mode=pl.Buffered(1))
    part = pl.BlockSpec((tokens, width), lambda part: (0, part))
    shape = (blocks, pieces, 2 * width // pieces, width)
    out_shape = (blocks, pieces // blocks) if pieces >= blocks else (1, pieces)
    return pl.pallas_call(
        ffn_weights_kernel,
        grid=(blocks,),
        in_specs=[whole, part, part, whole],
        out_specs=pl.BlockSpec(memory_space=pl.ANY),
        out_shape=jax.ShapeDtypeStruct(shape, bf16),
        scratch_shapes=[
            pltpu.VMEM((2, pieces, width // pieces, width), bf16),
            pltpu.VMEM((2,) + out_shape + (width // pieces, width), bf16),
            pltpu.SemaphoreType.DMA((2, 2)),
        ],
        compiler_params=params(),
        name="ffn_weights",
        cost_estimate=cost([(tokens, width, blocks * width)] * 2),
    )(second_low, grad_hidden, active, grad_out)


def wide(array):
    return array.astype(f32)


def weight_grad(left, right):
    return dot_tn(left, right).astype(bf16)


def forward(
    target, memory, cotangent, info, pieces, head, mid, tail, vectors,
    mid_step=lambda *same: same, mid_last=lambda *same: same,
):
    queries, keys, values = project_self(info, target, head, vectors)
    queries, mid = mid_step(queries, mid)
    context_self, stats_self = self_attend(info, queries, keys, values)
    context_self, mid = mid_last(context_self, mid)
    total_first, first_low, query_cross = first_norm(info, target, context_self, mid, vectors)
    key_cross, value_cross = project_memory(info, memory, mid, vectors)
    context_cross, stats_cross = cross_attend(info, query_cross, key_cross, value_cross)
    output, second_low, active, du, df, do_cross, dz2, dc_cross, sums_ffn, sums_wide = ffn_block(
        info, total_first, context_cross, cotangent, head, tail, vectors
    )
    grad_ffn = ffn_weights(second_low, du, active, df, pieces)
    dq_cross, dk_cross, dv_cross = cross_attend_back(
        info, query_cross, key_cross, value_cross, dc_cross, context_cross, stats_cross
    )
    dz1, do_self, dc_self, sums_first = first_back(info, dz2, dq_cross, total_first, mid, vectors)
    *grad_mid, sum_value = mid_weights(
        info, memory, dk_cross, dv_cross, (first_low, dq_cross, context_self, do_self)
    )
    self_inputs = (queries, keys, values, dc_self, context_self, stats_self)
    cross = (context_cross, do_cross)
    sums = (sums_first, sum_value, sums_ffn, sums_wide)
    return output, grad_ffn, grad_mid, dz1, self_inputs, dk_cross, dv_cross, cross, sums, mid


def forward_back(target, memory, cotangent, info, pieces, head, mid, tail, vectors):
    output, grad_ffn, grad_mid, dz1, self_inputs, dk_cross, dv_cross, cross, sums, mid = forward(
        target, memory, cotangent, info, pieces, head, mid, tail, vectors
    )
    grads = self_attend_back(info, *self_inputs)
    grad_self = self_weights(info, target, grads, cross, sums)
    target_grad = target_back(info, dz1, grads, head)
    memory_grad = memory_back(info, dk_cross, dv_cross, mid, 0, memory.shape[0])
    return (output, target_grad, memory_grad), grad_ffn, grad_mid, grad_self


def pair_swap(array, axis, bit):
    count = lax.axis_size(axis)
    return lax.ppermute(array, axis, [(place, place ^ bit) for place in range(count)])


def ring(array, axis, shift):
    count = lax.axis_size(axis)
    return lax.ppermute(array, axis, [(place, (place + shift) % count) for place in range(count)])


def pick(array, axis, index):
    return lax.dynamic_index_in_dim(array, index, axis, keepdims=False)


def places():
    dp, fsdp = lax.axis_index("dp"), lax.axis_index("fsdp")
    return dp // 2, dp % 2, fsdp // 2, fsdp % 2


def add_half(array, axis, mine, mesh_axis, bit):
    got = pair_swap(pick(array, axis, 1 - mine), mesh_axis, bit)
    return (wide(pick(array, axis, mine)) + wide(got)).astype(bf16)


def add_depth(array, depth):
    total = wide(pick(array, 0, depth))
    for step in (1, 2, 3):
        total = total + wide(ring(pick(array, 0, (depth + step) % 4), "fsdp", 2 * step))
    return total.astype(bf16)


def fence(*arrays):
    return lax.optimization_barrier(arrays)


def add(mine, got):
    return (wide(mine) + wide(got)).astype(bf16)


def cut(array):
    half = array.shape[-2] // 2 // 8 * 8
    return array[..., :half, :], array[..., half:, :]


def join_pair(array, axis, mine, mesh_axis, bit):
    return join(array, pair_swap(array, mesh_axis, bit), axis, mine)


def join(array, got, axis, mine):
    first = jnp.where(mine == 0, array, got)
    second = jnp.where(mine == 0, got, array)
    return jnp.stack([first, second], axis)


def share_dp(array):
    high, core, _, _ = places()
    both = join_pair(array, 0, high, "dp", 2)
    return join_pair(both, 1, core, "dp", 1).reshape((4,) + array.shape)


def join_depth(array, depth):
    parts = [array] + [ring(array, "fsdp", 2 * step) for step in (1, 2, 3)]
    out = jnp.zeros((4,) + array.shape, array.dtype)
    for step, part in enumerate(parts):
        out = lax.dynamic_update_index_in_dim(out, part, (depth - step) % 4, 0)
    return out


def lay_vectors(items, width):
    rows = [jnp.pad(item, ((0, 8 - item.shape[0]), (0, 0))) for item in items]
    row = jnp.concatenate(rows, 1)
    return jnp.pad(row, ((0, 0), (0, width - row.shape[1])))


def gather_vectors(rows, own):
    pieces, _, width = rows.shape
    groups = width // own
    rows = rows.reshape(pieces, 8, groups, own)
    hidden = rows[:, :4, 2].reshape(4, pieces * own)
    rows = jnp.transpose(rows, (2, 1, 0, 3)).reshape(groups * 8, pieces * own)
    return wide(jnp.concatenate([rows[:16], hidden, rows[20:]], 0))


def fast_layer(
    target, memory, cotangent, bucket, source_len, self_qkv, self_out, self_bias, cross_qkv,
    cross_out, cross_bias, ffn_in, ffn_in_bias, ffn_out, ffn_out_bias, norm_gain, norm_bias,
):
    dp = lax.axis_index("dp")
    high, core, depth, side = places()
    count, width = memory.shape[0], target.shape[1]
    own = self_out.shape[0]
    pieces = width // own
    info = jnp.concatenate([bucket, source_len, core[None]])
    vectors = lay_vectors(
        (self_bias, cross_bias, ffn_in_bias.reshape(4, own), ffn_out_bias[None], norm_gain, norm_bias), width
    )
    head = jnp.concatenate([pick(jnp.concatenate([self_qkv, cross_out[None]], 0), 0, dp), vectors], 0)
    mid = pick(jnp.concatenate([self_out[None], cross_qkv], 0), 0, dp)
    head, mid = fence(join_depth(head, depth), mid)
    one, two = cut(head)
    one, two = join_pair(one, 1, side, "fsdp", 1), join_pair(two, 1, high, "dp", 2)
    one, two, mid, ffn_in, ffn_out = fence(one, two, mid, ffn_in, ffn_out)
    one, two = join_pair(one, 2, high, "dp", 2), join_pair(two, 1, side, "fsdp", 1)
    in_cols = pick(ffn_in.reshape(own, 4, width), 1, dp)
    out_rows = pick(ffn_out.reshape(4, own, width), 0, dp)
    tail = lax.all_gather(
        jnp.concatenate([in_cols, out_rows], 0), ("dp", "fsdp"), axis=0, tiled=True
    ).reshape(4, pieces, 2 * own, width)
    half = own // 2
    mine = jnp.concatenate([one, two[:, :, :, :half]], 3).reshape(pieces, 2, own, width)
    mine, mid = fence(mine, join_depth(mid, depth))
    got = pair_swap(mine, "dp", 1)
    vectors = gather_vectors(two[:, :, 0, half:].reshape(pieces, 8, width), own)
    three, four = cut(mid)
    parts = (three, pair_swap(three, "fsdp", 1), four, pair_swap(four, "dp", 2))

    def mid_step(queries, parts):
        queries, three, got_three, four, got_four = fence(queries, *parts)
        three, four = join(three, got_three, 1, side), join(four, got_four, 1, high)
        return queries, (three, pair_swap(three, "dp", 2), four, pair_swap(four, "fsdp", 1))

    def mid_last(context, parts):
        context, three, got_three, four, got_four = fence(context, *parts)
        three, four = join(three, got_three, 2, high), join(four, got_four, 1, side)
        mine = jnp.concatenate([three, four], 3).reshape(pieces, 2, own, width)
        return context, (mine, pair_swap(mine, "dp", 1))

    head = (mine, got)
    output, grad_ffn, grad_mid, dz1, self_inputs, dk_cross, dv_cross, cross, sums, mid = forward(
        target, memory, cotangent, info, pieces, head, parts, tail, vectors, mid_step, mid_last
    )
    sum_ffn = lax.psum_scatter(
        grad_ffn.reshape(-1, width), ("dp", "fsdp"), scatter_dimension=0, tiled=True
    )
    pairs = width // PAIR
    by_owner = lambda rows: rows[: 2 * width].reshape(2, 4, 2, own, width)
    mine, other, queries = fence(*grad_mid, self_inputs[0])
    got = pair_swap(other, "dp", 1)
    grads = self_attend_back(info, queries, *self_inputs[1:], first=0, count=pairs // 2)
    got, *grads = fence(got, *grads)
    one, two = cut(by_owner(add(mine, got)))
    one, two, queries = fence(one, two, queries)
    got_one = pair_swap(pick(one, 0, 1 - high), "dp", 2)
    got_two = pair_swap(pick(two, 2, 1 - side), "fsdp", 1)
    grads = self_attend_back(
        info, queries, *self_inputs[1:], first=pairs // 2, count=pairs // 2, start=tuple(grads)
    )
    got_one, got_two, *grads = fence(got_one, got_two, *grads)
    one, two = add(pick(one, 0, high), got_one), add(pick(two, 2, side), got_two)
    one, two, target_late = fence(one, two, target)
    got_one = pair_swap(pick(one, 1, 1 - side), "fsdp", 1)
    got_two = pair_swap(pick(two, 0, 1 - high), "dp", 2)
    mine, other = self_weights(info, target_late, grads, cross, sums)
    got_one, got_two, mine, other = fence(got_one, got_two, mine, other)
    one, two = add(pick(one, 1, side), got_one), add(pick(two, 0, high), got_two)
    both = jnp.concatenate([one, two], 1)
    both, other, dz1 = fence(both, other, dz1)
    got = pair_swap(other, "dp", 1)
    rings = [ring(pick(both, 0, (depth + step) % 4), "fsdp", 2 * step) for step in (1, 2, 3)]
    target_grad = target_back(info, dz1, grads, head)
    got, *rings, target_grad = fence(got, *rings, target_grad)
    sum_mid = wide(pick(both, 0, depth))
    for item in rings:
        sum_mid = sum_mid + wide(item)
    total = add(mine, got)
    one, two = cut(by_owner(total))
    shape = one.shape
    flat = lambda item: item.reshape(-1, width)
    vectors = total[2 * width :]
    keep, send, vectors, two, dk_cross = fence(
        flat(pick(one, 0, high)), flat(pick(one, 0, 1 - high)), vectors, two, dk_cross
    )
    got_one = pair_swap(jnp.concatenate([send, vectors], 0), "dp", 2)
    got_two = pair_swap(pick(two, 2, 1 - side), "fsdp", 1)
    memory_grad = memory_back(info, dk_cross, dv_cross, mid, 0, count // 2)
    got_one, got_two, memory_grad = fence(got_one, got_two, memory_grad)
    one = add(keep, got_one[:-VECTORS]).reshape(4, 2, -1, width)
    vectors = add(vectors, got_one[-VECTORS:])
    two = add(pick(two, 2, side), got_two)
    keep, send, vectors, two, dk_cross = fence(
        flat(pick(one, 1, side)), flat(pick(one, 1, 1 - side)), vectors, two, dk_cross
    )
    got_one = pair_swap(jnp.concatenate([send, vectors], 0), "fsdp", 1)
    got_two = pair_swap(pick(two, 0, 1 - high), "dp", 2)
    memory_grad = memory_back(
        info, dk_cross, dv_cross, mid, count // 2, count - count // 2, start=(memory_grad,)
    )
    got_one, got_two, memory_grad = fence(got_one, got_two, memory_grad)
    one = add(keep, got_one[:-VECTORS]).reshape(4, -1, width)
    vectors = add(vectors, got_one[-VECTORS:])
    two = add(pick(two, 0, high), got_two)
    both = jnp.concatenate([one, two], 1)
    early = jnp.concatenate([sum_ffn, sum_mid.astype(bf16)], 0)
    both, vectors, early = fence(both, vectors, early)
    rings = [
        ring(jnp.concatenate([pick(both, 0, (depth + step) % 4), vectors], 0), "fsdp", 2 * step)
        for step in (1, 2, 3)
    ]
    early = join_pair(early, 0, high, "dp", 2)
    early, *rings = fence(early, *rings)
    late = jnp.concatenate([pick(both, 0, depth), vectors], 0)
    late = wide(late)
    for item in rings:
        late = late + wide(item)
    vectors = late[-VECTORS:][:17]
    late = join_pair(late[:-VECTORS].astype(bf16), 0, high, "dp", 2)
    early = join_pair(early, 1, core, "dp", 1)
    early, late = fence(early, late)
    late = join_pair(late, 1, core, "dp", 1)
    early = wide(early.reshape((4,) + early.shape[2:]))
    late = wide(late.reshape((4,) + late.shape[2:]))
    grad_in = jnp.swapaxes(early[:, :own], 0, 1).reshape(own, 4 * width)
    grad_out = early[:, own : 2 * own].reshape(4 * own, width)
    mid = early[:, 2 * own :]
    place = lax.axis_index("fsdp")
    hidden = pick(vectors[6:10].reshape(pieces, 4 * own), 0, place)
    vectors = lax.dynamic_slice_in_dim(vectors, place * own, own, 1)
    return (
        output, target_grad, memory_grad, late[:3], mid[0], vectors[:3], mid[1:], late[3], vectors[3:6],
        grad_in, hidden, grad_out, vectors[10], vectors[11:14], vectors[14:17],
    )


def plain_layer(
    target, memory, cotangent, bucket, source_len, self_qkv, self_out, self_bias, cross_qkv,
    cross_out, cross_bias, ffn_in, ffn_in_bias, ffn_out, ffn_out_bias, norm_gain, norm_bias,
):
    gather = lambda item, axis: lax.all_gather(item, "fsdp", axis=axis, tiled=True)
    info = jnp.concatenate([bucket, source_len, jnp.zeros_like(bucket)])
    width = target.shape[1]
    blocks = ffn_out.shape[0] * lax.axis_size("fsdp") // width
    split = lambda units: (units[None, 0::2], units[None, 1::2])
    head = split(jnp.concatenate([gather(self_qkv, 1), gather(cross_out, 0)[None]], 0))
    mid = split(jnp.concatenate([gather(self_out, 0)[None], gather(cross_qkv, 1)], 0))
    ffn_in_w = jnp.swapaxes(gather(ffn_in, 0).reshape(width, blocks, width), 0, 1)
    tail = jnp.concatenate([ffn_in_w, gather(ffn_out, 0).reshape(blocks, width, width)], 1)[:, None]
    vectors = (
        gather(self_bias, 1), gather(cross_bias, 1), gather(ffn_in_bias, 0).reshape(blocks, width),
        gather(ffn_out_bias, 0)[None], gather(norm_gain, 1), gather(norm_bias, 1),
    )
    vectors = wide(
        jnp.concatenate([jnp.pad(item, ((0, 8 - item.shape[0]), (0, 0))) for item in vectors], 0)
    )
    outs, grad_ffn, grad_mid, grad_self = forward_back(
        target, memory, cotangent, info, 1, head, mid, tail, vectors
    )

    def reduce(grad, axis):
        piece = lax.psum_scatter(wide(grad), "fsdp", scatter_dimension=axis, tiled=True)
        return lax.psum(piece, "dp")

    def units(mine, other):
        both = [item[: 2 * width].reshape(2, width, width) for item in (mine, other)]
        return jnp.stack(both, 1).reshape(4, width, width)

    grad_in = jnp.swapaxes(grad_ffn[:, 0, :width], 0, 1).reshape(width, blocks * width)
    grad_out = grad_ffn[:, 0, width:].reshape(blocks * width, width)
    vectors = grad_self[0][2 * width :]
    grad_self, grad_mid = units(*grad_self), units(*grad_mid)
    return outs + (
        reduce(grad_self[:3], 1),
        reduce(grad_mid[0], 0),
        reduce(vectors[:3], 1),
        reduce(grad_mid[1:], 1),
        reduce(grad_self[3], 0),
        reduce(vectors[3:6], 1),
        reduce(grad_in, 0),
        reduce(vectors[6 : 6 + blocks].reshape(-1), 0),
        reduce(grad_out, 0),
        reduce(vectors[10], 0),
        reduce(vectors[11:14], 1),
        reduce(vectors[14:17], 1),
    )


def solution(mesh):
    rows = P(("dp", "fsdp"))
    first = P("fsdp")
    second = P(None, "fsdp")
    weights = (second, first, second, second, first, second, first, first, first, first, second, second)
    layer = fast_layer if (mesh.shape["dp"], mesh.shape["fsdp"]) == (4, 8) else plain_layer
    return jax.shard_map(
        layer,
        mesh=mesh,
        in_specs=(rows,) * 5 + weights,
        out_specs=(rows,) * 3 + weights,
        check_vma=False,
    )
```

```python
import functools
import math
import jax
import jax.numpy as jnp
from jax import lax
from jax.sharding import PartitionSpec as P
from jax.experimental import pallas as pl
from jax.experimental.pallas import tpu as pltpu

HEAD = 64
PAIR = 2 * HEAD
BLOCK = 256
very_low = -1e30
VMEM_LIMIT = 60 * 2**20
f32 = jnp.float32
bf16 = jnp.bfloat16


def dot_nt(left, right):
    return lax.dot_general(left, right, (((1,), (1,)), ((), ())), preferred_element_type=f32)


def dot_nn(left, right):
    return lax.dot_general(left, right, (((1,), (0,)), ((), ())), preferred_element_type=f32)


def dot_tn(left, right):
    return lax.dot_general(left, right, (((0,), (0,)), ((), ())), preferred_element_type=f32)


def split_pair(pair):
    lane = lax.broadcasted_iota(jnp.int32, pair.shape, 1)
    none = jnp.zeros_like(pair)
    return (jnp.where(lane < HEAD, pair, none), jnp.where(lane < HEAD, none, pair))


def mask_tail(scores, valid):
    width = scores.shape[0]
    if width == BLOCK:
        return jnp.where(valid, scores, very_low)
    return jnp.concatenate(
        [scores[: width - BLOCK], jnp.where(valid, scores[width - BLOCK :], very_low)], 0
    )


def stacked(pair):
    return jnp.concatenate(split_pair(pair), 0)


def score_tile(queries, keys, valid):
    return mask_tail(dot_nt(keys, stacked(queries)), valid)


def attend_tile(scores, values):
    count = scores.shape[1] // 2
    values_t = values.T
    highest = jnp.max(scores, 0, keepdims=True)
    raised = jnp.exp(scores - highest)
    summed = jnp.sum(raised, 0, keepdims=True)
    raised = raised.astype(bf16)
    context = jnp.concatenate(
        [
            dot_nn(values_t[half * HEAD : (half + 1) * HEAD], raised[:, half * count : (half + 1) * count])
            / summed[:, half * count : (half + 1) * count]
            for half in range(2)
        ],
        0,
    )
    return context.T.astype(bf16), highest + jnp.log(summed)


def head_sums(pair):
    turned = pair.T
    return jnp.concatenate(
        [jnp.sum(turned[half * HEAD : (half + 1) * HEAD], 0, keepdims=True) for half in range(2)], 1
    )


def back_tile(scores, queries, keys, values, grads, contexts, logsum):
    count = scores.shape[1] // 2
    grad_rows = stacked(grads)
    grad_shares = dot_nt(values, grad_rows)
    inner = head_sums(grads.astype(f32) * contexts.astype(f32))
    keys_t = keys.T
    shares = jnp.exp(scores - logsum)
    grad_scores = (shares * (grad_shares - inner)).astype(bf16)
    grad_values = dot_nn(shares.astype(bf16), grad_rows)
    grad_keys = dot_nn(grad_scores, stacked(queries))
    grad_queries = jnp.concatenate(
        [
            dot_nn(keys_t[half * HEAD : (half + 1) * HEAD], grad_scores[:, half * count : (half + 1) * count])
            for half in range(2)
        ],
        0,
    ).T
    grad_queries = (grad_queries.astype(bf16).astype(f32) * HEAD**-0.5).astype(bf16)
    return grad_queries, grad_keys, grad_values


def causal(columns):
    key = lax.broadcasted_iota(jnp.int32, (BLOCK, columns), 0)
    query = lax.broadcasted_iota(jnp.int32, (BLOCK, columns), 1) % BLOCK
    return key <= query


def key_spans(tokens, whole):
    return [
        (0 if whole else low, low, low + BLOCK) for low in range(0, tokens, BLOCK)
    ]


def self_kernel(skip, info, q_ref, k_ref, v_ref, o_ref, stat_ref):
    tokens = q_ref.shape[0]
    valid = causal(2 * BLOCK)

    def run(whole):
        spans = key_spans(tokens, whole)
        score = lambda span: score_tile(q_ref[span[1] : span[2], :], k_ref[span[0] : span[2], :], valid)
        ahead = score(spans[0])
        for part, (low, start, stop) in enumerate(spans):
            scores = ahead
            if part + 1 < len(spans):
                ahead = score(spans[part + 1])
            o_ref[start:stop, :], stat_ref[0, part] = attend_tile(scores, v_ref[low:stop, :])

    pl.when(info[0] == 1)(functools.partial(run, False))
    pl.when(info[0] != 1)(functools.partial(run, True))


def self_back_kernel(skip, info, q_ref, k_ref, v_ref, g_ref, o_ref, stat_ref, *refs):
    dq_ref, dk_ref, dv_ref, key_sum, value_sum = refs[skip:]
    tokens = q_ref.shape[0]
    valid = causal(2 * BLOCK)

    def run(whole):
        spans = key_spans(tokens, whole)[::-1]
        score = lambda span: score_tile(q_ref[span[1] : span[2], :], k_ref[span[0] : span[2], :], valid)
        ahead = score(spans[0])
        for step, (low, start, stop) in enumerate(spans):
            scores = ahead
            if step + 1 < len(spans):
                ahead = score(spans[step + 1])
            dq_ref[start:stop, :], grad_keys, grad_values = back_tile(
                scores,
                q_ref[start:stop, :],
                k_ref[low:stop, :],
                v_ref[low:stop, :],
                g_ref[start:stop, :],
                o_ref[start:stop, :],
                stat_ref[0, start // BLOCK],
            )
            if not whole:
                dk_ref[start:stop, :] = grad_keys.astype(bf16)
                dv_ref[start:stop, :] = grad_values.astype(bf16)
            elif stop == tokens:
                key_sum[...] = grad_keys
                value_sum[...] = grad_values
            else:
                key_sum[:stop, :] += grad_keys
                value_sum[:stop, :] += grad_values
        if whole:
            dk_ref[...] = key_sum[...].astype(bf16)
            dv_ref[...] = value_sum[...].astype(bf16)

    pl.when(info[0] == 1)(functools.partial(run, False))
    pl.when(info[0] != 1)(functools.partial(run, True))


def by_length(info, row, mem_len, run):
    length = info[1 + row]
    for width in range(BLOCK, mem_len + 1, BLOCK):

        @pl.when((length > width - BLOCK) & (length <= width))
        def _(width=width):
            run(width, lambda columns: lax.broadcasted_iota(jnp.int32, (BLOCK, columns), 0) < length - (width - BLOCK))


def cross_kernel(skip, info, q_ref, k_ref, v_ref, o_ref, stat_ref):
    tokens = q_ref.shape[0]
    count, mem_len, _ = k_ref.shape
    parts = tokens // BLOCK

    @pl.when(info[0] == 1)
    def _():
        def step(row, none):
            rows = pl.ds(pl.multiple_of(row * BLOCK, BLOCK), BLOCK)

            def run(width, valid):
                scores = score_tile(q_ref[rows, :], k_ref[row, :width, :], valid(2 * BLOCK))
                o_ref[rows, :], stat_ref[0, row] = attend_tile(scores, v_ref[row, :width, :])

            by_length(info, row, mem_len, run)
            return none

        lax.fori_loop(0, count, step, None)

    @pl.when(info[0] != 1)
    def _():
        def run(width, valid):
            scores = score_tile(q_ref[...], k_ref[0, :width, :], valid(2 * tokens))
            o_ref[...], stats = attend_tile(scores, v_ref[0, :width, :])
            for part in range(parts):
                low = part * BLOCK
                stat_ref[0, part] = jnp.concatenate(
                    [stats[:, low : low + BLOCK], stats[:, tokens + low : tokens + low + BLOCK]], 1
                )

        by_length(info, 0, mem_len, run)


def cross_back_kernel(skip, info, q_ref, k_ref, v_ref, g_ref, o_ref, stat_ref, *refs):
    dq_ref, dk_ref, dv_ref = refs[skip:]
    tokens = q_ref.shape[0]
    count, mem_len, _ = k_ref.shape
    parts = tokens // BLOCK

    def store(row, width, grad_keys, grad_values):
        dk_ref[row, :width, :] = grad_keys.astype(bf16)
        dv_ref[row, :width, :] = grad_values.astype(bf16)
        if width < mem_len:
            rest = jnp.zeros((mem_len - width, PAIR), bf16)
            dk_ref[row, width:, :] = rest
            dv_ref[row, width:, :] = rest

    @pl.when(info[0] == 1)
    def _():
        def step(row, none):
            rows = pl.ds(pl.multiple_of(row * BLOCK, BLOCK), BLOCK)

            def run(width, valid):
                keys = k_ref[row, :width, :]
                scores = score_tile(q_ref[rows, :], keys, valid(2 * BLOCK))
                dq_ref[rows, :], grad_keys, grad_values = back_tile(
                    scores, q_ref[rows, :], keys, v_ref[row, :width, :], g_ref[rows, :], o_ref[rows, :],
                    stat_ref[0, row],
                )
                store(row, width, grad_keys, grad_values)

            by_length(info, row, mem_len, run)
            return none

        lax.fori_loop(0, count, step, None)

    @pl.when(info[0] != 1)
    def _():
        def run(width, valid):
            keys = k_ref[0, :width, :]
            scores = score_tile(q_ref[...], keys, valid(2 * tokens))
            stats = jnp.concatenate(
                [stat_ref[0, part][:, half * BLOCK : (half + 1) * BLOCK] for half in range(2) for part in range(parts)],
                1,
            )
            dq_ref[...], grad_keys, grad_values = back_tile(
                scores, q_ref[...], keys, v_ref[0, :width, :], g_ref[...], o_ref[...], stats
            )
            store(0, width, grad_keys, grad_values)

        by_length(info, 0, mem_len, run)


def params():
    return pltpu.CompilerParams(vmem_limit_bytes=VMEM_LIMIT)


def cost(matmuls, moved=2**23):
    flops = 2 * sum(math.prod(sizes) for sizes in matmuls)
    return pl.CostEstimate(flops=flops, bytes_accessed=moved, transcendentals=0)


def attend_call(kernel, name, info, queries, keys, values, rest=None, first=0, count=None, start=()):
    tokens, width = queries.shape
    pairs = width // PAIR
    count = count or pairs
    parts = tokens // BLOCK
    back = rest is not None
    own = pl.BlockSpec((tokens, PAIR), lambda pair, info: (0, pair + first))
    stat = pl.BlockSpec((1, parts, 1, 2 * BLOCK), lambda pair, info: (pair + first, 0, 0, 0))
    if keys.ndim == 2:
        other = own
        scratch = [pltpu.VMEM((tokens, PAIR), f32)] * 2 if back else []
    else:
        other = pl.BlockSpec(keys.shape[:2] + (PAIR,), lambda pair, info: (0, 0, pair + first))
        scratch = []
    queries_shape = jax.ShapeDtypeStruct((tokens, width), bf16)
    keys_shape = jax.ShapeDtypeStruct(keys.shape, bf16)
    stat_shape = jax.ShapeDtypeStruct((pairs, parts, 1, 2 * BLOCK), f32)
    inputs = (queries, keys, values) + (rest or ())
    return pl.pallas_call(
        functools.partial(kernel, len(start)),
        grid_spec=pltpu.PrefetchScalarGridSpec(
            num_scalar_prefetch=1,
            grid=(count,),
            in_specs=[own, other, other]
            + ([own, own, stat] if back else [])
            + [pl.BlockSpec(memory_space=pl.ANY)] * len(start),
            out_specs=[own, other, other] if back else [own, stat],
            scratch_shapes=scratch,
        ),
        out_shape=[queries_shape, keys_shape, keys_shape] if back else [queries_shape, stat_shape],
        input_output_aliases={1 + len(inputs) + place: place for place in range(len(start))},
        compiler_params=params(),
        name=name,
        cost_estimate=cost([(tokens, tokens, width)] * (24 if back else 12)),
    )(info, *inputs, *start)


def self_attend(info, queries, keys, values):
    return attend_call(self_kernel, "self_attend", info, queries, keys, values)


def cross_attend(info, queries, keys, values):
    return attend_call(cross_kernel, "cross_attend", info, queries, keys, values)


def self_attend_back(info, queries, keys, values, *rest, **span):
    return attend_call(self_back_kernel, "self_attend_back", info, queries, keys, values, rest, **span)


def cross_attend_back(info, queries, keys, values, *rest, **span):
    return attend_call(cross_back_kernel, "cross_attend_back", info, queries, keys, values, rest, **span)


epsilon = 1e-05
VECTORS = 32


def normalise(total):
    middle = jnp.mean(total, -1, keepdims=True)
    centred = total - middle
    variance = jnp.mean(centred * centred, -1, keepdims=True)
    scale = lax.rsqrt(variance + epsilon)
    return centred * scale, scale


def normalise_back(grad, gain, normal, scale):
    scaled = grad * gain
    first = jnp.mean(scaled, -1, keepdims=True)
    second = jnp.mean(scaled * normal, -1, keepdims=True)
    return (scaled - first - normal * second) * scale


def add_rows(ref, row, value):
    ref[row : row + 1, :] += jnp.sum(value, 0, keepdims=True)


def start_sums(*refs):
    @pl.when(pl.program_id(0) == 0)
    def _():
        for ref in refs:
            ref[...] = jnp.zeros_like(ref)


def full(array):
    return pl.BlockSpec(memory_space=pltpu.VMEM)


def row_block(rows, width):
    return pl.BlockSpec((rows, width), lambda part, *info: (part, 0))


def keep_block(rows, width):
    return pl.BlockSpec((rows, width), lambda part, *info: (0, 0))


def unit(ref, high=0):
    return ref[:, high].reshape(ref.shape[0] * ref.shape[2], ref.shape[3])


def by_core(info, mine, got, run):
    core = info[info.shape[0] - 1]
    pl.when(core == 0)(lambda: run(mine, got))
    pl.when(core != 0)(lambda: run(got, mine))


def unit_block(array, high):
    return pl.BlockSpec(
        array.shape[:1] + (1,) + array.shape[2:],
        lambda *place: (0, high, 0, 0),
        pipeline_mode=pl.Buffered(1),
    )


def first_kernel(info, x_ref, c_ref, mine, got, vec_ref, z_ref, low_ref, q_ref):
    def run(even, odd):
        total = x_ref[...].astype(f32) + dot_nn(c_ref[...], unit(even)) + vec_ref[2 : 3, :]
        normal, _ = normalise(total)
        first_low = (normal * vec_ref[32 : 33, :] + vec_ref[40 : 41, :]).astype(bf16)
        z_ref[...] = total
        low_ref[...] = first_low
        q_ref[...] = ((dot_nn(first_low, unit(odd)) + vec_ref[8 : 9, :]) * HEAD**-0.5).astype(bf16)

    by_core(info, mine, got, run)


def row_call(
    kernel, name, info, grid, in_specs, out_specs, out_shape, matmuls, inputs, scratch=(), aliases=None, limit=VMEM_LIMIT
):
    return pl.pallas_call(
        kernel,
        grid_spec=pltpu.PrefetchScalarGridSpec(
            num_scalar_prefetch=1,
            grid=grid,
            in_specs=in_specs,
            out_specs=out_specs,
            scratch_shapes=scratch,
        ),
        out_shape=out_shape,
        input_output_aliases=aliases or {},
        compiler_params=pltpu.CompilerParams(vmem_limit_bytes=limit),
        name=name,
        cost_estimate=cost(matmuls),
    )(info, *inputs)


def first_norm(info, x, context, mid, vectors, rows=256):
    tokens, width = x.shape
    block = row_block(rows, width)
    low = jax.ShapeDtypeStruct((tokens, width), bf16)
    return row_call(
        first_kernel, "first_norm", info, (tokens // rows,),
        [block, block, unit_block(mid[0], 0), unit_block(mid[1], 0), full(vectors)],
        [block] * 3, [jax.ShapeDtypeStruct((tokens, width), f32), low, low],
        [(tokens, width, width)] * 4, (x, context, *mid, vectors),
    )


def chunks(blocks, pieces, block):
    return [divmod(number, blocks) for number in range(block * pieces, (block + 1) * pieces)]


def ffn_kernel(
    info,
    z_ref,
    c_ref,
    cot_ref,
    mine,
    got,
    tail_ref,
    vec_ref,
    out_ref,
    low_ref,
    act_ref,
    du_ref,
    df_ref,
    do_ref,
    dz_ref,
    dc_ref,
    sum_ref,
    wide_ref,
    slope_ref,
    out_w,
):
    start_sums(sum_ref, wide_ref)

    @pl.when(pl.program_id(0) == 0)
    def _():
        def load(even, odd):
            out_w[...] = unit(odd)

        by_core(info, mine, got, load)

    width = z_ref.shape[1]
    blocks, pieces, both = tail_ref.shape[:3]
    in_w = lambda block: tail_ref[block, :, : both // 2].reshape(width, width)
    ffn_w = lambda block: jnp.concatenate(
        [tail_ref[d, f, both // 2 :, :] for f, d in chunks(blocks, pieces, block)], 0
    )
    gain_first, gain_mid, gain_last = [vec_ref[row : row + 1, :] for row in (32, 33, 34)]
    shift_first, shift_mid, shift_last = [vec_ref[row : row + 1, :] for row in (40, 41, 42)]
    normal_first, _ = normalise(z_ref[...])
    first = normal_first * gain_first + shift_first
    normal_mid, scale_mid = normalise(first + dot_nn(c_ref[...], out_w[...]) + vec_ref[10 : 11, :])
    second = normal_mid * gain_mid + shift_mid
    second_low = second.astype(bf16)
    low_ref[...] = second_low
    total = second + vec_ref[24 : 25, :]
    ahead = dot_nn(second_low, in_w(0))
    for block in range(blocks):
        cols = pl.ds(block * width, width)
        value = ahead + vec_ref[16 + block : 17 + block, :]
        if block + 1 < blocks:
            ahead = dot_nn(second_low, in_w(block + 1))
        share = 0.5 * (1.0 + lax.erf(value * 0.5**0.5))
        density = jnp.exp(-0.5 * value * value) * 0.3989422804014327
        active = (value * share).astype(bf16)
        slope_ref[:, cols] = share + value * density
        act_ref[:, cols] = active
        total = total + dot_nn(active, ffn_w(block))
    normal_last, scale_last = normalise(total)
    out_ref[...] = (normal_last * gain_last + shift_last).astype(bf16)
    cot = cot_ref[...].astype(f32)
    add_rows(sum_ref, 0, cot * normal_last)
    add_rows(sum_ref, 1, cot)
    grad_last = normalise_back(cot, gain_last, normal_last, scale_last)
    grad_low = grad_last.astype(bf16)
    df_ref[...] = grad_low
    add_rows(sum_ref, 2, grad_low.astype(f32))
    grad_second = grad_last
    ahead = dot_nt(grad_low, ffn_w(0))
    for block in range(blocks):
        cols = pl.ds(block * width, width)
        grad_hidden = (ahead * slope_ref[:, cols]).astype(bf16)
        if block + 1 < blocks:
            ahead = dot_nt(grad_low, ffn_w(block + 1))
        du_ref[:, cols] = grad_hidden
        wide_ref[:, cols] += jnp.sum(grad_hidden.astype(f32), 0, keepdims=True)
        grad_second = grad_second + dot_nt(grad_hidden, in_w(block))
    add_rows(sum_ref, 3, grad_second * normal_mid)
    add_rows(sum_ref, 4, grad_second)
    grad_mid = normalise_back(grad_second, gain_mid, normal_mid, scale_mid)
    dz_ref[...] = grad_mid
    grad_low = grad_mid.astype(bf16)
    do_ref[...] = grad_low
    add_rows(sum_ref, 5, grad_low.astype(f32))
    dc_ref[...] = dot_nt(grad_low, out_w[...]).astype(bf16)


def ffn_block(info, z, context, cotangent, head, tail, vectors, rows=256):
    tokens, width = z.shape
    hidden = tail.shape[0] * width
    block = row_block(rows, width)
    wide = row_block(rows, hidden)
    narrow_shape = jax.ShapeDtypeStruct((tokens, width), bf16)
    wide_shape = jax.ShapeDtypeStruct((tokens, hidden), bf16)
    return row_call(
        ffn_kernel, "ffn_block", info, (tokens // rows,),
        [block] * 3 + [unit_block(head[0], 1), unit_block(head[1], 1), full(tail), full(vectors)],
        [block, block, wide, wide, block, block, block, block, keep_block(8, width), keep_block(1, hidden)],
        [
            narrow_shape, narrow_shape, wide_shape, wide_shape, narrow_shape, narrow_shape,
            jax.ShapeDtypeStruct((tokens, width), f32), narrow_shape,
            jax.ShapeDtypeStruct((8, width), f32), jax.ShapeDtypeStruct((1, hidden), f32),
        ],
        [(tokens, width, hidden)] * 8, (z, context, cotangent, *head, tail, vectors),
        [pltpu.VMEM((rows, hidden), f32), pltpu.VMEM((width, width), bf16)],
    )


def first_back_kernel(info, dz2_ref, dq_ref, z_ref, mine, got, vec_ref, dz_ref, do_ref, dc_ref, sum_ref):
    start_sums(sum_ref)

    def run(even, odd):
        grad_query = dq_ref[...]
        grad_first = dz2_ref[...] + dot_nt(grad_query, unit(odd))
        normal, scale = normalise(z_ref[...])
        add_rows(sum_ref, 0, grad_first * normal)
        add_rows(sum_ref, 1, grad_first)
        grad_start = normalise_back(grad_first, vec_ref[32 : 33, :], normal, scale)
        dz_ref[...] = grad_start
        grad_low = grad_start.astype(bf16)
        do_ref[...] = grad_low
        add_rows(sum_ref, 2, grad_low.astype(f32))
        add_rows(sum_ref, 3, grad_query.astype(f32))
        dc_ref[...] = dot_nt(grad_low, unit(even)).astype(bf16)

    by_core(info, mine, got, run)


def first_back(info, dz2, grad_query, z, mid, vectors, rows=256):
    tokens, width = z.shape
    block = row_block(rows, width)
    low = jax.ShapeDtypeStruct((tokens, width), bf16)
    return row_call(
        first_back_kernel, "first_back", info, (tokens // rows,),
        [block] * 3 + [unit_block(mid[0], 0), unit_block(mid[1], 0), full(vectors)],
        [block] * 3 + [keep_block(8, width)],
        [jax.ShapeDtypeStruct((tokens, width), f32), low, low, jax.ShapeDtypeStruct((8, width), f32)],
        [(tokens, width, width)] * 4, (dz2, grad_query, z, *mid, vectors),
    )


def needed(info, row, part, rows):
    return ((info[0] == 1) | (row == 0)) & (part * rows < info[1 + row])


def needed_place(info, row, part, rows):
    used = jnp.where(info[0] == 1, row, 0)
    last = (info[1 + used] + rows - 1) // rows - 1
    return used, jnp.where(info[0] == 1, jnp.minimum(part, last), jnp.where(row == 0, jnp.minimum(part, last), last))


def project_kernel(rows, info, m_ref, mine, got, b_ref, k_ref, v_ref):
    @pl.when(needed(info, pl.program_id(0), pl.program_id(1), rows))
    def _():
        def run(even, odd):
            memory = m_ref[0]
            k_ref[0] = dot_nn(memory, unit(even)).astype(bf16)
            v_ref[0] = (dot_nn(memory, unit(odd)) + b_ref[9 : 10, :]).astype(bf16)

        by_core(info, mine, got, run)


def memory_block(rows, width, first=0):
    return pl.BlockSpec(
        (1, rows, width), lambda row, part, info: needed_place(info, row + first, part, rows) + (0,)
    )


def project_memory(info, memory, mid, vectors, rows=512):
    count, length, width = memory.shape
    block = memory_block(rows, width)
    return row_call(
        functools.partial(project_kernel, rows), "project_memory", info, (count, length // rows),
        [block, unit_block(mid[0], 1), unit_block(mid[1], 1), full(vectors)], [block] * 2,
        [jax.ShapeDtypeStruct(memory.shape, bf16)] * 2,
        [(count, length, width, width)] * 2, (memory, *mid, vectors),
    )


def memory_back_kernel(rows, first, info, dk_ref, dv_ref, mine, got, *refs):
    out_ref = refs[-1]
    here = needed(info, pl.program_id(0) + first, pl.program_id(1), rows)

    @pl.when(here)
    def _():
        def run(even, odd):
            out_ref[0] = dot_nt(dk_ref[0], unit(even)) + dot_nt(dv_ref[0], unit(odd))

        by_core(info, mine, got, run)

    @pl.when(jnp.logical_not(here))
    def _():
        out_ref[...] = jnp.zeros_like(out_ref)


def memory_back(info, grad_keys, grad_values, mid, first, count, start=(), rows=512):
    length, width = grad_keys.shape[1:]
    block = memory_block(rows, width, first)
    return row_call(
        functools.partial(memory_back_kernel, rows, first), "memory_back", info, (count, length // rows),
        [block, block, unit_block(mid[0], 1), unit_block(mid[1], 1)]
        + [pl.BlockSpec(memory_space=pl.ANY)] * len(start),
        pl.BlockSpec((1, rows, width), lambda row, part, info: (row + first, part, 0)),
        jax.ShapeDtypeStruct(grad_keys.shape, f32),
        [(count, length, width, width)] * 2, (grad_keys, grad_values, *mid, *start),
        aliases={5: 0} if start else {},
    )


def unit_copy(info, stage, sent, mine, other, number, act):
    width = stage.shape[1]
    here = info[info.shape[0] - 1] == number % 2
    for ref, chosen in ((mine, here), (other, jnp.logical_not(here))):

        @pl.when(chosen)
        def _(ref=ref):
            rows = ref.at[pl.ds(number // 2 * width, width), :]
            act(pltpu.make_async_copy(stage.at[number], rows, sent.at[number]))


def put_unit(info, stage, sent, mine, other, number, value):
    stage[number] = value.astype(bf16)
    unit_copy(info, stage, sent, mine, other, number, lambda copy: copy.start())


def end_units(info, stage, sent, mine, other):
    for number in range(4):
        unit_copy(info, stage, sent, mine, other, number, lambda copy: copy.wait())


def unit_scratch(width):
    return [pltpu.VMEM((4, width, width), bf16), pltpu.SemaphoreType.DMA((4,))]


def mid_weights_kernel(
    rows, info, m_ref, dk_ref, dv_ref, first_ref, dq_ref, self_ref, dself_ref,
    mine, other, sum_ref, key_sum, value_sum, stage, sent,
):
    row, part = pl.program_id(0), pl.program_id(1)
    out = (info, stage, sent, mine, other)

    @pl.when((row == 0) & (part == 0))
    def _():
        put_unit(*out, 0, dot_tn(self_ref[...], dself_ref[...]))
        put_unit(*out, 1, dot_tn(first_ref[...], dq_ref[...]))
        key_sum[...] = jnp.zeros_like(key_sum)
        value_sum[...] = jnp.zeros_like(value_sum)
        sum_ref[...] = jnp.zeros_like(sum_ref)

    @pl.when(needed(info, row, part, rows))
    def _():
        memory = m_ref[0]
        key_sum[...] += dot_tn(memory, dk_ref[0])
        value_sum[...] += dot_tn(memory, dv_ref[0])
        sum_ref[...] += jnp.sum(dv_ref[0].astype(f32), 0, keepdims=True)

    @pl.when((row == pl.num_programs(0) - 1) & (part == pl.num_programs(1) - 1))
    def _():
        put_unit(*out, 2, key_sum[...])
        put_unit(*out, 3, value_sum[...])
        end_units(*out)


def mid_weights(info, memory, grad_keys, grad_values, pairs):
    count, rows, width = memory.shape
    block = memory_block(rows, width)
    half = jax.ShapeDtypeStruct((2 * width, width), bf16)
    return row_call(
        functools.partial(mid_weights_kernel, rows), "mid_weights", info, (count, 1),
        [block] * 3 + [full(None)] * 4,
        [pl.BlockSpec(memory_space=pl.ANY)] * 2 + [pl.BlockSpec((1, width), lambda row, part, info: (0, 0))],
        [half, half, jax.ShapeDtypeStruct((1, width), f32)],
        [(count, rows, width, width)] * 2, (memory, grad_keys, grad_values, *pairs),
        [pltpu.VMEM((width, width), f32)] * 2 + unit_scratch(width),
    )


def qkv_kernel(info, x_ref, mine, got, vec_ref, q_ref, k_ref, v_ref):
    def run(even, odd):
        x = x_ref[...]
        q_ref[...] = ((dot_nn(x, unit(even, 0)) + vec_ref[0 : 1, :]) * HEAD**-0.5).astype(bf16)
        k_ref[...] = dot_nn(x, unit(odd, 0)).astype(bf16)
        v_ref[...] = (dot_nn(x, unit(even, 1)) + vec_ref[1 : 2, :]).astype(bf16)

    by_core(info, mine, got, run)


def project_self(info, x, head, vectors, rows=512):
    tokens, width = x.shape
    block = row_block(rows, width)
    return row_call(
        qkv_kernel, "project_self", info, (tokens // rows,),
        [block, full(None), full(None), full(None)], [block] * 3,
        [jax.ShapeDtypeStruct((tokens, width), bf16)] * 3,
        [(tokens, width, width)] * 4, (x, *head, vectors),
    )


def target_back_kernel(info, z_ref, q_ref, k_ref, v_ref, mine, got, out_ref):
    def run(even, odd):
        out_ref[...] = (
            z_ref[...]
            + dot_nt(q_ref[...], unit(even, 0))
            + dot_nt(k_ref[...], unit(odd, 0))
            + dot_nt(v_ref[...], unit(even, 1))
        )

    by_core(info, mine, got, run)


def target_back(info, dz, grads, head, rows=256):
    tokens, width = dz.shape
    block = row_block(rows, width)
    return row_call(
        target_back_kernel, "target_back", info, (tokens // rows,),
        [block] * 4 + [full(None)] * 2, block, jax.ShapeDtypeStruct((tokens, width), f32),
        [(tokens, width, width)] * 4, (dz, *grads, *head),
    )


def self_weights_kernel(
    info, x_hbm, q_hbm, k_hbm, v_hbm, cross_hbm, dcross_hbm, first_ref, value_ref, ffn_ref, wide_ref,
    mine, other, held, arrived, stage, sent, vectors, vectors_sent,
):
    sources = (cross_hbm, dcross_hbm, x_hbm, q_hbm, k_hbm, v_hbm)
    copies = [
        pltpu.make_async_copy(source, held.at[place], arrived.at[place])
        for place, source in enumerate(sources)
    ]
    for copy in copies:
        copy.start()
    width = x_hbm.shape[1]
    out = (info, stage, sent, mine, other)
    copies[0].wait()
    copies[1].wait()
    put_unit(*out, 3, dot_tn(held[0], held[1]))
    copies[2].wait()
    sums = []
    for number in range(3):
        copies[3 + number].wait()
        put_unit(*out, number, dot_tn(held[2], held[3 + number]))
        sums.append(jnp.sum(held[3 + number].astype(f32), 0, keepdims=True))
    row = lambda ref, number: ref[number : number + 1, :]
    vectors[...] = jnp.concatenate(
        [sums[0], sums[2], row(first_ref, 2), row(first_ref, 3), value_ref[...], row(ffn_ref, 5)]
        + [wide_ref[:, low : low + width] for low in range(0, wide_ref.shape[1], width)]
        + [
            row(ffn_ref, 2), row(first_ref, 0), row(ffn_ref, 3), row(ffn_ref, 0), row(first_ref, 1),
            row(ffn_ref, 4), row(ffn_ref, 1), jnp.zeros((VECTORS - 17, width), f32),
        ],
        0,
    ).astype(bf16)
    ends = [
        pltpu.make_async_copy(vectors, ref.at[pl.ds(2 * width, VECTORS), :], vectors_sent.at[place])
        for place, ref in enumerate((mine, other))
    ]
    for copy in ends:
        copy.start()
    end_units(*out)
    for copy in ends:
        copy.wait()


def self_weights(info, x, grads, cross, sums):
    tokens, width = x.shape
    half = jax.ShapeDtypeStruct((2 * width + VECTORS, width), bf16)
    return row_call(
        self_weights_kernel, "self_weights", info, (),
        [pl.BlockSpec(memory_space=pl.ANY)] * 6 + [full(None)] * 4, [pl.BlockSpec(memory_space=pl.ANY)] * 2,
        [half, half],
        [(tokens, width, width)] * 4, (x, *grads, *cross, *sums),
        [pltpu.VMEM((6, tokens, width), bf16), pltpu.SemaphoreType.DMA((6,))]
        + unit_scratch(width)
        + [pltpu.VMEM((VECTORS, width), bf16), pltpu.SemaphoreType.DMA((2,))],
    )


def ffn_weights_kernel(h_ref, du_ref, a_ref, df_ref, w_hbm, into, outof, sent):
    part = pl.program_id(0)
    blocks, pieces, rows, width = w_hbm.shape
    half = rows // 2
    owners = pieces // blocks if pieces >= blocks else 1
    slot = part % 2

    def copies(part, slot):
        if pieces >= blocks:
            rows_out = w_hbm.at[:, pl.ds(part * owners, owners), pl.ds(half, half), :]
        else:
            rows_out = w_hbm.at[pl.ds(part, 1), :, pl.ds(half, half), :]
        return (
            pltpu.make_async_copy(into.at[slot], w_hbm.at[part, :, pl.ds(0, half), :], sent.at[slot, 0]),
            pltpu.make_async_copy(outof.at[slot], rows_out, sent.at[slot, 1]),
        )

    @pl.when(part >= 2)
    def _():
        for copy in copies(part - 2, slot):
            copy.wait()

    into[slot] = dot_tn(h_ref[...], du_ref[...]).astype(bf16).reshape(pieces, half, width)
    grad_out = dot_tn(a_ref[...], df_ref[...]).astype(bf16)
    for place in range(pieces):
        piece = grad_out[place * half : (place + 1) * half]
        if pieces >= blocks:
            outof[slot, place % blocks, place // blocks] = piece
        else:
            outof[slot, 0, place] = piece
    for copy in copies(part, slot):
        copy.start()

    @pl.when(part == pl.num_programs(0) - 1)
    def _():
        for copy in copies(part - 1, 1 - slot) + copies(part, slot):
            copy.wait()


def ffn_weights(second_low, grad_hidden, active, grad_out, pieces):
    tokens, width = second_low.shape
    blocks = active.shape[1] // width
    whole = pl.BlockSpec((tokens, width), lambda part: (0, 0), pipeline_mode=pl.Buffered(1))
    part = pl.BlockSpec((tokens, width), lambda part: (0, part))
    shape = (blocks, pieces, 2 * width // pieces, width)
    out_shape = (blocks, pieces // blocks) if pieces >= blocks else (1, pieces)
    return pl.pallas_call(
        ffn_weights_kernel,
        grid=(blocks,),
        in_specs=[whole, part, part, whole],
        out_specs=pl.BlockSpec(memory_space=pl.ANY),
        out_shape=jax.ShapeDtypeStruct(shape, bf16),
        scratch_shapes=[
            pltpu.VMEM((2, pieces, width // pieces, width), bf16),
            pltpu.VMEM((2,) + out_shape + (width // pieces, width), bf16),
            pltpu.SemaphoreType.DMA((2, 2)),
        ],
        compiler_params=params(),
        name="ffn_weights",
        cost_estimate=cost([(tokens, width, blocks * width)] * 2),
    )(second_low, grad_hidden, active, grad_out)


def fold_call(kernel, name, spot, inputs, outs):
    return row_call(
        kernel, name, spot, (), [full(None)] * len(inputs), [full(None)] * len(outs),
        [jax.ShapeDtypeStruct(shape, kind) for shape, kind in outs], [], inputs, limit=12 * 2**20,
    )


def added(*parts):
    total = parts[0].astype(f32)
    for part in parts[1:]:
        total = total + part.astype(f32)
    return total


def fold_first_kernel(own, extra, spot, mine, got, keep_one, send_one, keep_two, send_two):
    high, side = spot[0], spot[3]
    half = own // 2
    slots = keep_one.shape[0] // half

    def take(place, low):
        rows = pl.ds(pl.multiple_of(place * own + low, 16), half)
        return added(mine[rows, :], got[rows, :]).astype(bf16)

    for slot in range(slots):
        rows = pl.ds(slot * half, half)
        keep_one[rows, :] = take(high * slots + slot, 0)
        send_one[rows, :] = take((1 - high) * slots + slot, 0)
        keep_two[rows, :] = take(2 * slot + side, half)
        send_two[rows, :] = take(2 * slot + 1 - side, half)
    if extra:
        vectors = added(mine[2 * slots * own :, :], got[2 * slots * own :, :]).astype(bf16)
        keep_one[slots * half :, :] = vectors
        send_one[slots * half :, :] = vectors


def fold_first(spot, mine, got, own):
    width = mine.shape[1]
    extra = mine.shape[0] - 2 * width
    rows = width // own * (own // 2)
    first, second = ((rows + extra, width), bf16), ((rows, width), bf16)
    return fold_call(
        functools.partial(fold_first_kernel, own, extra), "fold_first", spot, (mine, got),
        (first, first, second, second),
    )


def fold_second_kernel(
    half, extra, spot, keep_a, got_a, keep_b, got_b, keep_one, send_one, keep_two, send_two
):
    high, side = spot[0], spot[3]
    slots = keep_two.shape[0] // half

    def take(keep, got, place):
        rows = pl.ds(pl.multiple_of(place * half, 16), half)
        return added(keep[rows, :], got[rows, :]).astype(bf16)

    for slot in range(slots):
        rows = pl.ds(slot * half, half)
        keep_one[rows, :] = take(keep_a, got_a, 2 * slot + side)
        send_one[rows, :] = take(keep_a, got_a, 2 * slot + 1 - side)
        keep_two[rows, :] = take(keep_b, got_b, high * slots + slot)
        send_two[rows, :] = take(keep_b, got_b, (1 - high) * slots + slot)
    if extra:
        low = 2 * slots * half
        vectors = added(keep_a[low:, :], got_a[low:, :]).astype(bf16)
        keep_one[slots * half :, :] = vectors
        send_one[slots * half :, :] = vectors


def fold_second(spot, keep_a, got_a, keep_b, got_b, own):
    rows, width = keep_b.shape
    extra = keep_a.shape[0] - rows
    first, second = ((rows // 2 + extra, width), bf16), ((rows // 2, width), bf16)
    return fold_call(
        functools.partial(fold_second_kernel, own // 2, extra), "fold_second", spot,
        (keep_a, got_a, keep_b, got_b), (first, first, second, second),
    )


def fold_third_kernel(half, extra, spot, keep_a, got_a, keep_b, got_b, *parts):
    depth = spot[2]
    slots = keep_b.shape[0] // half
    for step, part in enumerate(parts):
        rows = pl.ds(pl.multiple_of((depth + step) % slots * half, 16), half)
        part[:half, :] = added(keep_a[rows, :], got_a[rows, :]).astype(bf16)
        part[half : 2 * half, :] = added(keep_b[rows, :], got_b[rows, :]).astype(bf16)
        if extra:
            low = slots * half
            part[2 * half :, :] = added(keep_a[low:, :], got_a[low:, :]).astype(bf16)


def fold_third(spot, keep_a, got_a, keep_b, got_b, own):
    rows, width = keep_b.shape
    extra = keep_a.shape[0] - rows
    part = ((own + extra, width), bf16)
    return fold_call(
        functools.partial(fold_third_kernel, own // 2, extra), "fold_third", spot,
        (keep_a, got_a, keep_b, got_b), (part,) * (rows // (own // 2)),
    )


def sources(spot, sent, got):
    high, core = spot[0], spot[1]
    rows = sent.shape[0] // 2
    return [
        (2 * y + c, ref, pl.ds(low, rows))
        for c, ref in ((core, sent), (1 - core, got))
        for y, low in ((high, 0), (1 - high, rows))
    ]


def finish_early_kernel(own, spot, sent, got, in_ref, out_ref, first_ref, rest_ref):
    width = sent.shape[1]
    for place, ref, rows in sources(spot, sent, got):
        low = rows.start
        in_ref[:, pl.ds(pl.multiple_of(place * width, width), width)] = ref[low : low + own, :].astype(f32)
        out_ref[pl.ds(pl.multiple_of(place * own, 8), own), :] = ref[low + own : low + 2 * own, :].astype(f32)
        unit = ref[low + 2 * own : low + 3 * own, :].astype(f32)

        @pl.when(place == 0)
        def _(unit=unit):
            first_ref[...] = unit

        @pl.when(place != 0)
        def _(unit=unit, place=place):
            rest_ref[place - 1] = unit


def finish_early(spot, sent, got, own):
    width = sent.shape[1]
    return fold_call(
        functools.partial(finish_early_kernel, own), "finish_early", spot, (sent, got),
        (((own, 4 * width), f32), ((4 * own, width), f32), ((own, width), f32), ((3, own, width), f32)),
    )


def finish_late_kernel(spot, sent, got, rest_ref, last_ref):
    for place, ref, rows in sources(spot, sent, got):
        unit = ref[rows, :].astype(f32)

        @pl.when(place == 3)
        def _(unit=unit):
            last_ref[...] = unit

        @pl.when(place != 3)
        def _(unit=unit, place=place):
            rest_ref[place] = unit


def finish_late(spot, sent, got):
    rows, width = sent.shape
    return fold_call(
        finish_late_kernel, "finish_late", spot, (sent, got),
        (((3, rows // 2, width), f32), ((rows // 2, width), f32)),
    )


def wide(array):
    return array.astype(f32)


def weight_grad(left, right):
    return dot_tn(left, right).astype(bf16)


def forward(
    target, memory, cotangent, info, pieces, head, mid, tail, vectors,
    mid_step=lambda *same: same, mid_last=lambda *same: same,
):
    queries, keys, values = project_self(info, target, head, vectors)
    queries, mid = mid_step(queries, mid)
    context_self, stats_self = self_attend(info, queries, keys, values)
    context_self, mid = mid_last(context_self, mid)
    total_first, first_low, query_cross = first_norm(info, target, context_self, mid, vectors)
    key_cross, value_cross = project_memory(info, memory, mid, vectors)
    context_cross, stats_cross = cross_attend(info, query_cross, key_cross, value_cross)
    output, second_low, active, du, df, do_cross, dz2, dc_cross, sums_ffn, sums_wide = ffn_block(
        info, total_first, context_cross, cotangent, head, tail, vectors
    )
    grad_ffn = ffn_weights(second_low, du, active, df, pieces)
    dq_cross, dk_cross, dv_cross = cross_attend_back(
        info, query_cross, key_cross, value_cross, dc_cross, context_cross, stats_cross
    )
    dz1, do_self, dc_self, sums_first = first_back(info, dz2, dq_cross, total_first, mid, vectors)
    grads = self_attend_back(info, queries, keys, values, dc_self, context_self, stats_self)
    memory, *grads = lax.optimization_barrier((memory, *grads))
    *grad_mid, sum_value = mid_weights(
        info, memory, dk_cross, dv_cross, (first_low, dq_cross, context_self, do_self)
    )
    cross = (context_cross, do_cross)
    sums = (sums_first, sum_value, sums_ffn, sums_wide)
    return output, grad_ffn, grad_mid, dz1, grads, dk_cross, dv_cross, cross, sums, mid


def forward_back(target, memory, cotangent, info, pieces, head, mid, tail, vectors):
    output, grad_ffn, grad_mid, dz1, grads, dk_cross, dv_cross, cross, sums, mid = forward(
        target, memory, cotangent, info, pieces, head, mid, tail, vectors
    )
    grad_self = self_weights(info, target, grads, cross, sums)
    target_grad = target_back(info, dz1, grads, head)
    memory_grad = memory_back(info, dk_cross, dv_cross, mid, 0, memory.shape[0])
    return (output, target_grad, memory_grad), grad_ffn, grad_mid, grad_self


def pair_swap(array, axis, bit):
    count = lax.axis_size(axis)
    return lax.ppermute(array, axis, [(place, place ^ bit) for place in range(count)])


def ring(array, axis, shift):
    count = lax.axis_size(axis)
    return lax.ppermute(array, axis, [(place, (place + shift) % count) for place in range(count)])


def pick(array, axis, index):
    return lax.dynamic_index_in_dim(array, index, axis, keepdims=False)


def places():
    dp, fsdp = lax.axis_index("dp"), lax.axis_index("fsdp")
    return dp // 2, dp % 2, fsdp // 2, fsdp % 2


def add_half(array, axis, mine, mesh_axis, bit):
    got = pair_swap(pick(array, axis, 1 - mine), mesh_axis, bit)
    return (wide(pick(array, axis, mine)) + wide(got)).astype(bf16)


def add_depth(array, depth):
    total = wide(pick(array, 0, depth))
    for step in (1, 2, 3):
        total = total + wide(ring(pick(array, 0, (depth + step) % 4), "fsdp", 2 * step))
    return total.astype(bf16)


def fence(*arrays):
    return lax.optimization_barrier(arrays)


def add(mine, got):
    return (wide(mine) + wide(got)).astype(bf16)


def cut(array):
    half = array.shape[-2] // 2 // 8 * 8
    return array[..., :half, :], array[..., half:, :]


def join_pair(array, axis, mine, mesh_axis, bit):
    return join(array, pair_swap(array, mesh_axis, bit), axis, mine)


def join(array, got, axis, mine):
    first = jnp.where(mine == 0, array, got)
    second = jnp.where(mine == 0, got, array)
    return jnp.stack([first, second], axis)


def share_dp(array):
    high, core, _, _ = places()
    both = join_pair(array, 0, high, "dp", 2)
    return join_pair(both, 1, core, "dp", 1).reshape((4,) + array.shape)


def join_depth(array, depth):
    parts = [array] + [ring(array, "fsdp", 2 * step) for step in (1, 2, 3)]
    out = jnp.zeros((4,) + array.shape, array.dtype)
    for step, part in enumerate(parts):
        out = lax.dynamic_update_index_in_dim(out, part, (depth - step) % 4, 0)
    return out


def lay_vectors(items, width):
    rows = [jnp.pad(item, ((0, 8 - item.shape[0]), (0, 0))) for item in items]
    row = jnp.concatenate(rows, 1)
    return jnp.pad(row, ((0, 0), (0, width - row.shape[1])))


def gather_vectors(rows, own):
    pieces, _, width = rows.shape
    groups = width // own
    rows = rows.reshape(pieces, 8, groups, own)
    hidden = rows[:, :4, 2].reshape(4, pieces * own)
    rows = jnp.transpose(rows, (2, 1, 0, 3)).reshape(groups * 8, pieces * own)
    return wide(jnp.concatenate([rows[:16], hidden, rows[20:]], 0))


def fast_layer(
    target, memory, cotangent, bucket, source_len, self_qkv, self_out, self_bias, cross_qkv,
    cross_out, cross_bias, ffn_in, ffn_in_bias, ffn_out, ffn_out_bias, norm_gain, norm_bias,
):
    dp = lax.axis_index("dp")
    high, core, depth, side = places()
    count, width = memory.shape[0], target.shape[1]
    own = self_out.shape[0]
    pieces = width // own
    info = jnp.concatenate([bucket, source_len, core[None]])
    vectors = lay_vectors(
        (self_bias, cross_bias, ffn_in_bias.reshape(4, own), ffn_out_bias[None], norm_gain, norm_bias), width
    )
    head = jnp.concatenate([pick(jnp.concatenate([self_qkv, cross_out[None]], 0), 0, dp), vectors], 0)
    mid = pick(jnp.concatenate([self_out[None], cross_qkv], 0), 0, dp)
    head, mid = fence(join_depth(head, depth), mid)
    one, two = cut(head)
    one, two = join_pair(one, 1, side, "fsdp", 1), join_pair(two, 1, high, "dp", 2)
    one, two, mid = fence(one, two, mid)
    one, two = join_pair(one, 2, high, "dp", 2), join_pair(two, 1, side, "fsdp", 1)
    half = own // 2
    mine = jnp.concatenate([one, two[:, :, :, :half]], 3).reshape(pieces, 2, own, width)
    mine, mid, ffn_in, ffn_out = fence(mine, join_depth(mid, depth), ffn_in, ffn_out)
    got = pair_swap(mine, "dp", 1)
    vectors = gather_vectors(two[:, :, 0, half:].reshape(pieces, 8, width), own)
    three, four = cut(mid)
    in_cols = pick(ffn_in.reshape(own, 4, width), 1, dp)
    out_rows = pick(ffn_out.reshape(4, own, width), 0, dp)
    tail = lax.all_gather(
        jnp.concatenate([in_cols, out_rows], 0), ("dp", "fsdp"), axis=0, tiled=True
    ).reshape(4, pieces, 2 * own, width)
    parts = (three, pair_swap(three, "fsdp", 1), four, pair_swap(four, "dp", 2))

    def mid_step(queries, parts):
        queries, three, got_three, four, got_four = fence(queries, *parts)
        three, four = join(three, got_three, 1, side), join(four, got_four, 1, high)
        return queries, (three, pair_swap(three, "dp", 2), four, pair_swap(four, "fsdp", 1))

    def mid_last(context, parts):
        context, three, got_three, four, got_four = fence(context, *parts)
        three, four = join(three, got_three, 2, high), join(four, got_four, 1, side)
        mine = jnp.concatenate([three, four], 3).reshape(pieces, 2, own, width)
        return context, (mine, pair_swap(mine, "dp", 1))

    head = (mine, got)
    output, grad_ffn, grad_mid, dz1, grads, dk_cross, dv_cross, cross, sums, mid = forward(
        target, memory, cotangent, info, pieces, head, parts, tail, vectors, mid_step, mid_last
    )
    sum_ffn = lax.psum_scatter(
        grad_ffn.reshape(-1, width), ("dp", "fsdp"), scatter_dimension=0, tiled=True
    )
    spot = jnp.stack([high, core, depth, side])
    mine, other, target_late = fence(*grad_mid, target)
    got = pair_swap(other, "dp", 1)
    own_part, other = self_weights(info, target_late, grads, cross, sums)
    got, own_part, other = fence(got, own_part, other)
    keep_one, send_one, keep_two, send_two = fold_first(spot, mine, got, own)
    send_one, send_two, other, dz1 = fence(send_one, send_two, other, dz1)
    got_one, got_two = pair_swap(send_one, "dp", 2), pair_swap(send_two, "fsdp", 1)
    got = pair_swap(other, "dp", 1)
    target_grad = target_back(info, dz1, grads, head)
    got_one, got_two, got, target_grad = fence(got_one, got_two, got, target_grad)
    keep_one, send_one, keep_two, send_two = fold_second(spot, keep_one, got_one, keep_two, got_two, own)
    keep_three, send_three, keep_four, send_four = fold_first(spot, own_part, got, own)
    send_one, send_two, send_three, send_four, dk_cross = fence(
        send_one, send_two, send_three, send_four, dk_cross
    )
    got_one, got_two = pair_swap(send_one, "fsdp", 1), pair_swap(send_two, "dp", 2)
    got_three, got_four = pair_swap(send_three, "dp", 2), pair_swap(send_four, "fsdp", 1)
    memory_grad = memory_back(info, dk_cross, dv_cross, mid, 0, count // 2)
    got_one, got_two, got_three, got_four, memory_grad = fence(
        got_one, got_two, got_three, got_four, memory_grad
    )
    sum_mid, *sends = fold_third(spot, keep_one, got_one, keep_two, got_two, own)
    keep_three, send_three, keep_four, send_four = fold_second(
        spot, keep_three, got_three, keep_four, got_four, own
    )
    *sends, send_three, send_four, dk_cross = fence(*sends, send_three, send_four, dk_cross)
    rings = [ring(item, "fsdp", 2 * step) for step, item in zip((1, 2, 3), sends)]
    got_three, got_four = pair_swap(send_three, "fsdp", 1), pair_swap(send_four, "dp", 2)
    memory_grad = memory_back(
        info, dk_cross, dv_cross, mid, count // 2, count - count // 2, start=(memory_grad,)
    )
    got_three, got_four, memory_grad, *rings = fence(got_three, got_four, memory_grad, *rings)
    sum_mid = added(sum_mid, *rings).astype(bf16)
    early = jnp.concatenate([sum_ffn, sum_mid], 0)
    sum_self, *sends = fold_third(spot, keep_three, got_three, keep_four, got_four, own)
    *sends, early = fence(*sends, early)
    rings = [ring(item, "fsdp", 2 * step) for step, item in zip((1, 2, 3), sends)]
    got = pair_swap(early, "dp", 2)
    got, *rings = fence(got, *rings)
    late = added(sum_self, *rings)
    vectors = late[-VECTORS:]
    late = late[:-VECTORS].astype(bf16)
    early = jnp.concatenate([early, got], 0)
    early, late = fence(early, late)
    got_early = pair_swap(early, "dp", 1)
    got = pair_swap(late, "dp", 2)
    late = jnp.concatenate([late, got], 0)
    late, got_early = fence(late, got_early)
    got = pair_swap(late, "dp", 1)
    grad_in, grad_out, grad_self_out, grad_cross_qkv = finish_early(spot, early, got_early, own)
    place = lax.axis_index("fsdp")
    hidden = pick(vectors[6:10].reshape(pieces, 4 * own), 0, place)
    vectors = lax.dynamic_slice_in_dim(vectors, place * own, own, 1)
    got, grad_in, hidden, vectors = fence(got, grad_in, hidden, vectors)
    grad_self_qkv, grad_cross_out = finish_late(spot, late, got)
    return (
        output, target_grad, memory_grad, grad_self_qkv, grad_self_out, vectors[:3], grad_cross_qkv,
        grad_cross_out, vectors[3:6], grad_in, hidden, grad_out, vectors[10], vectors[11:14], vectors[14:17],
    )


def plain_layer(
    target, memory, cotangent, bucket, source_len, self_qkv, self_out, self_bias, cross_qkv,
    cross_out, cross_bias, ffn_in, ffn_in_bias, ffn_out, ffn_out_bias, norm_gain, norm_bias,
):
    gather = lambda item, axis: lax.all_gather(item, "fsdp", axis=axis, tiled=True)
    info = jnp.concatenate([bucket, source_len, jnp.zeros_like(bucket)])
    width = target.shape[1]
    blocks = ffn_out.shape[0] * lax.axis_size("fsdp") // width
    split = lambda units: (units[None, 0::2], units[None, 1::2])
    head = split(jnp.concatenate([gather(self_qkv, 1), gather(cross_out, 0)[None]], 0))
    mid = split(jnp.concatenate([gather(self_out, 0)[None], gather(cross_qkv, 1)], 0))
    ffn_in_w = jnp.swapaxes(gather(ffn_in, 0).reshape(width, blocks, width), 0, 1)
    tail = jnp.concatenate([ffn_in_w, gather(ffn_out, 0).reshape(blocks, width, width)], 1)[:, None]
    vectors = (
        gather(self_bias, 1), gather(cross_bias, 1), gather(ffn_in_bias, 0).reshape(blocks, width),
        gather(ffn_out_bias, 0)[None], gather(norm_gain, 1), gather(norm_bias, 1),
    )
    vectors = wide(
        jnp.concatenate([jnp.pad(item, ((0, 8 - item.shape[0]), (0, 0))) for item in vectors], 0)
    )
    outs, grad_ffn, grad_mid, grad_self = forward_back(
        target, memory, cotangent, info, 1, head, mid, tail, vectors
    )

    def reduce(grad, axis):
        piece = lax.psum_scatter(wide(grad), "fsdp", scatter_dimension=axis, tiled=True)
        return lax.psum(piece, "dp")

    def units(mine, other):
        both = [item[: 2 * width].reshape(2, width, width) for item in (mine, other)]
        return jnp.stack(both, 1).reshape(4, width, width)

    grad_in = jnp.swapaxes(grad_ffn[:, 0, :width], 0, 1).reshape(width, blocks * width)
    grad_out = grad_ffn[:, 0, width:].reshape(blocks * width, width)
    vectors = grad_self[0][2 * width :]
    grad_self, grad_mid = units(*grad_self), units(*grad_mid)
    return outs + (
        reduce(grad_self[:3], 1),
        reduce(grad_mid[0], 0),
        reduce(vectors[:3], 1),
        reduce(grad_mid[1:], 1),
        reduce(grad_self[3], 0),
        reduce(vectors[3:6], 1),
        reduce(grad_in, 0),
        reduce(vectors[6 : 6 + blocks].reshape(-1), 0),
        reduce(grad_out, 0),
        reduce(vectors[10], 0),
        reduce(vectors[11:14], 1),
        reduce(vectors[14:17], 1),
    )


def solution(mesh):
    rows = P(("dp", "fsdp"))
    first = P("fsdp")
    second = P(None, "fsdp")
    weights = (second, first, second, second, first, second, first, first, first, first, second, second)
    layer = fast_layer if (mesh.shape["dp"], mesh.shape["fsdp"]) == (4, 8) else plain_layer
    return jax.shard_map(
        layer,
        mesh=mesh,
        in_specs=(rows,) * 5 + weights,
        out_specs=(rows,) * 3 + weights,
        check_vma=False,
    )
```

```python
import functools
import math
import jax
import jax.numpy as jnp
from jax import lax
from jax.sharding import PartitionSpec as P
from jax.experimental import pallas as pl
from jax.experimental.pallas import tpu as pltpu

HEAD = 64
PAIR = 2 * HEAD
BLOCK = 256
very_low = -1e30
VMEM_LIMIT = 60 * 2**20
f32 = jnp.float32
bf16 = jnp.bfloat16


def dot_nt(left, right):
    return lax.dot_general(left, right, (((1,), (1,)), ((), ())), preferred_element_type=f32)


def dot_nn(left, right):
    return lax.dot_general(left, right, (((1,), (0,)), ((), ())), preferred_element_type=f32)


def dot_tn(left, right):
    return lax.dot_general(left, right, (((0,), (0,)), ((), ())), preferred_element_type=f32)


def split_pair(pair):
    lane = lax.broadcasted_iota(jnp.int32, pair.shape, 1)
    none = jnp.zeros_like(pair)
    return (jnp.where(lane < HEAD, pair, none), jnp.where(lane < HEAD, none, pair))


def mask_tail(scores, valid):
    low = scores.shape[0] - valid.shape[0]
    if low == 0:
        return jnp.where(valid, scores, very_low)
    return jnp.concatenate([scores[:low], jnp.where(valid, scores[low:], very_low)], 0)


def stacked(pair):
    return jnp.concatenate(split_pair(pair), 0)


def score_tile(queries, keys, valid):
    return mask_tail(dot_nt(keys, stacked(queries)), valid)


def attend_tile(scores, values):
    count = scores.shape[1] // 2
    values_t = values.T
    highest = jnp.max(scores, 0, keepdims=True)
    raised = jnp.exp(scores - highest)
    summed = jnp.sum(raised, 0, keepdims=True)
    raised = raised.astype(bf16)
    context = jnp.concatenate(
        [
            dot_nn(values_t[half * HEAD : (half + 1) * HEAD], raised[:, half * count : (half + 1) * count])
            / summed[:, half * count : (half + 1) * count]
            for half in range(2)
        ],
        0,
    )
    return context.T.astype(bf16), highest + jnp.log(summed)


def head_sums(pair):
    turned = pair.T
    return jnp.concatenate(
        [jnp.sum(turned[half * HEAD : (half + 1) * HEAD], 0, keepdims=True) for half in range(2)], 1
    )


def back_tile(scores, queries, keys, values, grads, contexts, logsum):
    count = scores.shape[1] // 2
    grad_rows = stacked(grads)
    grad_shares = dot_nt(values, grad_rows)
    inner = head_sums(grads.astype(f32) * contexts.astype(f32))
    keys_t = keys.T
    shares = jnp.exp(scores - logsum)
    grad_scores = (shares * (grad_shares - inner)).astype(bf16)
    grad_values = dot_nn(shares.astype(bf16), grad_rows)
    grad_keys = dot_nn(grad_scores, stacked(queries))
    grad_queries = jnp.concatenate(
        [
            dot_nn(keys_t[half * HEAD : (half + 1) * HEAD], grad_scores[:, half * count : (half + 1) * count])
            for half in range(2)
        ],
        0,
    ).T
    grad_queries = (grad_queries.astype(bf16).astype(f32) * HEAD**-0.5).astype(bf16)
    return grad_queries, grad_keys, grad_values


def causal(columns):
    key = lax.broadcasted_iota(jnp.int32, (BLOCK, columns), 0)
    query = lax.broadcasted_iota(jnp.int32, (BLOCK, columns), 1) % BLOCK
    return key <= query


def key_spans(tokens, whole):
    return [
        (0 if whole else low, low, low + BLOCK) for low in range(0, tokens, BLOCK)
    ]


def self_kernel(skip, info, q_ref, k_ref, v_ref, o_ref, stat_ref):
    tokens = q_ref.shape[0]
    valid = causal(2 * BLOCK)

    def run(whole):
        spans = key_spans(tokens, whole)
        score = lambda span: score_tile(q_ref[span[1] : span[2], :], k_ref[span[0] : span[2], :], valid)
        ahead = score(spans[0])
        for part, (low, start, stop) in enumerate(spans):
            scores = ahead
            if part + 1 < len(spans):
                ahead = score(spans[part + 1])
            o_ref[start:stop, :], stat_ref[0, part] = attend_tile(scores, v_ref[low:stop, :])

    pl.when(info[0] == 1)(functools.partial(run, False))
    pl.when(info[0] != 1)(functools.partial(run, True))


def self_back_kernel(skip, info, q_ref, k_ref, v_ref, g_ref, o_ref, stat_ref, *refs):
    dq_ref, dk_ref, dv_ref, key_sum, value_sum = refs[skip:]
    tokens = q_ref.shape[0]
    valid = causal(2 * BLOCK)

    def run(whole):
        spans = key_spans(tokens, whole)[::-1]
        score = lambda span: score_tile(q_ref[span[1] : span[2], :], k_ref[span[0] : span[2], :], valid)
        ahead = score(spans[0])
        for step, (low, start, stop) in enumerate(spans):
            scores = ahead
            if step + 1 < len(spans):
                ahead = score(spans[step + 1])
            dq_ref[start:stop, :], grad_keys, grad_values = back_tile(
                scores,
                q_ref[start:stop, :],
                k_ref[low:stop, :],
                v_ref[low:stop, :],
                g_ref[start:stop, :],
                o_ref[start:stop, :],
                stat_ref[0, start // BLOCK],
            )
            if not whole:
                dk_ref[start:stop, :] = grad_keys.astype(bf16)
                dv_ref[start:stop, :] = grad_values.astype(bf16)
            elif stop == tokens:
                key_sum[...] = grad_keys
                value_sum[...] = grad_values
            else:
                key_sum[:stop, :] += grad_keys
                value_sum[:stop, :] += grad_values
        if whole:
            dk_ref[...] = key_sum[...].astype(bf16)
            dv_ref[...] = value_sum[...].astype(bf16)

    pl.when(info[0] == 1)(functools.partial(run, False))
    pl.when(info[0] != 1)(functools.partial(run, True))


def by_length(info, row, mem_len, run):
    length = info[1 + row]
    for width in range(BLOCK, mem_len + 1, BLOCK):

        @pl.when((length > width - BLOCK) & (length <= width))
        def _(width=width):
            run(width, lambda columns: lax.broadcasted_iota(jnp.int32, (BLOCK, columns), 0) < length - (width - BLOCK))


def cross_kernel(skip, info, q_ref, k_ref, v_ref, o_ref, stat_ref):
    tokens = q_ref.shape[0]
    count, mem_len, _ = k_ref.shape
    parts = tokens // BLOCK

    half = mem_len // 2

    @pl.when(info[0] == 1)
    def _():
        def step(pair, none):
            lengths = [info[1 + 2 * pair], info[2 + 2 * pair]]

            def run(*widths):
                tiles = []
                for place, width in enumerate(widths):
                    row = 2 * pair + place
                    rows = pl.ds(pl.multiple_of(row * BLOCK, BLOCK), BLOCK)
                    key = lax.broadcasted_iota(jnp.int32, (half, 2 * BLOCK), 0) + (width - half)
                    scores = score_tile(q_ref[rows, :], k_ref[row, :width, :], key < lengths[place])
                    tiles.append((row, rows, width, scores))
                for row, rows, width, scores in tiles:
                    o_ref[rows, :], stat_ref[0, row] = attend_tile(scores, v_ref[row, :width, :])

            for one in (False, True):
                for two in (False, True):
                    chosen = ((lengths[0] > half) == one) & ((lengths[1] > half) == two)
                    pl.when(chosen)(functools.partial(run, half << one, half << two))
            return none

        lax.fori_loop(0, count // 2, step, None)

    @pl.when(info[0] != 1)
    def _():
        def run(width, valid):
            scores = score_tile(q_ref[...], k_ref[0, :width, :], valid(2 * tokens))
            o_ref[...], stats = attend_tile(scores, v_ref[0, :width, :])
            for part in range(parts):
                low = part * BLOCK
                stat_ref[0, part] = jnp.concatenate(
                    [stats[:, low : low + BLOCK], stats[:, tokens + low : tokens + low + BLOCK]], 1
                )

        by_length(info, 0, mem_len, run)


def cross_back_kernel(skip, info, q_ref, k_ref, v_ref, g_ref, o_ref, stat_ref, *refs):
    dq_ref, dk_ref, dv_ref = refs[skip:]
    tokens = q_ref.shape[0]
    count, mem_len, _ = k_ref.shape
    parts = tokens // BLOCK

    def store(row, width, grad_keys, grad_values):
        dk_ref[row, :width, :] = grad_keys.astype(bf16)
        dv_ref[row, :width, :] = grad_values.astype(bf16)
        if width < mem_len:
            rest = jnp.zeros((mem_len - width, PAIR), bf16)
            dk_ref[row, width:, :] = rest
            dv_ref[row, width:, :] = rest

    @pl.when(info[0] == 1)
    def _():
        def step(row, none):
            rows = pl.ds(pl.multiple_of(row * BLOCK, BLOCK), BLOCK)

            def run(width, valid):
                keys = k_ref[row, :width, :]
                scores = score_tile(q_ref[rows, :], keys, valid(2 * BLOCK))
                dq_ref[rows, :], grad_keys, grad_values = back_tile(
                    scores, q_ref[rows, :], keys, v_ref[row, :width, :], g_ref[rows, :], o_ref[rows, :],
                    stat_ref[0, row],
                )
                store(row, width, grad_keys, grad_values)

            by_length(info, row, mem_len, run)
            return none

        lax.fori_loop(0, count, step, None)

    @pl.when(info[0] != 1)
    def _():
        def run(width, valid):
            keys = k_ref[0, :width, :]
            scores = score_tile(q_ref[...], keys, valid(2 * tokens))
            stats = jnp.concatenate(
                [stat_ref[0, part][:, half * BLOCK : (half + 1) * BLOCK] for half in range(2) for part in range(parts)],
                1,
            )
            dq_ref[...], grad_keys, grad_values = back_tile(
                scores, q_ref[...], keys, v_ref[0, :width, :], g_ref[...], o_ref[...], stats
            )
            store(0, width, grad_keys, grad_values)

        by_length(info, 0, mem_len, run)


def params():
    return pltpu.CompilerParams(vmem_limit_bytes=VMEM_LIMIT)


def cost(matmuls, moved=2**23):
    flops = 2 * sum(math.prod(sizes) for sizes in matmuls)
    return pl.CostEstimate(flops=flops, bytes_accessed=moved, transcendentals=0)


def attend_call(kernel, name, info, queries, keys, values, rest=None, first=0, count=None, start=()):
    tokens, width = queries.shape
    pairs = width // PAIR
    count = count or pairs
    parts = tokens // BLOCK
    back = rest is not None
    own = pl.BlockSpec((tokens, PAIR), lambda pair, info: (0, pair + first))
    stat = pl.BlockSpec((1, parts, 1, 2 * BLOCK), lambda pair, info: (pair + first, 0, 0, 0))
    if keys.ndim == 2:
        other = own
        scratch = [pltpu.VMEM((tokens, PAIR), f32)] * 2 if back else []
    else:
        other = pl.BlockSpec(keys.shape[:2] + (PAIR,), lambda pair, info: (0, 0, pair + first))
        scratch = []
    queries_shape = jax.ShapeDtypeStruct((tokens, width), bf16)
    keys_shape = jax.ShapeDtypeStruct(keys.shape, bf16)
    stat_shape = jax.ShapeDtypeStruct((pairs, parts, 1, 2 * BLOCK), f32)
    inputs = (queries, keys, values) + (rest or ())
    return pl.pallas_call(
        functools.partial(kernel, len(start)),
        grid_spec=pltpu.PrefetchScalarGridSpec(
            num_scalar_prefetch=1,
            grid=(count,),
            in_specs=[own, other, other]
            + ([own, own, stat] if back else [])
            + [pl.BlockSpec(memory_space=pl.ANY)] * len(start),
            out_specs=[own, other, other] if back else [own, stat],
            scratch_shapes=scratch,
        ),
        out_shape=[queries_shape, keys_shape, keys_shape] if back else [queries_shape, stat_shape],
        input_output_aliases={1 + len(inputs) + place: place for place in range(len(start))},
        compiler_params=params(),
        name=name,
        cost_estimate=cost([(tokens, tokens, width)] * (24 if back else 12)),
    )(info, *inputs, *start)


def self_attend(info, queries, keys, values):
    return attend_call(self_kernel, "self_attend", info, queries, keys, values)


def cross_attend(info, queries, keys, values):
    return attend_call(cross_kernel, "cross_attend", info, queries, keys, values)


def self_attend_back(info, queries, keys, values, *rest, **span):
    return attend_call(self_back_kernel, "self_attend_back", info, queries, keys, values, rest, **span)


def cross_attend_back(info, queries, keys, values, *rest, **span):
    return attend_call(cross_back_kernel, "cross_attend_back", info, queries, keys, values, rest, **span)


epsilon = 1e-05
VECTORS = 32
LANES = 128


def normalise(total):
    middle = jnp.mean(total, -1, keepdims=True)
    centred = total - middle
    variance = jnp.mean(centred * centred, -1, keepdims=True)
    scale = lax.rsqrt(variance + epsilon)
    return centred * scale, scale


def normalise_back(grad, gain, normal, scale):
    scaled = grad * gain
    first = jnp.mean(scaled, -1, keepdims=True)
    second = jnp.mean(scaled * normal, -1, keepdims=True)
    return (scaled - first - normal * second) * scale


def add_rows(ref, row, value):
    ref[row : row + 1, :] += jnp.sum(value, 0, keepdims=True)


def start_sums(*refs):
    @pl.when(pl.program_id(0) == 0)
    def _():
        for ref in refs:
            ref[...] = jnp.zeros_like(ref)


def full(array):
    return pl.BlockSpec(memory_space=pltpu.VMEM)


def row_block(rows, width):
    return pl.BlockSpec((rows, width), lambda part, *info: (part, 0))


def keep_block(rows, width):
    return pl.BlockSpec((rows, width), lambda part, *info: (0, 0))


def unit(ref, high=0):
    return ref[:, high].reshape(ref.shape[0] * ref.shape[2], ref.shape[3])


def by_core(info, mine, got, run):
    core = info[info.shape[0] - 1]
    pl.when(core == 0)(lambda: run(mine, got))
    pl.when(core != 0)(lambda: run(got, mine))


def unit_block(array, high):
    return pl.BlockSpec(
        array.shape[:1] + (1,) + array.shape[2:],
        lambda *place: (0, high, 0, 0),
        pipeline_mode=pl.Buffered(1),
    )


def first_kernel(info, x_ref, c_ref, mine, got, vec_ref, z_ref, low_ref, q_ref):
    def run(even, odd):
        total = x_ref[...].astype(f32) + dot_nn(c_ref[...], unit(even)) + vec_ref[2 : 3, :]
        normal, _ = normalise(total)
        first_low = (normal * vec_ref[32 : 33, :] + vec_ref[40 : 41, :]).astype(bf16)
        z_ref[...] = total
        low_ref[...] = first_low
        q_ref[...] = ((dot_nn(first_low, unit(odd)) + vec_ref[8 : 9, :]) * HEAD**-0.5).astype(bf16)

    by_core(info, mine, got, run)


def row_call(
    kernel, name, info, grid, in_specs, out_specs, out_shape, matmuls, inputs, scratch=(), aliases=None, limit=VMEM_LIMIT
):
    return pl.pallas_call(
        kernel,
        grid_spec=pltpu.PrefetchScalarGridSpec(
            num_scalar_prefetch=1,
            grid=grid,
            in_specs=in_specs,
            out_specs=out_specs,
            scratch_shapes=scratch,
        ),
        out_shape=out_shape,
        input_output_aliases=aliases or {},
        compiler_params=pltpu.CompilerParams(vmem_limit_bytes=limit),
        name=name,
        cost_estimate=cost(matmuls),
    )(info, *inputs)


def first_norm(info, x, context, mid, vectors, rows=512):
    tokens, width = x.shape
    block = row_block(rows, width)
    low = jax.ShapeDtypeStruct((tokens, width), bf16)
    return row_call(
        first_kernel, "first_norm", info, (tokens // rows,),
        [block, block, unit_block(mid[0], 0), unit_block(mid[1], 0), full(vectors)],
        [block] * 3, [jax.ShapeDtypeStruct((tokens, width), f32), low, low],
        [(tokens, width, width)] * 4, (x, context, *mid, vectors),
    )


def chunks(blocks, pieces, block):
    return [divmod(number, blocks) for number in range(block * pieces, (block + 1) * pieces)]


def ffn_kernel(
    info,
    z_ref,
    c_ref,
    cot_ref,
    mine,
    got,
    tail_ref,
    vec_ref,
    out_ref,
    low_ref,
    act_ref,
    du_ref,
    df_ref,
    do_ref,
    dz_ref,
    dc_ref,
    sum_ref,
    wide_ref,
    slope_ref,
    out_w,
):
    start_sums(sum_ref, wide_ref)

    @pl.when(pl.program_id(0) == 0)
    def _():
        def load(even, odd):
            out_w[...] = unit(odd)

        by_core(info, mine, got, load)

    width = z_ref.shape[1]
    blocks, pieces, both = tail_ref.shape[:3]
    in_w = lambda block: tail_ref[block, :, : both // 2].reshape(width, width)
    ffn_w = lambda block: jnp.concatenate(
        [tail_ref[d, f, both // 2 :, :] for f, d in chunks(blocks, pieces, block)], 0
    )
    gain_first, gain_mid, gain_last = [vec_ref[row : row + 1, :] for row in (32, 33, 34)]
    shift_first, shift_mid, shift_last = [vec_ref[row : row + 1, :] for row in (40, 41, 42)]
    normal_first, _ = normalise(z_ref[...])
    first = normal_first * gain_first + shift_first
    normal_mid, scale_mid = normalise(first + dot_nn(c_ref[...], out_w[...]) + vec_ref[10 : 11, :])
    second = normal_mid * gain_mid + shift_mid
    second_low = second.astype(bf16)
    low_ref[...] = second_low
    total = second + vec_ref[24 : 25, :]
    ahead = dot_nn(second_low, in_w(0))
    for block in range(blocks):
        cols = pl.ds(block * width, width)
        value = ahead + vec_ref[16 + block : 17 + block, :]
        if block + 1 < blocks:
            ahead = dot_nn(second_low, in_w(block + 1))
        share = 0.5 * (1.0 + lax.erf(value * 0.5**0.5))
        density = jnp.exp(-0.5 * value * value) * 0.3989422804014327
        active = (value * share).astype(bf16)
        slope_ref[:, cols] = share + value * density
        act_ref[:, cols] = active
        total = total + dot_nn(active, ffn_w(block))
    normal_last, scale_last = normalise(total)
    out_ref[...] = (normal_last * gain_last + shift_last).astype(bf16)
    cot = cot_ref[...].astype(f32)
    add_rows(sum_ref, 0, cot * normal_last)
    add_rows(sum_ref, 1, cot)
    grad_last = normalise_back(cot, gain_last, normal_last, scale_last)
    grad_low = grad_last.astype(bf16)
    df_ref[...] = grad_low
    add_rows(sum_ref, 2, grad_low.astype(f32))
    grad_second = grad_last
    ahead = dot_nt(grad_low, ffn_w(0))
    for block in range(blocks):
        cols = pl.ds(block * width, width)
        grad_hidden = (ahead * slope_ref[:, cols]).astype(bf16)
        if block + 1 < blocks:
            ahead = dot_nt(grad_low, ffn_w(block + 1))
        du_ref[:, cols] = grad_hidden
        wide_ref[:, cols] += jnp.sum(grad_hidden.astype(f32), 0, keepdims=True)
        grad_second = grad_second + dot_nt(grad_hidden, in_w(block))
    add_rows(sum_ref, 3, grad_second * normal_mid)
    add_rows(sum_ref, 4, grad_second)
    grad_mid = normalise_back(grad_second, gain_mid, normal_mid, scale_mid)
    dz_ref[...] = grad_mid
    grad_low = grad_mid.astype(bf16)
    do_ref[...] = grad_low
    add_rows(sum_ref, 5, grad_low.astype(f32))
    dc_ref[...] = dot_nt(grad_low, out_w[...]).astype(bf16)


def ffn_block(info, z, context, cotangent, head, tail, vectors, rows=256):
    tokens, width = z.shape
    hidden = tail.shape[0] * width
    block = row_block(rows, width)
    wide = row_block(rows, hidden)
    narrow_shape = jax.ShapeDtypeStruct((tokens, width), bf16)
    wide_shape = jax.ShapeDtypeStruct((tokens, hidden), bf16)
    return row_call(
        ffn_kernel, "ffn_block", info, (tokens // rows,),
        [block] * 3 + [unit_block(head[0], 1), unit_block(head[1], 1), full(tail), full(vectors)],
        [block, block, wide, wide, block, block, block, block, keep_block(8, width), keep_block(1, hidden)],
        [
            narrow_shape, narrow_shape, wide_shape, wide_shape, narrow_shape, narrow_shape,
            jax.ShapeDtypeStruct((tokens, width), f32), narrow_shape,
            jax.ShapeDtypeStruct((8, width), f32), jax.ShapeDtypeStruct((1, hidden), f32),
        ],
        [(tokens, width, hidden)] * 8, (z, context, cotangent, *head, tail, vectors),
        [pltpu.VMEM((rows, hidden), f32), pltpu.VMEM((width, width), bf16)],
    )


def first_back_kernel(info, dz2_ref, dq_ref, z_ref, mine, got, vec_ref, dz_ref, do_ref, dc_ref, sum_ref):
    start_sums(sum_ref)

    def run(even, odd):
        grad_query = dq_ref[...]
        grad_first = dz2_ref[...] + dot_nt(grad_query, unit(odd))
        normal, scale = normalise(z_ref[...])
        add_rows(sum_ref, 0, grad_first * normal)
        add_rows(sum_ref, 1, grad_first)
        grad_start = normalise_back(grad_first, vec_ref[32 : 33, :], normal, scale)
        dz_ref[...] = grad_start
        grad_low = grad_start.astype(bf16)
        do_ref[...] = grad_low
        add_rows(sum_ref, 2, grad_low.astype(f32))
        add_rows(sum_ref, 3, grad_query.astype(f32))
        dc_ref[...] = dot_nt(grad_low, unit(even)).astype(bf16)

    by_core(info, mine, got, run)


def first_back(info, dz2, grad_query, z, mid, vectors, rows=512):
    tokens, width = z.shape
    block = row_block(rows, width)
    low = jax.ShapeDtypeStruct((tokens, width), bf16)
    return row_call(
        first_back_kernel, "first_back", info, (tokens // rows,),
        [block] * 3 + [unit_block(mid[0], 0), unit_block(mid[1], 0), full(vectors)],
        [block] * 3 + [keep_block(8, width)],
        [jax.ShapeDtypeStruct((tokens, width), f32), low, low, jax.ShapeDtypeStruct((8, width), f32)],
        [(tokens, width, width)] * 4, (dz2, grad_query, z, *mid, vectors),
    )


def needed(info, row, part, rows):
    return ((info[0] == 1) | (row == 0)) & (part * rows < info[1 + row])


def needed_place(info, row, part, rows):
    used = jnp.where(info[0] == 1, row, 0)
    last = (info[1 + used] + rows - 1) // rows - 1
    return used, jnp.where(info[0] == 1, jnp.minimum(part, last), jnp.where(row == 0, jnp.minimum(part, last), last))


def project_kernel(rows, info, m_ref, mine, got, b_ref, k_ref, v_ref):
    @pl.when(needed(info, pl.program_id(0), pl.program_id(1), rows))
    def _():
        def run(even, odd):
            memory = m_ref[0]
            k_ref[0] = dot_nn(memory, unit(even)).astype(bf16)
            v_ref[0] = (dot_nn(memory, unit(odd)) + b_ref[9 : 10, :]).astype(bf16)

        by_core(info, mine, got, run)


def memory_block(rows, width, first=0):
    return pl.BlockSpec(
        (1, rows, width), lambda row, part, info: needed_place(info, row + first, part, rows) + (0,)
    )


def project_memory(info, memory, mid, vectors, rows=512):
    count, length, width = memory.shape
    block = memory_block(rows, width)
    return row_call(
        functools.partial(project_kernel, rows), "project_memory", info, (count, length // rows),
        [block, unit_block(mid[0], 1), unit_block(mid[1], 1), full(vectors)], [block] * 2,
        [jax.ShapeDtypeStruct(memory.shape, bf16)] * 2,
        [(count, length, width, width)] * 2, (memory, *mid, vectors),
    )


def memory_back_kernel(rows, first, info, dk_ref, dv_ref, mine, got, *refs):
    out_ref = refs[-1]
    here = needed(info, pl.program_id(0) + first, pl.program_id(1), rows)

    @pl.when(here)
    def _():
        def run(even, odd):
            out_ref[0] = dot_nt(dk_ref[0], unit(even)) + dot_nt(dv_ref[0], unit(odd))

        by_core(info, mine, got, run)

    @pl.when(jnp.logical_not(here))
    def _():
        out_ref[...] = jnp.zeros_like(out_ref)


def memory_back(info, grad_keys, grad_values, mid, first, count, start=(), rows=1024):
    length, width = grad_keys.shape[1:]
    block = memory_block(rows, width, first)
    return row_call(
        functools.partial(memory_back_kernel, rows, first), "memory_back", info, (count, length // rows),
        [block, block, unit_block(mid[0], 1), unit_block(mid[1], 1)]
        + [pl.BlockSpec(memory_space=pl.ANY)] * len(start),
        pl.BlockSpec((1, rows, width), lambda row, part, info: (row + first, part, 0)),
        jax.ShapeDtypeStruct(grad_keys.shape, f32),
        [(count, length, width, width)] * 2, (grad_keys, grad_values, *mid, *start),
        aliases={5: 0} if start else {},
    )


def unit_copy(info, stage, sent, mine, other, number, act):
    width = stage.shape[1]
    here = info[info.shape[0] - 1] == number % 2
    for ref, chosen in ((mine, here), (other, jnp.logical_not(here))):

        @pl.when(chosen)
        def _(ref=ref):
            rows = ref.at[pl.ds(number // 2 * width, width), :]
            act(pltpu.make_async_copy(stage.at[number], rows, sent.at[number]))


def put_unit(info, stage, sent, mine, other, number, value):
    stage[number] = value.astype(bf16)
    unit_copy(info, stage, sent, mine, other, number, lambda copy: copy.start())


def end_units(info, stage, sent, mine, other):
    for number in range(4):
        unit_copy(info, stage, sent, mine, other, number, lambda copy: copy.wait())


def unit_scratch(width):
    return [pltpu.VMEM((4, width, width), bf16), pltpu.SemaphoreType.DMA((4,))]


def mid_weights_kernel(
    rows, info, m_ref, dk_ref, dv_ref, first_hbm, dq_hbm, self_hbm, dself_hbm,
    mine, other, sum_ref, key_sum, value_sum, stage, sent, held, arrived,
):
    row, part = pl.program_id(0), pl.program_id(1)
    out = (info, stage, sent, mine, other)
    fetches = [
        pltpu.make_async_copy(source, held.at[place], arrived.at[place])
        for place, source in enumerate((self_hbm, dself_hbm, first_hbm, dq_hbm))
    ]

    @pl.when((row == 0) & (part == 0))
    def _():
        for fetch in fetches:
            fetch.start()
        key_sum[...] = jnp.zeros_like(key_sum)
        value_sum[...] = jnp.zeros_like(value_sum)
        sum_ref[...] = jnp.zeros_like(sum_ref)

    @pl.when(needed(info, row, part, rows))
    def _():
        memory = m_ref[0]
        key_sum[...] += dot_tn(memory, dk_ref[0])
        value_sum[...] += dot_tn(memory, dv_ref[0])
        sum_ref[...] += jnp.sum(dv_ref[0].astype(f32), 0, keepdims=True)

    @pl.when((row == pl.num_programs(0) - 1) & (part == pl.num_programs(1) - 1))
    def _():
        put_unit(*out, 2, key_sum[...])
        put_unit(*out, 3, value_sum[...])
        for fetch in fetches:
            fetch.wait()
        put_unit(*out, 0, dot_tn(held[0], held[1]))
        put_unit(*out, 1, dot_tn(held[2], held[3]))
        end_units(*out)


def mid_weights(info, memory, grad_keys, grad_values, pairs):
    count, rows, width = memory.shape
    block = memory_block(rows, width)
    half = jax.ShapeDtypeStruct((2 * width, width), bf16)
    return row_call(
        functools.partial(mid_weights_kernel, rows), "mid_weights", info, (count, 1),
        [block] * 3 + [pl.BlockSpec(memory_space=pl.ANY)] * 4,
        [pl.BlockSpec(memory_space=pl.ANY)] * 2 + [pl.BlockSpec((1, width), lambda row, part, info: (0, 0))],
        [half, half, jax.ShapeDtypeStruct((1, width), f32)],
        [(count, rows, width, width)] * 2, (memory, grad_keys, grad_values, *pairs),
        [pltpu.VMEM((width, width), f32)] * 2
        + unit_scratch(width)
        + [pltpu.VMEM((4,) + pairs[0].shape, bf16), pltpu.SemaphoreType.DMA((4,))],
    )


def qkv_kernel(info, x_ref, mine, got, vec_ref, q_ref, k_ref, v_ref):
    def run(even, odd):
        x = x_ref[...]
        q_ref[...] = ((dot_nn(x, unit(even, 0)) + vec_ref[0 : 1, :]) * HEAD**-0.5).astype(bf16)
        k_ref[...] = dot_nn(x, unit(odd, 0)).astype(bf16)
        v_ref[...] = (dot_nn(x, unit(even, 1)) + vec_ref[1 : 2, :]).astype(bf16)

    by_core(info, mine, got, run)


def project_self(info, x, head, vectors, rows=512):
    tokens, width = x.shape
    block = row_block(rows, width)
    return row_call(
        qkv_kernel, "project_self", info, (tokens // rows,),
        [block, full(None), full(None), full(None)], [block] * 3,
        [jax.ShapeDtypeStruct((tokens, width), bf16)] * 3,
        [(tokens, width, width)] * 4, (x, *head, vectors),
    )


def target_back_kernel(info, z_ref, q_ref, k_ref, v_ref, mine, got, out_ref):
    def run(even, odd):
        out_ref[...] = (
            z_ref[...]
            + dot_nt(q_ref[...], unit(even, 0))
            + dot_nt(k_ref[...], unit(odd, 0))
            + dot_nt(v_ref[...], unit(even, 1))
        )

    by_core(info, mine, got, run)


def target_back(info, dz, grads, head, rows=512):
    tokens, width = dz.shape
    block = row_block(rows, width)
    return row_call(
        target_back_kernel, "target_back", info, (tokens // rows,),
        [block] * 4 + [full(None)] * 2, block, jax.ShapeDtypeStruct((tokens, width), f32),
        [(tokens, width, width)] * 4, (dz, *grads, *head),
    )


def self_weights_kernel(
    info, x_hbm, q_hbm, k_hbm, v_hbm, cross_hbm, dcross_hbm, first_ref, value_ref, ffn_ref, wide_ref,
    mine, other, held, arrived, stage, sent, vectors, vectors_sent,
):
    sources = (cross_hbm, dcross_hbm, x_hbm, q_hbm, k_hbm, v_hbm)
    copies = [
        pltpu.make_async_copy(source, held.at[place], arrived.at[place])
        for place, source in enumerate(sources)
    ]
    for copy in copies:
        copy.start()
    width = x_hbm.shape[1]
    out = (info, stage, sent, mine, other)
    copies[0].wait()
    copies[1].wait()
    put_unit(*out, 3, dot_tn(held[0], held[1]))
    copies[2].wait()
    sums = []
    for number in range(3):
        copies[3 + number].wait()
        put_unit(*out, number, dot_tn(held[2], held[3 + number]))
        sums.append(jnp.sum(held[3 + number].astype(f32), 0, keepdims=True))
    row = lambda ref, number: ref[number : number + 1, :]
    vectors[...] = jnp.concatenate(
        [sums[0], sums[2], row(first_ref, 2), row(first_ref, 3), value_ref[...], row(ffn_ref, 5)]
        + [wide_ref[:, low : low + width] for low in range(0, wide_ref.shape[1], width)]
        + [
            row(ffn_ref, 2), row(first_ref, 0), row(ffn_ref, 3), row(ffn_ref, 0), row(first_ref, 1),
            row(ffn_ref, 4), row(ffn_ref, 1), jnp.zeros((VECTORS - 17, width), f32),
        ],
        0,
    ).astype(bf16)
    ends = [
        pltpu.make_async_copy(vectors, ref.at[pl.ds(2 * width, VECTORS), :], vectors_sent.at[place])
        for place, ref in enumerate((mine, other))
    ]
    for copy in ends:
        copy.start()
    end_units(*out)
    for copy in ends:
        copy.wait()


def self_weights(info, x, grads, cross, sums):
    tokens, width = x.shape
    half = jax.ShapeDtypeStruct((2 * width + VECTORS, width), bf16)
    return row_call(
        self_weights_kernel, "self_weights", info, (),
        [pl.BlockSpec(memory_space=pl.ANY)] * 6 + [full(None)] * 4, [pl.BlockSpec(memory_space=pl.ANY)] * 2,
        [half, half],
        [(tokens, width, width)] * 4, (x, *grads, *cross, *sums),
        [pltpu.VMEM((6, tokens, width), bf16), pltpu.SemaphoreType.DMA((6,))]
        + unit_scratch(width)
        + [pltpu.VMEM((VECTORS, width), bf16), pltpu.SemaphoreType.DMA((2,))],
    )


def ffn_weights_kernel(h_ref, du_ref, a_ref, df_ref, w_hbm, into, outof, sent):
    part = pl.program_id(0)
    blocks, pieces, rows, width = w_hbm.shape
    half = rows // 2
    owners = pieces // blocks if pieces >= blocks else 1
    slot = part % 2

    def copies(part, slot):
        if pieces >= blocks:
            rows_out = w_hbm.at[:, pl.ds(part * owners, owners), pl.ds(half, half), :]
        else:
            rows_out = w_hbm.at[pl.ds(part, 1), :, pl.ds(half, half), :]
        return (
            pltpu.make_async_copy(into.at[slot], w_hbm.at[part, :, pl.ds(0, half), :], sent.at[slot, 0]),
            pltpu.make_async_copy(outof.at[slot], rows_out, sent.at[slot, 1]),
        )

    @pl.when(part >= 2)
    def _():
        for copy in copies(part - 2, slot):
            copy.wait()

    into[slot] = dot_tn(h_ref[...], du_ref[...]).astype(bf16).reshape(pieces, half, width)
    grad_out = dot_tn(a_ref[...], df_ref[...]).astype(bf16)
    for place in range(pieces):
        piece = grad_out[place * half : (place + 1) * half]
        if pieces >= blocks:
            outof[slot, place % blocks, place // blocks] = piece
        else:
            outof[slot, 0, place] = piece
    for copy in copies(part, slot):
        copy.start()

    @pl.when(part == pl.num_programs(0) - 1)
    def _():
        for copy in copies(part - 1, 1 - slot) + copies(part, slot):
            copy.wait()


def ffn_weights(second_low, grad_hidden, active, grad_out, pieces):
    tokens, width = second_low.shape
    blocks = active.shape[1] // width
    whole = pl.BlockSpec((tokens, width), lambda part: (0, 0), pipeline_mode=pl.Buffered(1))
    part = pl.BlockSpec((tokens, width), lambda part: (0, part))
    shape = (blocks, pieces, 2 * width // pieces, width)
    out_shape = (blocks, pieces // blocks) if pieces >= blocks else (1, pieces)
    return pl.pallas_call(
        ffn_weights_kernel,
        grid=(blocks,),
        in_specs=[whole, part, part, whole],
        out_specs=pl.BlockSpec(memory_space=pl.ANY),
        out_shape=jax.ShapeDtypeStruct(shape, bf16),
        scratch_shapes=[
            pltpu.VMEM((2, pieces, width // pieces, width), bf16),
            pltpu.VMEM((2,) + out_shape + (width // pieces, width), bf16),
            pltpu.SemaphoreType.DMA((2, 2)),
        ],
        compiler_params=params(),
        name="ffn_weights",
        cost_estimate=cost([(tokens, width, blocks * width)] * 2),
    )(second_low, grad_hidden, active, grad_out)


def pack_head_kernel(count, place, units, last, *refs):
    sources, out_ref, rows_ref, arrived, held = refs[:count], refs[count], refs[count + 1], refs[count + 2], refs[count + 3 :]
    own = last.shape[0]
    copies = [
        pltpu.make_async_copy(source, target, arrived.at[number])
        for number, (source, target) in enumerate(zip(sources, held))
    ]
    for copy in copies:
        copy.start()

    def unit_copy_by(act):
        rows = out_ref.at[pl.ds(0, own), :]

        @pl.when(place[0] < 3)
        def _():
            act(pltpu.make_async_copy(units.at[jnp.minimum(place[0], 2)], rows, arrived.at[count]))

        @pl.when(place[0] == 3)
        def _():
            act(pltpu.make_async_copy(last, rows, arrived.at[count]))

    unit_copy_by(lambda copy: copy.start())
    rows_ref[...] = jnp.zeros_like(rows_ref)
    for copy in copies:
        copy.wait()
    for number, ref in enumerate(held):
        rows_ref[: ref.shape[0], number * LANES : number * LANES + own] = ref[...].astype(f32)
    out_ref[own:, :] = rows_ref[...].astype(bf16)
    unit_copy_by(lambda copy: copy.wait())


def pack_head(place, units, last, vectors):
    own, width = last.shape
    count = len(vectors)
    return row_call(
        functools.partial(pack_head_kernel, count), "pack_head", place, (),
        [pl.BlockSpec(memory_space=pl.ANY)] * (2 + count), full(None),
        jax.ShapeDtypeStruct((own + 8, width), bf16), [], (units, last, *vectors),
        [pltpu.VMEM((8, width), f32), pltpu.SemaphoreType.DMA((count + 1,))]
        + [pltpu.VMEM(item.shape, item.dtype) for item in vectors],
        limit=58 * 2**20,
    )


def fold_call(kernel, name, spot, inputs, outs):
    return row_call(
        kernel, name, spot, (), [full(None)] * len(inputs), [full(None)] * len(outs),
        [jax.ShapeDtypeStruct(shape, kind) for shape, kind in outs], [], inputs, limit=12 * 2**20,
    )


def added(*parts):
    total = parts[0].astype(f32)
    for part in parts[1:]:
        total = total + part.astype(f32)
    return total


def fold_first_kernel(own, extra, spot, mine, got, keep_one, send_one, keep_two, send_two):
    high, side = spot[0], spot[3]
    half = own // 2
    slots = keep_one.shape[0] // half

    def take(place, low):
        rows = pl.ds(pl.multiple_of(place * own + low, 16), half)
        return added(mine[rows, :], got[rows, :]).astype(bf16)

    for slot in range(slots):
        rows = pl.ds(slot * half, half)
        keep_one[rows, :] = take(high * slots + slot, 0)
        send_one[rows, :] = take((1 - high) * slots + slot, 0)
        keep_two[rows, :] = take(2 * slot + side, half)
        send_two[rows, :] = take(2 * slot + 1 - side, half)
    if extra:
        vectors = added(mine[2 * slots * own :, :], got[2 * slots * own :, :]).astype(bf16)
        keep_one[slots * half :, :] = vectors
        send_one[slots * half :, :] = vectors


def fold_first(spot, mine, got, own):
    width = mine.shape[1]
    extra = mine.shape[0] - 2 * width
    rows = width // own * (own // 2)
    first, second = ((rows + extra, width), bf16), ((rows, width), bf16)
    return fold_call(
        functools.partial(fold_first_kernel, own, extra), "fold_first", spot, (mine, got),
        (first, first, second, second),
    )


def fold_second_kernel(
    half, extra, spot, keep_a, got_a, keep_b, got_b, keep_one, send_one, keep_two, send_two
):
    high, side = spot[0], spot[3]
    slots = keep_two.shape[0] // half

    def take(keep, got, place):
        rows = pl.ds(pl.multiple_of(place * half, 16), half)
        return added(keep[rows, :], got[rows, :]).astype(bf16)

    for slot in range(slots):
        rows = pl.ds(slot * half, half)
        keep_one[rows, :] = take(keep_a, got_a, 2 * slot + side)
        send_one[rows, :] = take(keep_a, got_a, 2 * slot + 1 - side)
        keep_two[rows, :] = take(keep_b, got_b, high * slots + slot)
        send_two[rows, :] = take(keep_b, got_b, (1 - high) * slots + slot)
    if extra:
        low = 2 * slots * half
        vectors = added(keep_a[low:, :], got_a[low:, :]).astype(bf16)
        keep_one[slots * half :, :] = vectors
        send_one[slots * half :, :] = vectors


def fold_second(spot, keep_a, got_a, keep_b, got_b, own):
    rows, width = keep_b.shape
    extra = keep_a.shape[0] - rows
    first, second = ((rows // 2 + extra, width), bf16), ((rows // 2, width), bf16)
    return fold_call(
        functools.partial(fold_second_kernel, own // 2, extra), "fold_second", spot,
        (keep_a, got_a, keep_b, got_b), (first, first, second, second),
    )


def fold_third_kernel(half, extra, spot, keep_a, got_a, keep_b, got_b, *parts):
    depth = spot[2]
    slots = keep_b.shape[0] // half
    for step, part in enumerate(parts):
        rows = pl.ds(pl.multiple_of((depth + step) % slots * half, 16), half)
        part[:half, :] = added(keep_a[rows, :], got_a[rows, :]).astype(bf16)
        part[half : 2 * half, :] = added(keep_b[rows, :], got_b[rows, :]).astype(bf16)
        if extra:
            low = slots * half
            part[2 * half :, :] = added(keep_a[low:, :], got_a[low:, :]).astype(bf16)


def fold_third(spot, keep_a, got_a, keep_b, got_b, own):
    rows, width = keep_b.shape
    extra = keep_a.shape[0] - rows
    part = ((own + extra, width), bf16)
    return fold_call(
        functools.partial(fold_third_kernel, own // 2, extra), "fold_third", spot,
        (keep_a, got_a, keep_b, got_b), (part,) * (rows // (own // 2)),
    )


def sources(spot, sent, got):
    high, core = spot[0], spot[1]
    rows = sent.shape[0] // 2
    return [
        (2 * y + c, ref, pl.ds(low, rows))
        for c, ref in ((core, sent), (1 - core, got))
        for y, low in ((high, 0), (1 - high, rows))
    ]


def finish_early_kernel(own, spot, sent, got, in_ref, out_ref, first_ref, rest_ref):
    width = sent.shape[1]
    for place, ref, rows in sources(spot, sent, got):
        low = rows.start
        in_ref[:, pl.ds(pl.multiple_of(place * width, width), width)] = ref[low : low + own, :].astype(f32)
        out_ref[pl.ds(pl.multiple_of(place * own, 8), own), :] = ref[low + own : low + 2 * own, :].astype(f32)
        unit = ref[low + 2 * own : low + 3 * own, :].astype(f32)

        @pl.when(place == 0)
        def _(unit=unit):
            first_ref[...] = unit

        @pl.when(place != 0)
        def _(unit=unit, place=place):
            rest_ref[place - 1] = unit


def finish_early(spot, sent, got, own):
    width = sent.shape[1]
    return fold_call(
        functools.partial(finish_early_kernel, own), "finish_early", spot, (sent, got),
        (((own, 4 * width), f32), ((4 * own, width), f32), ((own, width), f32), ((3, own, width), f32)),
    )


def finish_late_kernel(spot, sent, got, rest_ref, last_ref):
    for place, ref, rows in sources(spot, sent, got):
        unit = ref[rows, :].astype(f32)

        @pl.when(place == 3)
        def _(unit=unit):
            last_ref[...] = unit

        @pl.when(place != 3)
        def _(unit=unit, place=place):
            rest_ref[place] = unit


def finish_late(spot, sent, got):
    rows, width = sent.shape
    return fold_call(
        finish_late_kernel, "finish_late", spot, (sent, got),
        (((3, rows // 2, width), f32), ((rows // 2, width), f32)),
    )


def wide(array):
    return array.astype(f32)


def weight_grad(left, right):
    return dot_tn(left, right).astype(bf16)


def forward(
    target, memory, cotangent, info, pieces, head, mid, tail, vectors,
    mid_step=lambda *same: same, mid_last=lambda *same: same,
):
    queries, keys, values = project_self(info, target, head, vectors)
    queries, mid = mid_step(queries, mid)
    context_self, stats_self = self_attend(info, queries, keys, values)
    context_self, mid = mid_last(context_self, mid)
    total_first, first_low, query_cross = first_norm(info, target, context_self, mid, vectors)
    key_cross, value_cross = project_memory(info, memory, mid, vectors)
    context_cross, stats_cross = cross_attend(info, query_cross, key_cross, value_cross)
    output, second_low, active, du, df, do_cross, dz2, dc_cross, sums_ffn, sums_wide = ffn_block(
        info, total_first, context_cross, cotangent, head, tail, vectors
    )
    grad_ffn = ffn_weights(second_low, du, active, df, pieces)
    dq_cross, dk_cross, dv_cross = cross_attend_back(
        info, query_cross, key_cross, value_cross, dc_cross, context_cross, stats_cross
    )
    dz1, do_self, dc_self, sums_first = first_back(info, dz2, dq_cross, total_first, mid, vectors)
    grads = self_attend_back(info, queries, keys, values, dc_self, context_self, stats_self)
    memory, *grads = lax.optimization_barrier((memory, *grads))
    *grad_mid, sum_value = mid_weights(
        info, memory, dk_cross, dv_cross, (first_low, dq_cross, context_self, do_self)
    )
    cross = (context_cross, do_cross)
    sums = (sums_first, sum_value, sums_ffn, sums_wide)
    return output, grad_ffn, grad_mid, dz1, grads, dk_cross, dv_cross, cross, sums, mid


def forward_back(target, memory, cotangent, info, pieces, head, mid, tail, vectors):
    output, grad_ffn, grad_mid, dz1, grads, dk_cross, dv_cross, cross, sums, mid = forward(
        target, memory, cotangent, info, pieces, head, mid, tail, vectors
    )
    grad_self = self_weights(info, target, grads, cross, sums)
    target_grad = target_back(info, dz1, grads, head)
    memory_grad = memory_back(info, dk_cross, dv_cross, mid, 0, memory.shape[0])
    return (output, target_grad, memory_grad), grad_ffn, grad_mid, grad_self


def pair_swap(array, axis, bit):
    count = lax.axis_size(axis)
    return lax.ppermute(array, axis, [(place, place ^ bit) for place in range(count)])


def ring(array, axis, shift):
    count = lax.axis_size(axis)
    return lax.ppermute(array, axis, [(place, (place + shift) % count) for place in range(count)])


def pick(array, axis, index):
    return lax.dynamic_index_in_dim(array, index, axis, keepdims=False)


def places():
    dp, fsdp = lax.axis_index("dp"), lax.axis_index("fsdp")
    return dp // 2, dp % 2, fsdp // 2, fsdp % 2


def add_half(array, axis, mine, mesh_axis, bit):
    got = pair_swap(pick(array, axis, 1 - mine), mesh_axis, bit)
    return (wide(pick(array, axis, mine)) + wide(got)).astype(bf16)


def add_depth(array, depth):
    total = wide(pick(array, 0, depth))
    for step in (1, 2, 3):
        total = total + wide(ring(pick(array, 0, (depth + step) % 4), "fsdp", 2 * step))
    return total.astype(bf16)


def fence(*arrays):
    return lax.optimization_barrier(arrays)


def add(mine, got):
    return (wide(mine) + wide(got)).astype(bf16)


def cut(array):
    half = array.shape[-2] // 2 // 8 * 8
    return array[..., :half, :], array[..., half:, :]


def join_pair(array, axis, mine, mesh_axis, bit):
    return join(array, pair_swap(array, mesh_axis, bit), axis, mine)


def join(array, got, axis, mine):
    first = jnp.where(mine == 0, array, got)
    second = jnp.where(mine == 0, got, array)
    return jnp.stack([first, second], axis)


def share_dp(array):
    high, core, _, _ = places()
    both = join_pair(array, 0, high, "dp", 2)
    return join_pair(both, 1, core, "dp", 1).reshape((4,) + array.shape)


def join_depth(array, depth):
    parts = [array] + [ring(array, "fsdp", 2 * step) for step in (1, 2, 3)]
    out = jnp.zeros((4,) + array.shape, array.dtype)
    for step, part in enumerate(parts):
        out = lax.dynamic_update_index_in_dim(out, part, (depth - step) % 4, 0)
    return out


def gather_vectors(rows, own):
    pieces, _, width = rows.shape
    groups = width // LANES
    rows = rows.reshape(pieces, 8, groups, LANES)[..., :own]
    hidden = rows[:, :4, 2].reshape(4, pieces * own)
    rows = jnp.transpose(rows, (2, 1, 0, 3)).reshape(groups * 8, pieces * own)
    return wide(jnp.concatenate([rows[:16], hidden, rows[20:]], 0))


def fast_layer(
    target, memory, cotangent, bucket, source_len, self_qkv, self_out, self_bias, cross_qkv,
    cross_out, cross_bias, ffn_in, ffn_in_bias, ffn_out, ffn_out_bias, norm_gain, norm_bias,
):
    dp = lax.axis_index("dp")
    high, core, depth, side = places()
    count, width = memory.shape[0], target.shape[1]
    own = self_out.shape[0]
    pieces = width // own
    info = jnp.concatenate([bucket, source_len, core[None]])
    head = pack_head(
        dp[None],
        self_qkv,
        cross_out,
        (self_bias, cross_bias, ffn_in_bias.reshape(4, own), ffn_out_bias[None], norm_gain, norm_bias),
    )
    mid = pick(jnp.concatenate([self_out[None], cross_qkv], 0), 0, dp)
    head, mid = fence(join_depth(head, depth), mid)
    one, two = cut(head)
    one, two = join_pair(one, 1, side, "fsdp", 1), join_pair(two, 1, high, "dp", 2)
    one, two, mid = fence(one, two, mid)
    one, two = join_pair(one, 2, high, "dp", 2), join_pair(two, 1, side, "fsdp", 1)
    half = own // 2
    mine = jnp.concatenate([one, two[:, :, :, :half]], 3).reshape(pieces, 2, own, width)
    mine, mid, ffn_in, ffn_out = fence(mine, join_depth(mid, depth), ffn_in, ffn_out)
    got = pair_swap(mine, "dp", 1)
    vectors = gather_vectors(two[:, :, 0, half:].reshape(pieces, 8, width), own)
    three, four = cut(mid)
    in_cols = pick(ffn_in.reshape(own, 4, width), 1, dp)
    out_rows = pick(ffn_out.reshape(4, own, width), 0, dp)
    tail = lax.all_gather(
        jnp.concatenate([in_cols, out_rows], 0), ("dp", "fsdp"), axis=0, tiled=True
    ).reshape(4, pieces, 2 * own, width)
    parts = (three, pair_swap(three, "fsdp", 1), four, pair_swap(four, "dp", 2))

    def mid_step(queries, parts):
        queries, three, got_three, four, got_four = fence(queries, *parts)
        three, four = join(three, got_three, 1, side), join(four, got_four, 1, high)
        return queries, (three, pair_swap(three, "dp", 2), four, pair_swap(four, "fsdp", 1))

    def mid_last(context, parts):
        context, three, got_three, four, got_four = fence(context, *parts)
        three, four = join(three, got_three, 2, high), join(four, got_four, 1, side)
        mine = jnp.concatenate([three, four], 3).reshape(pieces, 2, own, width)
        return context, (mine, pair_swap(mine, "dp", 1))

    head = (mine, got)
    output, grad_ffn, grad_mid, dz1, grads, dk_cross, dv_cross, cross, sums, mid = forward(
        target, memory, cotangent, info, pieces, head, parts, tail, vectors, mid_step, mid_last
    )
    sum_ffn = lax.psum_scatter(
        grad_ffn.reshape(-1, width), ("dp", "fsdp"), scatter_dimension=0, tiled=True
    )
    spot = jnp.stack([high, core, depth, side])
    mine, other, target_late = fence(*grad_mid, target)
    got = pair_swap(other, "dp", 1)
    own_part, other = self_weights(info, target_late, grads, cross, sums)
    got, own_part, other = fence(got, own_part, other)
    keep_one, send_one, keep_two, send_two = fold_first(spot, mine, got, own)
    send_one, send_two, other, dz1 = fence(send_one, send_two, other, dz1)
    got_one, got_two = pair_swap(send_one, "dp", 2), pair_swap(send_two, "fsdp", 1)
    got = pair_swap(other, "dp", 1)
    target_grad = target_back(info, dz1, grads, head)
    got_one, got_two, got, target_grad = fence(got_one, got_two, got, target_grad)
    keep_one, send_one, keep_two, send_two = fold_second(spot, keep_one, got_one, keep_two, got_two, own)
    keep_three, send_three, keep_four, send_four = fold_first(spot, own_part, got, own)
    send_one, send_two, send_three, send_four, dk_cross = fence(
        send_one, send_two, send_three, send_four, dk_cross
    )
    got_one, got_two = pair_swap(send_one, "fsdp", 1), pair_swap(send_two, "dp", 2)
    got_three, got_four = pair_swap(send_three, "dp", 2), pair_swap(send_four, "fsdp", 1)
    memory_grad = memory_back(info, dk_cross, dv_cross, mid, 0, count // 2)
    got_one, got_two, got_three, got_four, memory_grad = fence(
        got_one, got_two, got_three, got_four, memory_grad
    )
    sum_mid, *sends = fold_third(spot, keep_one, got_one, keep_two, got_two, own)
    keep_three, send_three, keep_four, send_four = fold_second(
        spot, keep_three, got_three, keep_four, got_four, own
    )
    *sends, send_three, send_four, dk_cross = fence(*sends, send_three, send_four, dk_cross)
    rings = [ring(item, "fsdp", 2 * step) for step, item in zip((1, 2, 3), sends)]
    got_three, got_four = pair_swap(send_three, "fsdp", 1), pair_swap(send_four, "dp", 2)
    memory_grad = memory_back(
        info, dk_cross, dv_cross, mid, count // 2, count - count // 2, start=(memory_grad,)
    )
    got_three, got_four, memory_grad, *rings = fence(got_three, got_four, memory_grad, *rings)
    sum_mid = added(sum_mid, *rings).astype(bf16)
    early = jnp.concatenate([sum_ffn, sum_mid], 0)
    sum_self, *sends = fold_third(spot, keep_three, got_three, keep_four, got_four, own)
    *sends, early = fence(*sends, early)
    rings = [ring(item, "fsdp", 2 * step) for step, item in zip((1, 2, 3), sends)]
    got = pair_swap(early, "dp", 2)
    got, *rings = fence(got, *rings)
    late = added(sum_self, *rings)
    vectors = late[-VECTORS:]
    late = late[:-VECTORS].astype(bf16)
    early = jnp.concatenate([early, got], 0)
    early, late = fence(early, late)
    got_early = pair_swap(early, "dp", 1)
    got = pair_swap(late, "dp", 2)
    late = jnp.concatenate([late, got], 0)
    late, got_early = fence(late, got_early)
    got = pair_swap(late, "dp", 1)
    grad_in, grad_out, grad_self_out, grad_cross_qkv = finish_early(spot, early, got_early, own)
    place = lax.axis_index("fsdp")
    hidden = pick(vectors[6:10].reshape(pieces, 4 * own), 0, place)
    vectors = lax.dynamic_slice_in_dim(vectors, place * own, own, 1)
    got, grad_in, hidden, vectors = fence(got, grad_in, hidden, vectors)
    grad_self_qkv, grad_cross_out = finish_late(spot, late, got)
    return (
        output, target_grad, memory_grad, grad_self_qkv, grad_self_out, vectors[:3], grad_cross_qkv,
        grad_cross_out, vectors[3:6], grad_in, hidden, grad_out, vectors[10], vectors[11:14], vectors[14:17],
    )


def plain_layer(
    target, memory, cotangent, bucket, source_len, self_qkv, self_out, self_bias, cross_qkv,
    cross_out, cross_bias, ffn_in, ffn_in_bias, ffn_out, ffn_out_bias, norm_gain, norm_bias,
):
    gather = lambda item, axis: lax.all_gather(item, "fsdp", axis=axis, tiled=True)
    info = jnp.concatenate([bucket, source_len, jnp.zeros_like(bucket)])
    width = target.shape[1]
    blocks = ffn_out.shape[0] * lax.axis_size("fsdp") // width
    split = lambda units: (units[None, 0::2], units[None, 1::2])
    head = split(jnp.concatenate([gather(self_qkv, 1), gather(cross_out, 0)[None]], 0))
    mid = split(jnp.concatenate([gather(self_out, 0)[None], gather(cross_qkv, 1)], 0))
    ffn_in_w = jnp.swapaxes(gather(ffn_in, 0).reshape(width, blocks, width), 0, 1)
    tail = jnp.concatenate([ffn_in_w, gather(ffn_out, 0).reshape(blocks, width, width)], 1)[:, None]
    vectors = (
        gather(self_bias, 1), gather(cross_bias, 1), gather(ffn_in_bias, 0).reshape(blocks, width),
        gather(ffn_out_bias, 0)[None], gather(norm_gain, 1), gather(norm_bias, 1),
    )
    vectors = wide(
        jnp.concatenate([jnp.pad(item, ((0, 8 - item.shape[0]), (0, 0))) for item in vectors], 0)
    )
    outs, grad_ffn, grad_mid, grad_self = forward_back(
        target, memory, cotangent, info, 1, head, mid, tail, vectors
    )

    def reduce(grad, axis):
        piece = lax.psum_scatter(wide(grad), "fsdp", scatter_dimension=axis, tiled=True)
        return lax.psum(piece, "dp")

    def units(mine, other):
        both = [item[: 2 * width].reshape(2, width, width) for item in (mine, other)]
        return jnp.stack(both, 1).reshape(4, width, width)

    grad_in = jnp.swapaxes(grad_ffn[:, 0, :width], 0, 1).reshape(width, blocks * width)
    grad_out = grad_ffn[:, 0, width:].reshape(blocks * width, width)
    vectors = grad_self[0][2 * width :]
    grad_self, grad_mid = units(*grad_self), units(*grad_mid)
    return outs + (
        reduce(grad_self[:3], 1),
        reduce(grad_mid[0], 0),
        reduce(vectors[:3], 1),
        reduce(grad_mid[1:], 1),
        reduce(grad_self[3], 0),
        reduce(vectors[3:6], 1),
        reduce(grad_in, 0),
        reduce(vectors[6 : 6 + blocks].reshape(-1), 0),
        reduce(grad_out, 0),
        reduce(vectors[10], 0),
        reduce(vectors[11:14], 1),
        reduce(vectors[14:17], 1),
    )


def solution(mesh):
    rows = P(("dp", "fsdp"))
    first = P("fsdp")
    second = P(None, "fsdp")
    weights = (second, first, second, second, first, second, first, first, first, first, second, second)
    layer = fast_layer if (mesh.shape["dp"], mesh.shape["fsdp"]) == (4, 8) else plain_layer
    return jax.shard_map(
        layer,
        mesh=mesh,
        in_specs=(rows,) * 5 + weights,
        out_specs=(rows,) * 3 + weights,
        check_vma=False,
    )
```

```python
import functools
import math
import jax
import jax.numpy as jnp
from jax import lax
from jax.sharding import PartitionSpec as P
from jax.experimental import pallas as pl
from jax.experimental.pallas import tpu as pltpu

HEAD = 64
PAIR = 2 * HEAD
BLOCK = 256
very_low = -1e30
VMEM_LIMIT = 60 * 2**20
f32 = jnp.float32
bf16 = jnp.bfloat16


def dot_nt(left, right):
    return lax.dot_general(left, right, (((1,), (1,)), ((), ())), preferred_element_type=f32)


def dot_nn(left, right):
    return lax.dot_general(left, right, (((1,), (0,)), ((), ())), preferred_element_type=f32)


def dot_tn(left, right):
    return lax.dot_general(left, right, (((0,), (0,)), ((), ())), preferred_element_type=f32)


def split_pair(pair):
    lane = lax.broadcasted_iota(jnp.int32, pair.shape, 1)
    none = jnp.zeros_like(pair)
    return (jnp.where(lane < HEAD, pair, none), jnp.where(lane < HEAD, none, pair))


def mask_tail(scores, valid):
    low = scores.shape[0] - valid.shape[0]
    if low == 0:
        return jnp.where(valid, scores, very_low)
    return jnp.concatenate([scores[:low], jnp.where(valid, scores[low:], very_low)], 0)


def stacked(pair):
    return jnp.concatenate(split_pair(pair), 0)


def score_tile(queries, keys, valid):
    return mask_tail(dot_nt(keys, stacked(queries)), valid)


def attend_tile(scores, values):
    count = scores.shape[1] // 2
    values_t = values.T
    highest = jnp.max(scores, 0, keepdims=True)
    raised = jnp.exp(scores - highest)
    summed = jnp.sum(raised, 0, keepdims=True)
    raised = raised.astype(bf16)
    context = jnp.concatenate(
        [
            dot_nn(values_t[half * HEAD : (half + 1) * HEAD], raised[:, half * count : (half + 1) * count])
            / summed[:, half * count : (half + 1) * count]
            for half in range(2)
        ],
        0,
    )
    return context.T.astype(bf16), highest + jnp.log(summed)


def head_sums(pair):
    turned = pair.T
    return jnp.concatenate(
        [jnp.sum(turned[half * HEAD : (half + 1) * HEAD], 0, keepdims=True) for half in range(2)], 1
    )


def back_tile(scores, queries, keys, values, grads, contexts, logsum):
    count = scores.shape[1] // 2
    grad_rows = stacked(grads)
    grad_shares = dot_nt(values, grad_rows)
    inner = head_sums(grads.astype(f32) * contexts.astype(f32))
    keys_t = keys.T
    shares = jnp.exp(scores - logsum)
    grad_scores = (shares * (grad_shares - inner)).astype(bf16)
    grad_values = dot_nn(shares.astype(bf16), grad_rows)
    grad_keys = dot_nn(grad_scores, stacked(queries))
    grad_queries = jnp.concatenate(
        [
            dot_nn(keys_t[half * HEAD : (half + 1) * HEAD], grad_scores[:, half * count : (half + 1) * count])
            for half in range(2)
        ],
        0,
    ).T
    grad_queries = (grad_queries.astype(bf16).astype(f32) * HEAD**-0.5).astype(bf16)
    return grad_queries, grad_keys, grad_values


def causal(columns):
    key = lax.broadcasted_iota(jnp.int32, (BLOCK, columns), 0)
    query = lax.broadcasted_iota(jnp.int32, (BLOCK, columns), 1) % BLOCK
    return key <= query


def key_spans(tokens, whole):
    return [
        (0 if whole else low, low, low + BLOCK) for low in range(0, tokens, BLOCK)
    ]


def self_kernel(skip, info, q_ref, k_ref, v_ref, o_ref, stat_ref):
    tokens = q_ref.shape[0]
    valid = causal(2 * BLOCK)

    def run(whole):
        spans = key_spans(tokens, whole)
        score = lambda span: score_tile(q_ref[span[1] : span[2], :], k_ref[span[0] : span[2], :], valid)
        ahead = score(spans[0])
        for part, (low, start, stop) in enumerate(spans):
            scores = ahead
            if part + 1 < len(spans):
                ahead = score(spans[part + 1])
            o_ref[start:stop, :], stat_ref[0, part] = attend_tile(scores, v_ref[low:stop, :])

    pl.when(info[0] == 1)(functools.partial(run, False))
    pl.when(info[0] != 1)(functools.partial(run, True))


def self_back_kernel(skip, info, q_ref, k_ref, v_ref, g_ref, o_ref, stat_ref, *refs):
    dq_ref, dk_ref, dv_ref, key_sum, value_sum = refs[skip:]
    tokens = q_ref.shape[0]
    valid = causal(2 * BLOCK)

    def run(whole):
        spans = key_spans(tokens, whole)[::-1]
        score = lambda span: score_tile(q_ref[span[1] : span[2], :], k_ref[span[0] : span[2], :], valid)
        ahead = score(spans[0])
        for step, (low, start, stop) in enumerate(spans):
            scores = ahead
            if step + 1 < len(spans):
                ahead = score(spans[step + 1])
            dq_ref[start:stop, :], grad_keys, grad_values = back_tile(
                scores,
                q_ref[start:stop, :],
                k_ref[low:stop, :],
                v_ref[low:stop, :],
                g_ref[start:stop, :],
                o_ref[start:stop, :],
                stat_ref[0, start // BLOCK],
            )
            if not whole:
                dk_ref[start:stop, :] = grad_keys.astype(bf16)
                dv_ref[start:stop, :] = grad_values.astype(bf16)
            elif stop == tokens:
                key_sum[...] = grad_keys
                value_sum[...] = grad_values
            else:
                key_sum[:stop, :] += grad_keys
                value_sum[:stop, :] += grad_values
        if whole:
            dk_ref[...] = key_sum[...].astype(bf16)
            dv_ref[...] = value_sum[...].astype(bf16)

    pl.when(info[0] == 1)(functools.partial(run, False))
    pl.when(info[0] != 1)(functools.partial(run, True))


def by_length(info, row, mem_len, run):
    length = info[1 + row]
    for width in range(BLOCK, mem_len + 1, BLOCK):

        @pl.when((length > width - BLOCK) & (length <= width))
        def _(width=width):
            run(width, lambda columns: lax.broadcasted_iota(jnp.int32, (BLOCK, columns), 0) < length - (width - BLOCK))


def cross_kernel(skip, info, q_ref, k_ref, v_ref, o_ref, stat_ref):
    tokens = q_ref.shape[0]
    count, mem_len, _ = k_ref.shape
    parts = tokens // BLOCK

    half = mem_len // 2

    @pl.when(info[0] == 1)
    def _():
        def step(pair, none):
            lengths = [info[1 + 2 * pair], info[2 + 2 * pair]]

            def run(*widths):
                tiles = []
                for place, width in enumerate(widths):
                    row = 2 * pair + place
                    rows = pl.ds(pl.multiple_of(row * BLOCK, BLOCK), BLOCK)
                    key = lax.broadcasted_iota(jnp.int32, (half, 2 * BLOCK), 0) + (width - half)
                    scores = score_tile(q_ref[rows, :], k_ref[row, :width, :], key < lengths[place])
                    tiles.append((row, rows, width, scores))
                for row, rows, width, scores in tiles:
                    o_ref[rows, :], stat_ref[0, row] = attend_tile(scores, v_ref[row, :width, :])

            for one in (False, True):
                for two in (False, True):
                    chosen = ((lengths[0] > half) == one) & ((lengths[1] > half) == two)
                    pl.when(chosen)(functools.partial(run, half << one, half << two))
            return none

        lax.fori_loop(0, count // 2, step, None)

    @pl.when(info[0] != 1)
    def _():
        def run(width, valid):
            scores = score_tile(q_ref[...], k_ref[0, :width, :], valid(2 * tokens))
            o_ref[...], stats = attend_tile(scores, v_ref[0, :width, :])
            for part in range(parts):
                low = part * BLOCK
                stat_ref[0, part] = jnp.concatenate(
                    [stats[:, low : low + BLOCK], stats[:, tokens + low : tokens + low + BLOCK]], 1
                )

        by_length(info, 0, mem_len, run)


def cross_back_kernel(skip, info, q_ref, k_ref, v_ref, g_ref, o_ref, stat_ref, *refs):
    dq_ref, dk_ref, dv_ref = refs[skip:]
    tokens = q_ref.shape[0]
    count, mem_len, _ = k_ref.shape
    parts = tokens // BLOCK

    def store(row, width, grad_keys, grad_values):
        dk_ref[row, :width, :] = grad_keys.astype(bf16)
        dv_ref[row, :width, :] = grad_values.astype(bf16)
        if width < mem_len:
            rest = jnp.zeros((mem_len - width, PAIR), bf16)
            dk_ref[row, width:, :] = rest
            dv_ref[row, width:, :] = rest

    @pl.when(info[0] == 1)
    def _():
        def step(row, none):
            rows = pl.ds(pl.multiple_of(row * BLOCK, BLOCK), BLOCK)

            def run(width, valid):
                keys = k_ref[row, :width, :]
                scores = score_tile(q_ref[rows, :], keys, valid(2 * BLOCK))
                dq_ref[rows, :], grad_keys, grad_values = back_tile(
                    scores, q_ref[rows, :], keys, v_ref[row, :width, :], g_ref[rows, :], o_ref[rows, :],
                    stat_ref[0, row],
                )
                store(row, width, grad_keys, grad_values)

            by_length(info, row, mem_len, run)
            return none

        lax.fori_loop(0, count, step, None)

    @pl.when(info[0] != 1)
    def _():
        def run(width, valid):
            keys = k_ref[0, :width, :]
            scores = score_tile(q_ref[...], keys, valid(2 * tokens))
            stats = jnp.concatenate(
                [stat_ref[0, part][:, half * BLOCK : (half + 1) * BLOCK] for half in range(2) for part in range(parts)],
                1,
            )
            dq_ref[...], grad_keys, grad_values = back_tile(
                scores, q_ref[...], keys, v_ref[0, :width, :], g_ref[...], o_ref[...], stats
            )
            store(0, width, grad_keys, grad_values)

        by_length(info, 0, mem_len, run)


def params():
    return pltpu.CompilerParams(vmem_limit_bytes=VMEM_LIMIT)


def cost(matmuls, moved=2**23):
    flops = 2 * sum(math.prod(sizes) for sizes in matmuls)
    return pl.CostEstimate(flops=flops, bytes_accessed=moved, transcendentals=0)


def attend_call(kernel, name, info, queries, keys, values, rest=None, first=0, count=None, start=()):
    tokens, width = queries.shape
    pairs = width // PAIR
    count = count or pairs
    parts = tokens // BLOCK
    back = rest is not None
    own = pl.BlockSpec((tokens, PAIR), lambda pair, info: (0, pair + first))
    stat = pl.BlockSpec((1, parts, 1, 2 * BLOCK), lambda pair, info: (pair + first, 0, 0, 0))
    if keys.ndim == 2:
        other = own
        scratch = [pltpu.VMEM((tokens, PAIR), f32)] * 2 if back else []
    else:
        other = pl.BlockSpec(keys.shape[:2] + (PAIR,), lambda pair, info: (0, 0, pair + first))
        scratch = []
    queries_shape = jax.ShapeDtypeStruct((tokens, width), bf16)
    keys_shape = jax.ShapeDtypeStruct(keys.shape, bf16)
    stat_shape = jax.ShapeDtypeStruct((pairs, parts, 1, 2 * BLOCK), f32)
    inputs = (queries, keys, values) + (rest or ())
    return pl.pallas_call(
        functools.partial(kernel, len(start)),
        grid_spec=pltpu.PrefetchScalarGridSpec(
            num_scalar_prefetch=1,
            grid=(count,),
            in_specs=[own, other, other]
            + ([own, own, stat] if back else [])
            + [pl.BlockSpec(memory_space=pl.ANY)] * len(start),
            out_specs=[own, other, other] if back else [own, stat],
            scratch_shapes=scratch,
        ),
        out_shape=[queries_shape, keys_shape, keys_shape] if back else [queries_shape, stat_shape],
        input_output_aliases={1 + len(inputs) + place: place for place in range(len(start))},
        compiler_params=params(),
        name=name,
        cost_estimate=cost([(tokens, tokens, width)] * (24 if back else 12)),
    )(info, *inputs, *start)


def self_attend(info, queries, keys, values):
    return attend_call(self_kernel, "self_attend", info, queries, keys, values)


def cross_attend(info, queries, keys, values):
    return attend_call(cross_kernel, "cross_attend", info, queries, keys, values)


def self_attend_back(info, queries, keys, values, *rest, **span):
    return attend_call(self_back_kernel, "self_attend_back", info, queries, keys, values, rest, **span)


def cross_attend_back(info, queries, keys, values, *rest, **span):
    return attend_call(cross_back_kernel, "cross_attend_back", info, queries, keys, values, rest, **span)


epsilon = 1e-05
VECTORS = 32
LANES = 128


def normalise(total):
    middle = jnp.mean(total, -1, keepdims=True)
    centred = total - middle
    variance = jnp.mean(centred * centred, -1, keepdims=True)
    scale = lax.rsqrt(variance + epsilon)
    return centred * scale, scale


def normalise_back(grad, gain, normal, scale):
    scaled = grad * gain
    first = jnp.mean(scaled, -1, keepdims=True)
    second = jnp.mean(scaled * normal, -1, keepdims=True)
    return (scaled - first - normal * second) * scale


def add_rows(ref, row, value):
    ref[row : row + 1, :] += jnp.sum(value, 0, keepdims=True)


def start_sums(*refs):
    @pl.when(pl.program_id(0) == 0)
    def _():
        for ref in refs:
            ref[...] = jnp.zeros_like(ref)


def full(array):
    return pl.BlockSpec(memory_space=pltpu.VMEM)


def row_block(rows, width):
    return pl.BlockSpec((rows, width), lambda part, *info: (part, 0))


def keep_block(rows, width):
    return pl.BlockSpec((rows, width), lambda part, *info: (0, 0))


def unit(ref, high=0):
    return ref[:, high].reshape(ref.shape[0] * ref.shape[2], ref.shape[3])


def by_core(info, mine, got, run):
    core = info[info.shape[0] - 1]
    pl.when(core == 0)(lambda: run(mine, got))
    pl.when(core != 0)(lambda: run(got, mine))


def unit_block(array, high):
    return pl.BlockSpec(
        array.shape[:1] + (1,) + array.shape[2:],
        lambda *place: (0, high, 0, 0),
        pipeline_mode=pl.Buffered(1),
    )


def first_kernel(info, x_ref, c_ref, mine, got, vec_ref, z_ref, low_ref):
    def run(even, odd):
        total = x_ref[...].astype(f32) + dot_nn(c_ref[...], unit(odd)) + vec_ref[2:3, :]
        normal, _ = normalise(total)
        z_ref[...] = total
        low_ref[...] = (normal * vec_ref[32:33, :] + vec_ref[40:41, :]).astype(bf16)

    by_core(info, mine, got, run)


def row_call(
    kernel, name, info, grid, in_specs, out_specs, out_shape, matmuls, inputs, scratch=(), aliases=None, limit=VMEM_LIMIT
):
    return pl.pallas_call(
        kernel,
        grid_spec=pltpu.PrefetchScalarGridSpec(
            num_scalar_prefetch=1,
            grid=grid,
            in_specs=in_specs,
            out_specs=out_specs,
            scratch_shapes=scratch,
        ),
        out_shape=out_shape,
        input_output_aliases=aliases or {},
        compiler_params=pltpu.CompilerParams(vmem_limit_bytes=limit),
        name=name,
        cost_estimate=cost(matmuls),
    )(info, *inputs)


def first_norm(info, x, context, head, vectors, rows=512):
    tokens, width = x.shape
    block = row_block(rows, width)
    low = jax.ShapeDtypeStruct((tokens, width), bf16)
    return row_call(
        first_kernel, "first_norm", info, (tokens // rows,),
        [block, block, unit_block(head[0], 1), unit_block(head[1], 1), full(vectors)],
        [block] * 2, [jax.ShapeDtypeStruct((tokens, width), f32), low],
        [(tokens, width, width)] * 2, (x, context, *head, vectors),
    )


def chunks(blocks, pieces, block):
    return [divmod(number, blocks) for number in range(block * pieces, (block + 1) * pieces)]


def ffn_kernel(
    info,
    z_ref,
    c_ref,
    cot_ref,
    mine,
    got,
    tail_ref,
    vec_ref,
    out_ref,
    low_ref,
    act_ref,
    du_ref,
    df_ref,
    do_ref,
    dz_ref,
    dc_ref,
    sum_ref,
    wide_ref,
    slope_ref,
    out_w,
):
    start_sums(sum_ref, wide_ref)

    @pl.when(pl.program_id(0) == 0)
    def _():
        def load(even, odd):
            out_w[...] = unit(even)

        by_core(info, mine, got, load)

    width = z_ref.shape[1]
    blocks, pieces, both = tail_ref.shape[:3]
    in_w = lambda block: tail_ref[block, :, : both // 2].reshape(width, width)
    ffn_w = lambda block: jnp.concatenate(
        [tail_ref[d, f, both // 2 :, :] for f, d in chunks(blocks, pieces, block)], 0
    )
    gain_first, gain_mid, gain_last = [vec_ref[row : row + 1, :] for row in (32, 33, 34)]
    shift_first, shift_mid, shift_last = [vec_ref[row : row + 1, :] for row in (40, 41, 42)]
    normal_first, _ = normalise(z_ref[...])
    first = normal_first * gain_first + shift_first
    normal_mid, scale_mid = normalise(first + dot_nn(c_ref[...], out_w[...]) + vec_ref[10 : 11, :])
    second = normal_mid * gain_mid + shift_mid
    second_low = second.astype(bf16)
    low_ref[...] = second_low
    total = second + vec_ref[24 : 25, :]
    ahead = dot_nn(second_low, in_w(0))
    for block in range(blocks):
        cols = pl.ds(block * width, width)
        value = ahead + vec_ref[16 + block : 17 + block, :]
        if block + 1 < blocks:
            ahead = dot_nn(second_low, in_w(block + 1))
        share = 0.5 * (1.0 + lax.erf(value * 0.5**0.5))
        density = jnp.exp(-0.5 * value * value) * 0.3989422804014327
        active = (value * share).astype(bf16)
        slope_ref[:, cols] = share + value * density
        act_ref[:, cols] = active
        total = total + dot_nn(active, ffn_w(block))
    normal_last, scale_last = normalise(total)
    out_ref[...] = (normal_last * gain_last + shift_last).astype(bf16)
    cot = cot_ref[...].astype(f32)
    add_rows(sum_ref, 0, cot * normal_last)
    add_rows(sum_ref, 1, cot)
    grad_last = normalise_back(cot, gain_last, normal_last, scale_last)
    grad_low = grad_last.astype(bf16)
    df_ref[...] = grad_low
    add_rows(sum_ref, 2, grad_low.astype(f32))
    grad_second = grad_last
    ahead = dot_nt(grad_low, ffn_w(0))
    for block in range(blocks):
        cols = pl.ds(block * width, width)
        grad_hidden = (ahead * slope_ref[:, cols]).astype(bf16)
        if block + 1 < blocks:
            ahead = dot_nt(grad_low, ffn_w(block + 1))
        du_ref[:, cols] = grad_hidden
        wide_ref[:, cols] += jnp.sum(grad_hidden.astype(f32), 0, keepdims=True)
        grad_second = grad_second + dot_nt(grad_hidden, in_w(block))
    add_rows(sum_ref, 3, grad_second * normal_mid)
    add_rows(sum_ref, 4, grad_second)
    grad_mid = normalise_back(grad_second, gain_mid, normal_mid, scale_mid)
    dz_ref[...] = grad_mid
    grad_low = grad_mid.astype(bf16)
    do_ref[...] = grad_low
    add_rows(sum_ref, 5, grad_low.astype(f32))
    dc_ref[...] = dot_nt(grad_low, out_w[...]).astype(bf16)


def ffn_block(info, z, context, cotangent, mid, tail, vectors, rows=256):
    tokens, width = z.shape
    hidden = tail.shape[0] * width
    block = row_block(rows, width)
    wide = row_block(rows, hidden)
    narrow_shape = jax.ShapeDtypeStruct((tokens, width), bf16)
    wide_shape = jax.ShapeDtypeStruct((tokens, hidden), bf16)
    return row_call(
        ffn_kernel, "ffn_block", info, (tokens // rows,),
        [block] * 3 + [unit_block(mid[0], 0), unit_block(mid[1], 0), full(tail), full(vectors)],
        [block, block, wide, wide, block, block, block, block, keep_block(8, width), keep_block(1, hidden)],
        [
            narrow_shape, narrow_shape, wide_shape, wide_shape, narrow_shape, narrow_shape,
            jax.ShapeDtypeStruct((tokens, width), f32), narrow_shape,
            jax.ShapeDtypeStruct((8, width), f32), jax.ShapeDtypeStruct((1, hidden), f32),
        ],
        [(tokens, width, hidden)] * 8, (z, context, cotangent, *mid, tail, vectors),
        [pltpu.VMEM((rows, hidden), f32), pltpu.VMEM((width, width), bf16)],
    )


def first_back_kernel(
    info, dz2_ref, dq_ref, z_ref, mine, got, head_mine, head_got, vec_ref, dz_ref, do_ref, dc_ref, sum_ref
):
    start_sums(sum_ref)

    def run(query, out):
        grad_query = dq_ref[...]
        grad_first = dz2_ref[...] + dot_nt(grad_query, unit(query))
        normal, scale = normalise(z_ref[...])
        add_rows(sum_ref, 0, grad_first * normal)
        add_rows(sum_ref, 1, grad_first)
        grad_start = normalise_back(grad_first, vec_ref[32 : 33, :], normal, scale)
        dz_ref[...] = grad_start
        grad_low = grad_start.astype(bf16)
        do_ref[...] = grad_low
        add_rows(sum_ref, 2, grad_low.astype(f32))
        add_rows(sum_ref, 3, grad_query.astype(f32))
        dc_ref[...] = dot_nt(grad_low, unit(out)).astype(bf16)

    core = info[info.shape[0] - 1]
    pl.when(core == 0)(lambda: run(got, head_got))
    pl.when(core != 0)(lambda: run(mine, head_mine))


def first_back(info, dz2, grad_query, z, head, mid, vectors, rows=512):
    tokens, width = z.shape
    block = row_block(rows, width)
    low = jax.ShapeDtypeStruct((tokens, width), bf16)
    return row_call(
        first_back_kernel, "first_back", info, (tokens // rows,),
        [block] * 3
        + [unit_block(item, 0) for item in mid]
        + [unit_block(item, 1) for item in head]
        + [full(vectors)],
        [block] * 3 + [keep_block(8, width)],
        [jax.ShapeDtypeStruct((tokens, width), f32), low, low, jax.ShapeDtypeStruct((8, width), f32)],
        [(tokens, width, width)] * 4, (dz2, grad_query, z, *mid, *head, vectors),
    )


def needed(info, row, part, rows):
    return ((info[0] == 1) | (row == 0)) & (part * rows < info[1 + row])


def needed_place(info, row, part, rows):
    used = jnp.where(info[0] == 1, row, 0)
    last = (info[1 + used] + rows - 1) // rows - 1
    return used, jnp.where(info[0] == 1, jnp.minimum(part, last), jnp.where(row == 0, jnp.minimum(part, last), last))


def project_kernel(
    rows, info, m_ref, mine, got, low_ref, query_mine, query_got, vec_ref, k_ref, v_ref, q_ref
):
    row, part = pl.program_id(0), pl.program_id(1)

    @pl.when((row == 0) & (part == 0))
    def _():
        def query(even, odd):
            q_ref[...] = ((dot_nn(low_ref[...], unit(odd)) + vec_ref[8:9, :]) * HEAD**-0.5).astype(bf16)

        by_core(info, query_mine, query_got, query)

    @pl.when(needed(info, row, part, rows))
    def _():
        def run(even, odd):
            memory = m_ref[0]
            k_ref[0] = dot_nn(memory, unit(even)).astype(bf16)
            v_ref[0] = (dot_nn(memory, unit(odd)) + vec_ref[9:10, :]).astype(bf16)

        by_core(info, mine, got, run)


def memory_block(rows, width, first=0):
    return pl.BlockSpec(
        (1, rows, width), lambda row, part, info: needed_place(info, row + first, part, rows) + (0,)
    )


def project_memory(info, memory, low, mid, vectors, rows=512):
    count, length, width = memory.shape
    block = memory_block(rows, width)
    return row_call(
        functools.partial(project_kernel, rows), "project_memory", info, (count, length // rows),
        [block]
        + [unit_block(item, 1) for item in mid]
        + [full(low)]
        + [unit_block(item, 0) for item in mid]
        + [full(vectors)],
        [block] * 2 + [pl.BlockSpec(low.shape, lambda row, part, info: (0, 0))],
        [jax.ShapeDtypeStruct(memory.shape, bf16)] * 2 + [jax.ShapeDtypeStruct(low.shape, bf16)],
        [(count, length, width, width)] * 2, (memory, *mid, low, *mid, vectors),
    )


def memory_back_kernel(rows, first, info, dk_ref, dv_ref, mine, got, *refs):
    out_ref = refs[-1]
    here = needed(info, pl.program_id(0) + first, pl.program_id(1), rows)

    @pl.when(here)
    def _():
        def run(even, odd):
            out_ref[0] = dot_nt(dk_ref[0], unit(even)) + dot_nt(dv_ref[0], unit(odd))

        by_core(info, mine, got, run)

    @pl.when(jnp.logical_not(here))
    def _():
        out_ref[...] = jnp.zeros_like(out_ref)


def memory_back(info, grad_keys, grad_values, mid, first, count, start=(), rows=1024):
    length, width = grad_keys.shape[1:]
    block = memory_block(rows, width, first)
    return row_call(
        functools.partial(memory_back_kernel, rows, first), "memory_back", info, (count, length // rows),
        [block, block, unit_block(mid[0], 1), unit_block(mid[1], 1)]
        + [pl.BlockSpec(memory_space=pl.ANY)] * len(start),
        pl.BlockSpec((1, rows, width), lambda row, part, info: (row + first, part, 0)),
        jax.ShapeDtypeStruct(grad_keys.shape, f32),
        [(count, length, width, width)] * 2, (grad_keys, grad_values, *mid, *start),
        aliases={5: 0} if start else {},
    )


def unit_copy(info, stage, sent, mine, other, number, act):
    width = stage.shape[1]
    here = info[info.shape[0] - 1] == number % 2
    for ref, chosen in ((mine, here), (other, jnp.logical_not(here))):

        @pl.when(chosen)
        def _(ref=ref):
            rows = ref.at[pl.ds(number // 2 * width, width), :]
            act(pltpu.make_async_copy(stage.at[number], rows, sent.at[number]))


def put_unit(info, stage, sent, mine, other, number, value):
    stage[number] = value.astype(bf16)
    unit_copy(info, stage, sent, mine, other, number, lambda copy: copy.start())


def end_units(info, stage, sent, mine, other):
    for number in range(4):
        unit_copy(info, stage, sent, mine, other, number, lambda copy: copy.wait())


def unit_scratch(width):
    return [pltpu.VMEM((4, width, width), bf16), pltpu.SemaphoreType.DMA((4,))]


def mid_weights_kernel(
    rows, info, m_ref, dk_ref, dv_ref, first_hbm, dq_hbm, self_hbm, dself_hbm,
    mine, other, sum_ref, key_sum, value_sum, stage, sent, held, arrived,
):
    row, part = pl.program_id(0), pl.program_id(1)
    out = (info, stage, sent, mine, other)
    fetches = [
        pltpu.make_async_copy(source, held.at[place], arrived.at[place])
        for place, source in enumerate((self_hbm, dself_hbm, first_hbm, dq_hbm))
    ]

    @pl.when((row == 0) & (part == 0))
    def _():
        for fetch in fetches:
            fetch.start()
        key_sum[...] = jnp.zeros_like(key_sum)
        value_sum[...] = jnp.zeros_like(value_sum)
        sum_ref[...] = jnp.zeros_like(sum_ref)

    @pl.when(needed(info, row, part, rows))
    def _():
        memory = m_ref[0]
        key_sum[...] += dot_tn(memory, dk_ref[0])
        value_sum[...] += dot_tn(memory, dv_ref[0])
        sum_ref[...] += jnp.sum(dv_ref[0].astype(f32), 0, keepdims=True)

    @pl.when((row == pl.num_programs(0) - 1) & (part == pl.num_programs(1) - 1))
    def _():
        put_unit(*out, 2, key_sum[...])
        put_unit(*out, 3, value_sum[...])
        for fetch in fetches:
            fetch.wait()
        put_unit(*out, 0, dot_tn(held[0], held[1]))
        put_unit(*out, 1, dot_tn(held[2], held[3]))
        end_units(*out)


def mid_weights(info, memory, grad_keys, grad_values, pairs):
    count, rows, width = memory.shape
    block = memory_block(rows, width)
    half = jax.ShapeDtypeStruct((2 * width, width), bf16)
    return row_call(
        functools.partial(mid_weights_kernel, rows), "mid_weights", info, (count, 1),
        [block] * 3 + [pl.BlockSpec(memory_space=pl.ANY)] * 4,
        [pl.BlockSpec(memory_space=pl.ANY)] * 2 + [pl.BlockSpec((1, width), lambda row, part, info: (0, 0))],
        [half, half, jax.ShapeDtypeStruct((1, width), f32)],
        [(count, rows, width, width)] * 2, (memory, grad_keys, grad_values, *pairs),
        [pltpu.VMEM((width, width), f32)] * 2
        + unit_scratch(width)
        + [pltpu.VMEM((4,) + pairs[0].shape, bf16), pltpu.SemaphoreType.DMA((4,))],
    )


def qkv_kernel(info, x_ref, mine, got, vec_ref, q_ref, k_ref, v_ref):
    def run(even, odd):
        x = x_ref[...]
        q_ref[...] = ((dot_nn(x, unit(even, 0)) + vec_ref[0 : 1, :]) * HEAD**-0.5).astype(bf16)
        k_ref[...] = dot_nn(x, unit(odd, 0)).astype(bf16)
        v_ref[...] = (dot_nn(x, unit(even, 1)) + vec_ref[1 : 2, :]).astype(bf16)

    by_core(info, mine, got, run)


def project_self(info, x, head, vectors, rows=512):
    tokens, width = x.shape
    block = row_block(rows, width)
    return row_call(
        qkv_kernel, "project_self", info, (tokens // rows,),
        [block, full(None), full(None), full(None)], [block] * 3,
        [jax.ShapeDtypeStruct((tokens, width), bf16)] * 3,
        [(tokens, width, width)] * 4, (x, *head, vectors),
    )


def target_back_kernel(info, z_ref, q_ref, k_ref, v_ref, mine, got, out_ref):
    def run(even, odd):
        out_ref[...] = (
            z_ref[...]
            + dot_nt(q_ref[...], unit(even, 0))
            + dot_nt(k_ref[...], unit(odd, 0))
            + dot_nt(v_ref[...], unit(even, 1))
        )

    by_core(info, mine, got, run)


def target_back(info, dz, grads, head, rows=512):
    tokens, width = dz.shape
    block = row_block(rows, width)
    return row_call(
        target_back_kernel, "target_back", info, (tokens // rows,),
        [block] * 4 + [full(None)] * 2, block, jax.ShapeDtypeStruct((tokens, width), f32),
        [(tokens, width, width)] * 4, (dz, *grads, *head),
    )


def self_weights_kernel(
    info, x_hbm, q_hbm, k_hbm, v_hbm, cross_hbm, dcross_hbm, first_ref, value_ref, ffn_ref, wide_ref,
    mine, other, held, arrived, stage, sent, vectors, vectors_sent,
):
    sources = (cross_hbm, dcross_hbm, x_hbm, q_hbm, k_hbm, v_hbm)
    copies = [
        pltpu.make_async_copy(source, held.at[place], arrived.at[place])
        for place, source in enumerate(sources)
    ]
    for copy in copies:
        copy.start()
    width = x_hbm.shape[1]
    out = (info, stage, sent, mine, other)
    copies[0].wait()
    copies[1].wait()
    put_unit(*out, 3, dot_tn(held[0], held[1]))
    copies[2].wait()
    sums = []
    for number in range(3):
        copies[3 + number].wait()
        put_unit(*out, number, dot_tn(held[2], held[3 + number]))
        sums.append(jnp.sum(held[3 + number].astype(f32), 0, keepdims=True))
    row = lambda ref, number: ref[number : number + 1, :]
    vectors[...] = jnp.concatenate(
        [sums[0], sums[2], row(first_ref, 2), row(first_ref, 3), value_ref[...], row(ffn_ref, 5)]
        + [wide_ref[:, low : low + width] for low in range(0, wide_ref.shape[1], width)]
        + [
            row(ffn_ref, 2), row(first_ref, 0), row(ffn_ref, 3), row(ffn_ref, 0), row(first_ref, 1),
            row(ffn_ref, 4), row(ffn_ref, 1), jnp.zeros((VECTORS - 17, width), f32),
        ],
        0,
    ).astype(bf16)
    ends = [
        pltpu.make_async_copy(vectors, ref.at[pl.ds(2 * width, VECTORS), :], vectors_sent.at[place])
        for place, ref in enumerate((mine, other))
    ]
    for copy in ends:
        copy.start()
    end_units(*out)
    for copy in ends:
        copy.wait()


def self_weights(info, x, grads, cross, sums):
    tokens, width = x.shape
    half = jax.ShapeDtypeStruct((2 * width + VECTORS, width), bf16)
    return row_call(
        self_weights_kernel, "self_weights", info, (),
        [pl.BlockSpec(memory_space=pl.ANY)] * 6 + [full(None)] * 4, [pl.BlockSpec(memory_space=pl.ANY)] * 2,
        [half, half],
        [(tokens, width, width)] * 4, (x, *grads, *cross, *sums),
        [pltpu.VMEM((6, tokens, width), bf16), pltpu.SemaphoreType.DMA((6,))]
        + unit_scratch(width)
        + [pltpu.VMEM((VECTORS, width), bf16), pltpu.SemaphoreType.DMA((2,))],
    )


def ffn_weights_kernel(h_ref, du_ref, a_ref, df_ref, w_hbm, into, outof, sent):
    part = pl.program_id(0)
    blocks, pieces, rows, width = w_hbm.shape
    half = rows // 2
    owners = pieces // blocks if pieces >= blocks else 1
    slot = part % 2

    def copies(part, slot):
        if pieces >= blocks:
            rows_out = w_hbm.at[:, pl.ds(part * owners, owners), pl.ds(half, half), :]
        else:
            rows_out = w_hbm.at[pl.ds(part, 1), :, pl.ds(half, half), :]
        return (
            pltpu.make_async_copy(into.at[slot], w_hbm.at[part, :, pl.ds(0, half), :], sent.at[slot, 0]),
            pltpu.make_async_copy(outof.at[slot], rows_out, sent.at[slot, 1]),
        )

    @pl.when(part >= 2)
    def _():
        for copy in copies(part - 2, slot):
            copy.wait()

    into[slot] = dot_tn(h_ref[...], du_ref[...]).astype(bf16).reshape(pieces, half, width)
    grad_out = dot_tn(a_ref[...], df_ref[...]).astype(bf16)
    for place in range(pieces):
        piece = grad_out[place * half : (place + 1) * half]
        if pieces >= blocks:
            outof[slot, place % blocks, place // blocks] = piece
        else:
            outof[slot, 0, place] = piece
    for copy in copies(part, slot):
        copy.start()

    @pl.when(part == pl.num_programs(0) - 1)
    def _():
        for copy in copies(part - 1, 1 - slot) + copies(part, slot):
            copy.wait()


def ffn_weights(second_low, grad_hidden, active, grad_out, pieces):
    tokens, width = second_low.shape
    blocks = active.shape[1] // width
    whole = pl.BlockSpec((tokens, width), lambda part: (0, 0), pipeline_mode=pl.Buffered(1))
    part = pl.BlockSpec((tokens, width), lambda part: (0, part))
    shape = (blocks, pieces, 2 * width // pieces, width)
    out_shape = (blocks, pieces // blocks) if pieces >= blocks else (1, pieces)
    return pl.pallas_call(
        ffn_weights_kernel,
        grid=(blocks,),
        in_specs=[whole, part, part, whole],
        out_specs=pl.BlockSpec(memory_space=pl.ANY),
        out_shape=jax.ShapeDtypeStruct(shape, bf16),
        scratch_shapes=[
            pltpu.VMEM((2, pieces, width // pieces, width), bf16),
            pltpu.VMEM((2,) + out_shape + (width // pieces, width), bf16),
            pltpu.SemaphoreType.DMA((2, 2)),
        ],
        compiler_params=params(),
        name="ffn_weights",
        cost_estimate=cost([(tokens, width, blocks * width)] * 2),
    )(second_low, grad_hidden, active, grad_out)


def pack_head_kernel(count, place, units, last, *refs):
    sources, out_ref, rows_ref, arrived, held = refs[:count], refs[count], refs[count + 1], refs[count + 2], refs[count + 3 :]
    own = last.shape[0]
    copies = [
        pltpu.make_async_copy(source, target, arrived.at[number])
        for number, (source, target) in enumerate(zip(sources, held))
    ]
    for copy in copies:
        copy.start()

    def unit_copy_by(act):
        rows = out_ref.at[pl.ds(0, own), :]

        @pl.when(place[0] < 3)
        def _():
            act(pltpu.make_async_copy(units.at[jnp.minimum(place[0], 2)], rows, arrived.at[count]))

        @pl.when(place[0] == 3)
        def _():
            act(pltpu.make_async_copy(last, rows, arrived.at[count]))

    unit_copy_by(lambda copy: copy.start())
    rows_ref[...] = jnp.zeros_like(rows_ref)
    for copy in copies:
        copy.wait()
    for number, ref in enumerate(held):
        rows_ref[: ref.shape[0], number * LANES : number * LANES + own] = ref[...].astype(f32)
    out_ref[own:, :] = rows_ref[...].astype(bf16)
    unit_copy_by(lambda copy: copy.wait())


def pack_head(place, units, last, vectors):
    own, width = last.shape
    count = len(vectors)
    return row_call(
        functools.partial(pack_head_kernel, count), "pack_head", place, (),
        [pl.BlockSpec(memory_space=pl.ANY)] * (2 + count), full(None),
        jax.ShapeDtypeStruct((own + 8, width), bf16), [], (units, last, *vectors),
        [pltpu.VMEM((8, width), f32), pltpu.SemaphoreType.DMA((count + 1,))]
        + [pltpu.VMEM(item.shape, item.dtype) for item in vectors],
        limit=58 * 2**20,
    )


def fold_call(kernel, name, spot, inputs, outs):
    return row_call(
        kernel, name, spot, (), [full(None)] * len(inputs), [full(None)] * len(outs),
        [jax.ShapeDtypeStruct(shape, kind) for shape, kind in outs], [], inputs, limit=12 * 2**20,
    )


def added(*parts):
    total = parts[0].astype(f32)
    for part in parts[1:]:
        total = total + part.astype(f32)
    return total


def fold_first_kernel(own, extra, spot, mine, got, keep_one, send_one, keep_two, send_two):
    high, side = spot[0], spot[3]
    half = own // 2
    slots = keep_one.shape[0] // half

    def take(place, low):
        rows = pl.ds(pl.multiple_of(place * own + low, 16), half)
        return added(mine[rows, :], got[rows, :]).astype(bf16)

    for slot in range(slots):
        rows = pl.ds(slot * half, half)
        keep_one[rows, :] = take(high * slots + slot, 0)
        send_one[rows, :] = take((1 - high) * slots + slot, 0)
        keep_two[rows, :] = take(2 * slot + side, half)
        send_two[rows, :] = take(2 * slot + 1 - side, half)
    if extra:
        vectors = added(mine[2 * slots * own :, :], got[2 * slots * own :, :]).astype(bf16)
        keep_one[slots * half :, :] = vectors
        send_one[slots * half :, :] = vectors


def fold_first(spot, mine, got, own):
    width = mine.shape[1]
    extra = mine.shape[0] - 2 * width
    rows = width // own * (own // 2)
    first, second = ((rows + extra, width), bf16), ((rows, width), bf16)
    return fold_call(
        functools.partial(fold_first_kernel, own, extra), "fold_first", spot, (mine, got),
        (first, first, second, second),
    )


def fold_second_kernel(
    half, extra, spot, keep_a, got_a, keep_b, got_b, keep_one, send_one, keep_two, send_two
):
    high, side = spot[0], spot[3]
    slots = keep_two.shape[0] // half

    def take(keep, got, place):
        rows = pl.ds(pl.multiple_of(place * half, 16), half)
        return added(keep[rows, :], got[rows, :]).astype(bf16)

    for slot in range(slots):
        rows = pl.ds(slot * half, half)
        keep_one[rows, :] = take(keep_a, got_a, 2 * slot + side)
        send_one[rows, :] = take(keep_a, got_a, 2 * slot + 1 - side)
        keep_two[rows, :] = take(keep_b, got_b, high * slots + slot)
        send_two[rows, :] = take(keep_b, got_b, (1 - high) * slots + slot)
    if extra:
        low = 2 * slots * half
        vectors = added(keep_a[low:, :], got_a[low:, :]).astype(bf16)
        keep_one[slots * half :, :] = vectors
        send_one[slots * half :, :] = vectors


def fold_second(spot, keep_a, got_a, keep_b, got_b, own):
    rows, width = keep_b.shape
    extra = keep_a.shape[0] - rows
    first, second = ((rows // 2 + extra, width), bf16), ((rows // 2, width), bf16)
    return fold_call(
        functools.partial(fold_second_kernel, own // 2, extra), "fold_second", spot,
        (keep_a, got_a, keep_b, got_b), (first, first, second, second),
    )


def fold_third_kernel(half, extra, spot, keep_a, got_a, keep_b, got_b, *parts):
    depth = spot[2]
    slots = keep_b.shape[0] // half
    for step, part in enumerate(parts):
        rows = pl.ds(pl.multiple_of((depth + step) % slots * half, 16), half)
        part[:half, :] = added(keep_a[rows, :], got_a[rows, :]).astype(bf16)
        part[half : 2 * half, :] = added(keep_b[rows, :], got_b[rows, :]).astype(bf16)
        if extra:
            low = slots * half
            part[2 * half :, :] = added(keep_a[low:, :], got_a[low:, :]).astype(bf16)


def fold_third(spot, keep_a, got_a, keep_b, got_b, own):
    rows, width = keep_b.shape
    extra = keep_a.shape[0] - rows
    part = ((own + extra, width), bf16)
    return fold_call(
        functools.partial(fold_third_kernel, own // 2, extra), "fold_third", spot,
        (keep_a, got_a, keep_b, got_b), (part,) * (rows // (own // 2)),
    )


def sources(spot, sent, got):
    high, core = spot[0], spot[1]
    rows = sent.shape[0] // 2
    return [
        (2 * y + c, ref, pl.ds(low, rows))
        for c, ref in ((core, sent), (1 - core, got))
        for y, low in ((high, 0), (1 - high, rows))
    ]


def finish_early_kernel(own, spot, sent, got, in_ref, out_ref, first_ref, rest_ref):
    width = sent.shape[1]
    for place, ref, rows in sources(spot, sent, got):
        low = rows.start
        in_ref[:, pl.ds(pl.multiple_of(place * width, width), width)] = ref[low : low + own, :].astype(f32)
        out_ref[pl.ds(pl.multiple_of(place * own, 8), own), :] = ref[low + own : low + 2 * own, :].astype(f32)
        unit = ref[low + 2 * own : low + 3 * own, :].astype(f32)

        @pl.when(place == 0)
        def _(unit=unit):
            first_ref[...] = unit

        @pl.when(place != 0)
        def _(unit=unit, place=place):
            rest_ref[place - 1] = unit


def finish_early(spot, sent, got, own):
    width = sent.shape[1]
    return fold_call(
        functools.partial(finish_early_kernel, own), "finish_early", spot, (sent, got),
        (((own, 4 * width), f32), ((4 * own, width), f32), ((own, width), f32), ((3, own, width), f32)),
    )


def finish_late_kernel(spot, sent, got, rest_ref, last_ref):
    for place, ref, rows in sources(spot, sent, got):
        unit = ref[rows, :].astype(f32)

        @pl.when(place == 3)
        def _(unit=unit):
            last_ref[...] = unit

        @pl.when(place != 3)
        def _(unit=unit, place=place):
            rest_ref[place] = unit


def finish_late(spot, sent, got):
    rows, width = sent.shape
    return fold_call(
        finish_late_kernel, "finish_late", spot, (sent, got),
        (((3, rows // 2, width), f32), ((rows // 2, width), f32)),
    )


def wide(array):
    return array.astype(f32)


def weight_grad(left, right):
    return dot_tn(left, right).astype(bf16)


def forward(
    target, memory, cotangent, info, pieces, head, mid, tail, vectors,
    mid_step=lambda *same: same, mid_last=lambda *same: same,
):
    queries, keys, values = project_self(info, target, head, vectors)
    queries, mid = mid_step(queries, mid)
    context_self, stats_self = self_attend(info, queries, keys, values)
    context_self, mid = mid_last(context_self, mid)
    total_first, first_low = first_norm(info, target, context_self, head, vectors)
    key_cross, value_cross, query_cross = project_memory(info, memory, first_low, mid, vectors)
    context_cross, stats_cross = cross_attend(info, query_cross, key_cross, value_cross)
    output, second_low, active, du, df, do_cross, dz2, dc_cross, sums_ffn, sums_wide = ffn_block(
        info, total_first, context_cross, cotangent, mid, tail, vectors
    )
    grad_ffn = ffn_weights(second_low, du, active, df, pieces)
    dq_cross, dk_cross, dv_cross = cross_attend_back(
        info, query_cross, key_cross, value_cross, dc_cross, context_cross, stats_cross
    )
    dz1, do_self, dc_self, sums_first = first_back(info, dz2, dq_cross, total_first, head, mid, vectors)
    grads = self_attend_back(info, queries, keys, values, dc_self, context_self, stats_self)
    memory, *grads = lax.optimization_barrier((memory, *grads))
    *grad_mid, sum_value = mid_weights(
        info, memory, dk_cross, dv_cross, (first_low, dq_cross, context_self, do_self)
    )
    cross = (context_cross, do_cross)
    sums = (sums_first, sum_value, sums_ffn, sums_wide)
    return output, grad_ffn, grad_mid, dz1, grads, dk_cross, dv_cross, cross, sums, mid


def forward_back(target, memory, cotangent, info, pieces, head, mid, tail, vectors):
    output, grad_ffn, grad_mid, dz1, grads, dk_cross, dv_cross, cross, sums, mid = forward(
        target, memory, cotangent, info, pieces, head, mid, tail, vectors
    )
    grad_self = self_weights(info, target, grads, cross, sums)
    target_grad = target_back(info, dz1, grads, head)
    memory_grad = memory_back(info, dk_cross, dv_cross, mid, 0, memory.shape[0])
    return (output, target_grad, memory_grad), grad_ffn, grad_mid, grad_self


def pair_swap(array, axis, bit):
    count = lax.axis_size(axis)
    return lax.ppermute(array, axis, [(place, place ^ bit) for place in range(count)])


def ring(array, axis, shift):
    count = lax.axis_size(axis)
    return lax.ppermute(array, axis, [(place, (place + shift) % count) for place in range(count)])


def pick(array, axis, index):
    return lax.dynamic_index_in_dim(array, index, axis, keepdims=False)


def places():
    dp, fsdp = lax.axis_index("dp"), lax.axis_index("fsdp")
    return dp // 2, dp % 2, fsdp // 2, fsdp % 2


def add_half(array, axis, mine, mesh_axis, bit):
    got = pair_swap(pick(array, axis, 1 - mine), mesh_axis, bit)
    return (wide(pick(array, axis, mine)) + wide(got)).astype(bf16)


def add_depth(array, depth):
    total = wide(pick(array, 0, depth))
    for step in (1, 2, 3):
        total = total + wide(ring(pick(array, 0, (depth + step) % 4), "fsdp", 2 * step))
    return total.astype(bf16)


def fence(*arrays):
    return lax.optimization_barrier(arrays)


def add(mine, got):
    return (wide(mine) + wide(got)).astype(bf16)


def cut(array):
    half = array.shape[-2] // 2 // 8 * 8
    return array[..., :half, :], array[..., half:, :]


def join_pair(array, axis, mine, mesh_axis, bit):
    return join(array, pair_swap(array, mesh_axis, bit), axis, mine)


def join(array, got, axis, mine):
    first = jnp.where(mine == 0, array, got)
    second = jnp.where(mine == 0, got, array)
    return jnp.stack([first, second], axis)


def share_dp(array):
    high, core, _, _ = places()
    both = join_pair(array, 0, high, "dp", 2)
    return join_pair(both, 1, core, "dp", 1).reshape((4,) + array.shape)


def join_depth(array, depth):
    parts = [array] + [ring(array, "fsdp", 2 * step) for step in (1, 2, 3)]
    out = jnp.zeros((4,) + array.shape, array.dtype)
    for step, part in enumerate(parts):
        out = lax.dynamic_update_index_in_dim(out, part, (depth - step) % 4, 0)
    return out


def gather_vectors(rows, own):
    pieces, _, width = rows.shape
    groups = width // LANES
    rows = rows.reshape(pieces, 8, groups, LANES)[..., :own]
    hidden = rows[:, :4, 2].reshape(4, pieces * own)
    rows = jnp.transpose(rows, (2, 1, 0, 3)).reshape(groups * 8, pieces * own)
    return wide(jnp.concatenate([rows[:16], hidden, rows[20:]], 0))


def fast_layer(
    target, memory, cotangent, bucket, source_len, self_qkv, self_out, self_bias, cross_qkv,
    cross_out, cross_bias, ffn_in, ffn_in_bias, ffn_out, ffn_out_bias, norm_gain, norm_bias,
):
    dp = lax.axis_index("dp")
    high, core, depth, side = places()
    count, width = memory.shape[0], target.shape[1]
    own = self_out.shape[0]
    pieces = width // own
    info = jnp.concatenate([bucket, source_len, core[None]])
    head = pack_head(
        dp[None],
        self_qkv,
        self_out,
        (self_bias, cross_bias, ffn_in_bias.reshape(4, own), ffn_out_bias[None], norm_gain, norm_bias),
    )
    mid = pick(jnp.concatenate([cross_out[None], cross_qkv], 0), 0, dp)
    head, mid = fence(join_depth(head, depth), mid)
    one, two = cut(head)
    one, two = join_pair(one, 1, side, "fsdp", 1), join_pair(two, 1, high, "dp", 2)
    one, two, mid = fence(one, two, mid)
    one, two = join_pair(one, 2, high, "dp", 2), join_pair(two, 1, side, "fsdp", 1)
    half = own // 2
    mine = jnp.concatenate([one, two[:, :, :, :half]], 3).reshape(pieces, 2, own, width)
    mine, mid, ffn_in, ffn_out = fence(mine, join_depth(mid, depth), ffn_in, ffn_out)
    got = pair_swap(mine, "dp", 1)
    vectors = gather_vectors(two[:, :, 0, half:].reshape(pieces, 8, width), own)
    three, four = cut(mid)
    in_cols = pick(ffn_in.reshape(own, 4, width), 1, dp)
    out_rows = pick(ffn_out.reshape(4, own, width), 0, dp)
    tail = lax.all_gather(
        jnp.concatenate([in_cols, out_rows], 0), ("dp", "fsdp"), axis=0, tiled=True
    ).reshape(4, pieces, 2 * own, width)
    parts = (three, pair_swap(three, "fsdp", 1), four, pair_swap(four, "dp", 2))

    def mid_step(queries, parts):
        queries, three, got_three, four, got_four = fence(queries, *parts)
        three, four = join(three, got_three, 1, side), join(four, got_four, 1, high)
        return queries, (three, pair_swap(three, "dp", 2), four, pair_swap(four, "fsdp", 1))

    def mid_last(context, parts):
        context, three, got_three, four, got_four = fence(context, *parts)
        three, four = join(three, got_three, 2, high), join(four, got_four, 1, side)
        mine = jnp.concatenate([three, four], 3).reshape(pieces, 2, own, width)
        return context, (mine, pair_swap(mine, "dp", 1))

    head = (mine, got)
    output, grad_ffn, grad_mid, dz1, grads, dk_cross, dv_cross, cross, sums, mid = forward(
        target, memory, cotangent, info, pieces, head, parts, tail, vectors, mid_step, mid_last
    )
    sum_ffn = lax.psum_scatter(
        grad_ffn.reshape(-1, width), ("dp", "fsdp"), scatter_dimension=0, tiled=True
    )
    spot = jnp.stack([high, core, depth, side])
    mine, other, target_late = fence(*grad_mid, target)
    got = pair_swap(other, "dp", 1)
    own_part, other = self_weights(info, target_late, grads, cross, sums)
    got, own_part, other = fence(got, own_part, other)
    keep_one, send_one, keep_two, send_two = fold_first(spot, mine, got, own)
    send_one, send_two, other, dz1 = fence(send_one, send_two, other, dz1)
    got_one, got_two = pair_swap(send_one, "dp", 2), pair_swap(send_two, "fsdp", 1)
    got = pair_swap(other, "dp", 1)
    target_grad = target_back(info, dz1, grads, head)
    got_one, got_two, got, target_grad = fence(got_one, got_two, got, target_grad)
    keep_one, send_one, keep_two, send_two = fold_second(spot, keep_one, got_one, keep_two, got_two, own)
    keep_three, send_three, keep_four, send_four = fold_first(spot, own_part, got, own)
    send_one, send_two, send_three, send_four, dk_cross = fence(
        send_one, send_two, send_three, send_four, dk_cross
    )
    got_one, got_two = pair_swap(send_one, "fsdp", 1), pair_swap(send_two, "dp", 2)
    got_three, got_four = pair_swap(send_three, "dp", 2), pair_swap(send_four, "fsdp", 1)
    memory_grad = memory_back(info, dk_cross, dv_cross, mid, 0, count // 2)
    got_one, got_two, got_three, got_four, memory_grad = fence(
        got_one, got_two, got_three, got_four, memory_grad
    )
    sum_mid, *sends = fold_third(spot, keep_one, got_one, keep_two, got_two, own)
    keep_three, send_three, keep_four, send_four = fold_second(
        spot, keep_three, got_three, keep_four, got_four, own
    )
    *sends, send_three, send_four, dk_cross = fence(*sends, send_three, send_four, dk_cross)
    rings = [ring(item, "fsdp", 2 * step) for step, item in zip((1, 2, 3), sends)]
    got_three, got_four = pair_swap(send_three, "fsdp", 1), pair_swap(send_four, "dp", 2)
    memory_grad = memory_back(
        info, dk_cross, dv_cross, mid, count // 2, count - count // 2, start=(memory_grad,)
    )
    got_three, got_four, memory_grad, *rings = fence(got_three, got_four, memory_grad, *rings)
    sum_mid = added(sum_mid, *rings).astype(bf16)
    early = jnp.concatenate([sum_ffn, sum_mid], 0)
    sum_self, *sends = fold_third(spot, keep_three, got_three, keep_four, got_four, own)
    *sends, early = fence(*sends, early)
    rings = [ring(item, "fsdp", 2 * step) for step, item in zip((1, 2, 3), sends)]
    got = pair_swap(early, "dp", 2)
    got, *rings = fence(got, *rings)
    late = added(sum_self, *rings)
    vectors = late[-VECTORS:]
    late = late[:-VECTORS].astype(bf16)
    early = jnp.concatenate([early, got], 0)
    early, late = fence(early, late)
    got_early = pair_swap(early, "dp", 1)
    got = pair_swap(late, "dp", 2)
    late = jnp.concatenate([late, got], 0)
    late, got_early = fence(late, got_early)
    got = pair_swap(late, "dp", 1)
    grad_in, grad_out, grad_self_out, grad_cross_qkv = finish_early(spot, early, got_early, own)
    place = lax.axis_index("fsdp")
    hidden = pick(vectors[6:10].reshape(pieces, 4 * own), 0, place)
    vectors = lax.dynamic_slice_in_dim(vectors, place * own, own, 1)
    got, grad_in, hidden, vectors = fence(got, grad_in, hidden, vectors)
    grad_self_qkv, grad_cross_out = finish_late(spot, late, got)
    return (
        output, target_grad, memory_grad, grad_self_qkv, grad_self_out, vectors[:3], grad_cross_qkv,
        grad_cross_out, vectors[3:6], grad_in, hidden, grad_out, vectors[10], vectors[11:14], vectors[14:17],
    )


def plain_layer(
    target, memory, cotangent, bucket, source_len, self_qkv, self_out, self_bias, cross_qkv,
    cross_out, cross_bias, ffn_in, ffn_in_bias, ffn_out, ffn_out_bias, norm_gain, norm_bias,
):
    gather = lambda item, axis: lax.all_gather(item, "fsdp", axis=axis, tiled=True)
    info = jnp.concatenate([bucket, source_len, jnp.zeros_like(bucket)])
    width = target.shape[1]
    blocks = ffn_out.shape[0] * lax.axis_size("fsdp") // width
    split = lambda units: (units[None, 0::2], units[None, 1::2])
    head = split(jnp.concatenate([gather(self_qkv, 1), gather(self_out, 0)[None]], 0))
    mid = split(jnp.concatenate([gather(cross_out, 0)[None], gather(cross_qkv, 1)], 0))
    ffn_in_w = jnp.swapaxes(gather(ffn_in, 0).reshape(width, blocks, width), 0, 1)
    tail = jnp.concatenate([ffn_in_w, gather(ffn_out, 0).reshape(blocks, width, width)], 1)[:, None]
    vectors = (
        gather(self_bias, 1), gather(cross_bias, 1), gather(ffn_in_bias, 0).reshape(blocks, width),
        gather(ffn_out_bias, 0)[None], gather(norm_gain, 1), gather(norm_bias, 1),
    )
    vectors = wide(
        jnp.concatenate([jnp.pad(item, ((0, 8 - item.shape[0]), (0, 0))) for item in vectors], 0)
    )
    outs, grad_ffn, grad_mid, grad_self = forward_back(
        target, memory, cotangent, info, 1, head, mid, tail, vectors
    )

    def reduce(grad, axis):
        piece = lax.psum_scatter(wide(grad), "fsdp", scatter_dimension=axis, tiled=True)
        return lax.psum(piece, "dp")

    def units(mine, other):
        both = [item[: 2 * width].reshape(2, width, width) for item in (mine, other)]
        return jnp.stack(both, 1).reshape(4, width, width)

    grad_in = jnp.swapaxes(grad_ffn[:, 0, :width], 0, 1).reshape(width, blocks * width)
    grad_out = grad_ffn[:, 0, width:].reshape(blocks * width, width)
    vectors = grad_self[0][2 * width :]
    grad_self, grad_mid = units(*grad_self), units(*grad_mid)
    return outs + (
        reduce(grad_self[:3], 1),
        reduce(grad_mid[0], 0),
        reduce(vectors[:3], 1),
        reduce(grad_mid[1:], 1),
        reduce(grad_self[3], 0),
        reduce(vectors[3:6], 1),
        reduce(grad_in, 0),
        reduce(vectors[6 : 6 + blocks].reshape(-1), 0),
        reduce(grad_out, 0),
        reduce(vectors[10], 0),
        reduce(vectors[11:14], 1),
        reduce(vectors[14:17], 1),
    )


def solution(mesh):
    rows = P(("dp", "fsdp"))
    first = P("fsdp")
    second = P(None, "fsdp")
    weights = (second, first, second, second, first, second, first, first, first, first, second, second)
    layer = fast_layer if (mesh.shape["dp"], mesh.shape["fsdp"]) == (4, 8) else plain_layer
    return jax.shard_map(
        layer,
        mesh=mesh,
        in_specs=(rows,) * 5 + weights,
        out_specs=(rows,) * 3 + weights,
        check_vma=False,
    )
```
